128 devices in a mesh: req: 32 (over y, z, x_hi), kvh: 4 (over x_lo, core).
Axes of the slice: x: 4 (x_hi: 2, x_lo: 2; x = x_hi * 2 + x_lo), y: 4, z: 4, core: 2. Of those that a mesh axis runs over, the one named last changes fastest.
Arguments:
- queries: bfloat16 [1536, 8192], P('req', 'kvh'), may hold values from -64 to 64
- keys: bfloat16 [1536, 4, 192, 128], P('req', 'kvh'), may hold values from -4 to 4
- values: bfloat16 [1536, 4, 192, 128], P('req', 'kvh'), may hold values from -5 to 5
- lengths: int32 [1536], P('req'), may hold values from 2 to 192, as said below
- o_proj: bfloat16 [8192, 4096], P('kvh', 'req'), may hold values from -0.5 to 0.5
- residual: bfloat16 [1536, 4096], P(('req', 'kvh')), may hold values from -6 to 6
- norm_gain: float32 [4096], replicated, may hold values from 0.1 to 1.9
- gate_up: bfloat16 [128, 4096, 1536], P(('req', 'kvh')), may hold values from -0.09375 to 0.09375
- down: bfloat16 [128, 768, 4096], P(('req', 'kvh')), may hold values from -0.21875 to 0.21875
- routes: int32 [1536, 8], P(('req', 'kvh')), may hold values from 0 to 127, all different within a row; in each aligned block of 12 rows (0 to 11, 12 to 23, ...) at most 2 rows name the same one
- route_weights: float32 [1536, 8], P(('req', 'kvh')), may hold values from 0.05 to 0.5
Outputs:
- mixed: bfloat16 [1536, 4096], P(('req', 'kvh'))
The draws below stay inside these ranges and needn't reach their ends.
Inputs may be any that keep to these rules, and one draw needn't show every extreme that they name: `lengths`: request 0 has all 192 positions. `routes`: among the 12 rows of one device, no expert is named by more than 2 rows.
All inputs are finite; a program needn't handle non-finite values.
Results may differ from the reference program's by a relative error of at most 0.0056.
Values may be sent and summed in bfloat16 or wider, within the bound.
A program may use at most 128 MiB of HBM per device.

```python
import math
import jax
import jax.numpy as jnp
import numpy as np
from jax import lax

D = 4096
HEADS = 64
KV_HEADS = 4
HEAD_DIM = 128
HID = 768
TOP = 8
CTX = 192
TOK_SRC = 12
EXPERTS = 128
TOKENS = 1536
REQ_DEV = 48
CAP = 2


def draw_queries(key, part):
    key = jax.random.fold_in(key, 2)
    shape = (TOKENS, HEADS * HEAD_DIM)
    drawn = jnp.clip(jax.random.normal(key, shape, jnp.float32), -4.0, 4.0)
    return drawn.astype(jnp.bfloat16)


def draw_keys(key, part):
    key = jax.random.fold_in(key, 1)
    shape = (TOKENS, KV_HEADS, CTX, HEAD_DIM)
    drawn = jnp.clip(jax.random.normal(key, shape, jnp.float32), -4.0, 4.0)
    return drawn.astype(jnp.bfloat16)


def draw_lengths(key, part):
    key = jax.random.fold_in(key, 5)
    first, second = jax.random.split(key)
    blocks = TOKENS // REQ_DEV
    level = jax.random.randint(first, (blocks, 1), 1, 5)
    spread = jax.random.randint(second, (blocks, REQ_DEV), 0, CTX - 1)
    counted = (2 + spread * level // 4).reshape(-1)
    counted = jnp.where(jnp.arange(TOKENS) == 0, CTX, counted)
    return counted.astype(jnp.int32)


def shard_levels(key, extent, cuts, low, high):
    gain = 1.0
    for axis_at, parts in cuts:
        heights = jax.random.uniform(jax.random.fold_in(jax.random.fold_in(key, 6), axis_at), (parts,), jnp.float32, low / len(cuts), high / len(cuts))
        gain = gain * jnp.repeat(jnp.exp(heights), extent[axis_at] // parts).reshape((-1,) + (1,) * (len(extent) - 1 - axis_at))
    return gain


def assign_block(key, own, number, rows, amount, top, limit, skew):
    order = jax.random.permutation(key, amount)
    crowded, usual = load_shares(amount, rows * top, limit, skew, True), load_shares(amount, rows * top, limit, skew, False)
    places = jnp.arange(amount)

    def named(tallies, rotation):
        used = int((tallies > 0).sum())
        fixed = max(1, used // 4)
        moved = fixed + (places - fixed + rotation * (used - fixed)) % max(1, amount - fixed)
        return jnp.zeros((amount,), jnp.int32).at[order[jnp.where(places < fixed, places, moved)]].set(jnp.asarray(tallies, jnp.int32))

    tallies = jnp.where(number % 4 == 0, named(crowded, number // 4), named(usual, number - number // 4 - 1))
    mixed = jax.random.permutation(jax.random.fold_in(own, 3), amount)
    giver, receiver = mixed[0:amount // 2 * 2:2], mixed[1:amount // 2 * 2:2]
    slack = jnp.minimum(tallies[giver] - 1, limit - tallies[receiver]) // 2
    slack = jnp.where((giver == order[0]) | (receiver == order[0]) | (tallies[receiver] == 0), 0, jnp.maximum(slack, 0))
    moved = jax.random.randint(jax.random.fold_in(own, 4), (amount // 2,), 0, 1 << 20) % (slack + 1)
    tallies = tallies.at[giver].add(-moved).at[receiver].add(moved)
    labels = jnp.searchsorted(jnp.cumsum(tallies), jnp.arange(rows * top), side="right").astype(jnp.int32)
    grid = labels.reshape(top, rows).T
    grid = grid[jax.random.permutation(jax.random.fold_in(own, 1), rows)]
    rotation = jax.random.randint(jax.random.fold_in(own, 2), (rows, 1), 0, top)
    return jnp.take_along_axis(grid, (jnp.arange(top)[None, :] + rotation) % top, axis=1)


def load_shares(count, total, reach, slope, full):
    portions = [(1 << 20) // math.isqrt(standing ** slope) + 1 for standing in range(1, count + 1)]
    largest = reach if full else min(reach, max(-(-total // count), total * portions[0] // sum(portions)))
    least = 1 if total - largest >= count - 1 else 0
    counts, surplus = [largest] + [least] * (count - 1), total - largest - least * (count - 1)
    while surplus > 0:
        movable = [i for i in range(1, count) if counts[i] < largest] or [i for i in range(1, count) if counts[i] < reach]
        mass, remaining = sum([portions[i] for i in movable]), surplus
        for i in movable:
            extra = min(reach - counts[i], max(1, remaining * portions[i] // mass), surplus)
            counts[i] = counts[i] + extra
            surplus = surplus - extra
    return np.array(counts)


def normal_values(stream_key, dims, scale, bound, pieces=(), kind=jnp.bfloat16):
    entries = scale * jax.random.normal(stream_key, dims, jnp.float32)
    if pieces:
        entries = entries * shard_levels(stream_key, dims, pieces, -0.22, 0.18)
    return jnp.clip(entries, -bound, bound).astype(kind)


def setup_inputs(seed: int = 0) -> dict:
    seeds = jax.random.split(jax.random.key(seed), 12)
    queries = draw_queries(jax.random.fold_in(seeds[11], 71), 0)
    keys = draw_keys(jax.random.fold_in(seeds[11], 71), 0)
    values = normal_values(seeds[2], (TOKENS, KV_HEADS, CTX, HEAD_DIM), 1.0, 5.0, ((0, 32), (1, 4)))
    lengths = draw_lengths(jax.random.fold_in(seeds[11], 71), 0)
    o_proj = normal_values(seeds[4], (HEADS * HEAD_DIM, D), HEAD_DIM ** -0.5, 0.5, ((0, 4), (1, 32)))
    residual = normal_values(seeds[5], (TOKENS, D), 1.0, 6.0, ((0, 128),))
    norm_gain = jnp.clip(1.0 + 0.18 * jax.random.normal(seeds[6], (D,), jnp.float32), 0.1, 1.9)
    gate_up = normal_values(seeds[7], (EXPERTS, D, 2 * HID), D ** -0.5, 0.09375, ((0, 128),))
    down = normal_values(seeds[8], (EXPERTS, HID, D), HID ** -0.5, 0.21875, ((0, 128),))
    routes_keys = jax.random.split(jax.random.fold_in(seeds[9], 1), TOKENS // TOK_SRC)
    routes_turns = jax.random.permutation(jax.random.fold_in(seeds[9], 3), TOKENS // TOK_SRC)
    routes = jax.vmap(lambda own, number: assign_block(jax.random.fold_in(seeds[9], 2), own, number, TOK_SRC, EXPERTS, TOP, CAP, 2))(routes_keys, routes_turns).reshape((TOKENS, TOP))
    route_weights = jnp.clip(jnp.exp(math.log(0.5) - 2.3025851 * jax.random.uniform(seeds[10], (TOKENS, TOP), jnp.float32) ** shard_levels(seeds[10], (TOKENS, TOP), ((0, 128),), -0.2, 0.2)), 0.05, 0.5)
    return dict(queries=queries, keys=keys, values=values, lengths=lengths, o_proj=o_proj, residual=residual, norm_gain=norm_gain, gate_up=gate_up, down=down, routes=routes, route_weights=route_weights)


def expert_rows(rows, weight_gate_up, weight_down):
    both = jnp.dot(rows, weight_gate_up, preferred_element_type=jnp.float32)
    active = (jax.nn.silu(both[:, :HID]) * both[:, HID:]).astype(jnp.bfloat16)
    return jnp.dot(active, weight_down, preferred_element_type=jnp.float32).astype(jnp.bfloat16)

def reference(queries, keys, values, lengths, o_proj, residual, norm_gain, gate_up, down, routes, route_weights):
    count = queries.shape[0]
    group = HEADS // KV_HEADS
    query_heads = queries.reshape(count, KV_HEADS, group, HEAD_DIM).astype(jnp.float32)
    scores = jnp.einsum('tkgd,tkpd->tkgp', query_heads, keys.astype(jnp.float32)) / math.sqrt(HEAD_DIM)
    valid = jnp.arange(CTX, dtype=jnp.int32)[None, :] < lengths[:, None]
    scores = jnp.where(valid[:, None, None, :], scores, -1e+30)
    shifted = jnp.exp(scores - lax.optimization_barrier(jnp.max(scores, axis=3, keepdims=True)))
    probabilities = (shifted / lax.optimization_barrier(jnp.sum(shifted, axis=3, keepdims=True))).astype(jnp.bfloat16)
    attended = jnp.einsum('tkgp,tkpd->tkgd', probabilities.astype(jnp.float32), values.astype(jnp.float32))
    attended = attended.astype(jnp.bfloat16).reshape(count, HEADS * HEAD_DIM)
    projected = jnp.dot(attended, o_proj, preferred_element_type=jnp.float32)
    state = residual.astype(jnp.float32) + projected
    factor = lax.rsqrt(lax.optimization_barrier(jnp.mean(state * state, axis=1, keepdims=True)) + 1e-06)
    normed = (state * factor * norm_gain.astype(jnp.float32)).astype(jnp.bfloat16)
    sources = count // TOK_SRC
    flat = routes.reshape(sources, TOK_SRC * TOP)
    hits = (flat[:, :, None] == jnp.arange(EXPERTS, dtype=jnp.int32)[None, None, :]).astype(jnp.int32)
    slot = lax.optimization_barrier(jnp.sum(hits * (jnp.cumsum(hits, axis=1) - 1), axis=2)).astype(jnp.int32)
    source_ids = jnp.broadcast_to(jnp.arange(sources, dtype=jnp.int32)[:, None], flat.shape)
    repeated = jnp.repeat(normed, TOP, axis=0).reshape(sources, TOK_SRC * TOP, D)
    buffer = jnp.zeros((EXPERTS, sources, CAP, D), normed.dtype).at[flat, source_ids, slot].set(repeated)

    def serve(operands):
        return expert_rows(operands[0], operands[1], operands[2])
    served = lax.map(serve, (buffer.reshape(EXPERTS, sources * CAP, D), gate_up, down))
    served = served.reshape(EXPERTS, sources, CAP, D)
    picked = served[flat, source_ids, slot].reshape(count, TOP, D)
    blended = lax.optimization_barrier(jnp.sum(picked.astype(jnp.float32) * route_weights[:, :, None], axis=1))
    return (state + blended).astype(jnp.bfloat16)
```

```python
import math

import jax
import jax.numpy as jnp
from jax import lax
from jax.sharding import PartitionSpec as P
from jax.experimental import pallas as pl
from jax.experimental.pallas import tpu as pltpu

K_STEP = 37
K_INV = 45
N_DEV = 128
MESH = pl.DeviceIdType.MESH


def coords():
    r = lax.axis_index("req")
    k = lax.axis_index("kvh")
    return lax.rem(r, 2) * 2 + k // 2, r // 8, lax.rem(r // 2, 4), lax.rem(k, 2)


def place(x, y, z, c):
    x, y, z, c = lax.rem(x, 4), lax.rem(y, 4), lax.rem(z, 4), lax.rem(c, 2)
    return ((y * 4 + z) * 2 + x // 2, lax.rem(x, 2) * 2 + c)


def enter(along_y, along_z):
    x, y, z, c = coords()
    barrier = pltpu.get_barrier_semaphore()
    for dx in range(4):
        for dc in range(2):
            if dx or dc:
                pl.semaphore_signal(barrier, inc=1, device_id=place(x + dx, y, z, c + dc), device_id_type=MESH)
    for d in range(1, 4):
        pl.semaphore_signal(barrier, inc=1, device_id=place(x, y + d, z, c), device_id_type=MESH)
        pl.semaphore_signal(barrier, inc=1, device_id=place(x, y, z + d, c), device_id_type=MESH)
    pl.semaphore_wait(barrier, 13)
    for d in range(1, 4):
        pl.semaphore_signal(along_y, inc=1, device_id=place(x, y + d, z, c), device_id_type=MESH)
    pl.semaphore_wait(along_y, 3)
    for d in range(1, 4):
        pl.semaphore_signal(along_z, inc=1, device_id=place(x, y, z + d, c), device_id_type=MESH)
    pl.semaphore_wait(along_z, 3)


def iota(shape, dim):
    return lax.broadcasted_iota(jnp.int32, shape, dim)


def route_keys(expert, token, routes_smem, me):
    slot = jnp.zeros_like(expert)
    for t in range(12):
        for k in range(8):
            slot = slot + jnp.where((expert == routes_smem[t, k]) & (token > t), 1, 0)
    key = (((expert - me + N_DEV) * K_INV) & (N_DEV - 1)) * 2 + slot
    return jnp.where(token < 12, key, -1)


def expert_kernel(
    state_ref, gain_ref, routes_smem, routes_ref, weights_ref, gate_up_hbm, down_hbm,
    out_ref,
    gate_up, down, sent, received, rows, active, permuted, results, returned, normed, mix,
    weight_sem, send_sem, recv_sem, back_sem, return_sem, along_y, along_z,
):
    me = lax.axis_index("req") * 4 + lax.axis_index("kvh")
    bf16, f32 = jnp.bfloat16, jnp.float32
    loads = [
        pltpu.make_async_copy(gate_up_hbm, gate_up, weight_sem.at[0]),
        pltpu.make_async_copy(down_hbm, down, weight_sem.at[1]),
    ]
    for load in loads:
        load.start()
    enter(along_y, along_z)

    state = state_ref[...]
    factor = lax.rsqrt(jnp.sum(state * state, axis=1, keepdims=True) * (1.0 / 4096.0) + 1e-06)
    scaled = (state * factor * gain_ref[...]).astype(bf16)
    for s in range(8):
        normed[s * 16 : (s + 1) * 16, :] = scaled[:, s * 512 : (s + 1) * 512]

    lane = iota((8, 128), 1)
    sub = iota((8, 128), 0)
    token = lane & 15
    expert = jnp.full((8, 128), -1, jnp.int32)
    for t in range(12):
        for k in range(8):
            expert = jnp.where((sub == k) & (token == t), routes_smem[t, k], expert)
    keys = route_keys(expert, token, routes_smem, me)
    for part in range(8):
        row = iota((256, 128), 0) + part * 256
        hit = jnp.zeros((256, 128), f32)
        for k in range(8):
            hit = jnp.where(row // 8 == keys[k : k + 1, :], 1.0, hit)
        table = jnp.where((row & 7) == iota((256, 128), 1) // 16, hit, 0.0).astype(bf16)
        block = jnp.dot(table, normed[...], preferred_element_type=f32).astype(bf16)
        sent[part * 16 : (part + 1) * 16] = block.reshape(16, 16, 512)

    def send(d, carry):
        to = lax.rem(me + d * K_STEP, N_DEV)
        group = d // 64
        pltpu.make_async_remote_copy(
            src_ref=sent.at[d], dst_ref=received.at[d], send_sem=send_sem.at[group],
            recv_sem=recv_sem.at[group], device_id=(to // 4, lax.rem(to, 4)), device_id_type=MESH,
        ).start()
        return carry

    lax.fori_loop(1, N_DEV, send, 0)
    received[0] = sent[0]

    expert_column = jnp.concatenate([routes_ref[...]] * 8, axis=0)
    token_column = iota((128, 8), 0) & 15
    key_column = route_keys(expert_column, token_column, routes_smem, me)
    gates = jnp.concatenate([weights_ref[...]] * 8, axis=0)
    for part in range(8):
        column = iota((128, 256), 1) + part * 256
        share = jnp.zeros((128, 256), f32)
        for k in range(8):
            share = jnp.where(column // 8 == key_column[:, k : k + 1], gates[:, k : k + 1], share)
        share = jnp.where((column & 7) == iota((128, 256), 0) // 16, share, 0.0)
        high = share.astype(bf16)
        mix[:128, part * 256 : (part + 1) * 256] = high
        mix[128:, part * 256 : (part + 1) * 256] = (share - high.astype(f32)).astype(bf16)

    i, j = iota((256, 256), 0), iota((256, 256), 1)
    spread = jnp.where(j == (i & 31) * 8 + i // 32, 1.0, 0.0).astype(bf16)
    gather = jnp.where(i == (j & 31) * 8 + j // 32, 1.0, 0.0).astype(bf16)

    for group in range(2):
        first = 1 if group == 0 else 64
        landed = received.at[pl.ds(first, 64 * (group + 1) - first)]
        pltpu.make_async_copy(landed, landed, recv_sem.at[group]).wait()
        for chunk in range(4):
            block = received[group * 64 + chunk * 16 : group * 64 + (chunk + 1) * 16].reshape(256, 512)
            block = jnp.dot(spread, block, preferred_element_type=f32).astype(bf16)
            for s in range(8):
                rows[chunk * 32 : (chunk + 1) * 32, s * 512 : (s + 1) * 512] = block[s * 32 : (s + 1) * 32]
        if group == 0:
            loads[0].wait()
        for n in range(3):
            gate = jnp.dot(rows[...], gate_up[:, n * 256 : (n + 1) * 256], preferred_element_type=f32)
            up = jnp.dot(rows[...], gate_up[:, 768 + n * 256 : 768 + (n + 1) * 256], preferred_element_type=f32)
            active[:, n * 256 : (n + 1) * 256] = (gate / (1.0 + jnp.exp(-gate)) * up).astype(bf16)
        if group == 0:
            loads[1].wait()
        for s in range(8):
            part = jnp.dot(active[...], down[:, s * 512 : (s + 1) * 512], preferred_element_type=f32).astype(bf16)
            for chunk in range(4):
                permuted[chunk, s * 32 : (s + 1) * 32, :] = part[chunk * 32 : (chunk + 1) * 32]
        for chunk in range(4):
            block = jnp.dot(gather, permuted[chunk], preferred_element_type=f32).astype(bf16)
            results[group * 64 + chunk * 16 : group * 64 + (chunk + 1) * 16] = block.reshape(16, 16, 512)

        def send_back(d, carry):
            to = lax.rem(me + N_DEV * K_STEP - d * K_STEP, N_DEV)
            pltpu.make_async_remote_copy(
                src_ref=results.at[d], dst_ref=returned.at[d], send_sem=back_sem.at[0],
                recv_sem=return_sem.at[0], device_id=(to // 4, lax.rem(to, 4)), device_id_type=MESH,
            ).start()
            return carry

        lax.fori_loop(first, 64 * (group + 1), send_back, 0)
        if group == 0:
            returned[0] = results[0]

    landed = returned.at[pl.ds(1, 127)]
    pltpu.make_async_copy(landed, landed, return_sem.at[0]).wait()
    both = jnp.dot(mix[...], returned[...].reshape(2048, 512), preferred_element_type=f32)
    blended = both[:128] + both[128:]
    for s in range(8):
        columns = slice(s * 512, (s + 1) * 512)
        total = state_ref[:, columns] + blended[s * 16 : (s + 1) * 16]
        out_ref[:, columns] = total[:12].astype(bf16)
    gone = sent.at[pl.ds(1, 63)]
    pltpu.make_async_copy(gone, gone, send_sem.at[0]).wait()
    gone = sent.at[pl.ds(64, 64)]
    pltpu.make_async_copy(gone, gone, send_sem.at[1]).wait()
    gone = results.at[pl.ds(1, 127)]
    pltpu.make_async_copy(gone, gone, back_sem.at[0]).wait()


def experts(state, gain, routes, weights, gate_up, down):
    bf16, f32 = jnp.bfloat16, jnp.float32
    vmem = pl.BlockSpec(memory_space=pltpu.VMEM)
    smem = pl.BlockSpec(memory_space=pltpu.SMEM)
    hbm = pl.BlockSpec(memory_space=pl.ANY)
    pad = lambda a: jnp.pad(a, ((0, 4), (0, 0)))
    return pl.pallas_call(
        expert_kernel,
        out_shape=jax.ShapeDtypeStruct((12, 4096), bf16),
        in_specs=[vmem, vmem, smem, vmem, vmem, hbm, hbm],
        out_specs=vmem,
        scratch_shapes=[
            pltpu.VMEM((4096, 1536), bf16),
            pltpu.VMEM((768, 4096), bf16),
            pltpu.VMEM((128, 16, 512), bf16),
            pltpu.VMEM((128, 16, 512), bf16),
            pltpu.VMEM((128, 4096), bf16),
            pltpu.VMEM((128, 768), bf16),
            pltpu.VMEM((4, 256, 512), bf16),
            pltpu.VMEM((128, 16, 512), bf16),
            pltpu.VMEM((128, 16, 512), bf16),
            pltpu.VMEM((128, 512), bf16),
            pltpu.VMEM((256, 2048), bf16),
            pltpu.SemaphoreType.DMA((2,)),
            pltpu.SemaphoreType.DMA((2,)),
            pltpu.SemaphoreType.DMA((2,)),
            pltpu.SemaphoreType.DMA((1,)),
            pltpu.SemaphoreType.DMA((1,)),
            pltpu.SemaphoreType.REGULAR,
            pltpu.SemaphoreType.REGULAR,
        ],
        compiler_params=pltpu.CompilerParams(
            collective_id=1, has_side_effects=True, vmem_limit_bytes=56 * 2**20
        ),
        cost_estimate=pl.CostEstimate(flops=6 * 10**9, bytes_accessed=2 * 10**7, transcendentals=10**6),
        name="experts",
    )(pad(state), gain[None, :], routes, pad(routes), pad(weights), gate_up, down)


def attend(queries, keys, values, lengths):
    rows = queries.shape[0]
    width = keys.shape[3]
    group = queries.shape[1] // width
    query_heads = queries.reshape(rows, group, width)
    scores = jnp.einsum(
        "rgd,rpd->rgp", query_heads, keys[:, 0], preferred_element_type=jnp.float32
    ) / math.sqrt(width)
    valid = lax.broadcasted_iota(jnp.int32, (rows, keys.shape[2]), 1) < lengths[:, None]
    scores = jnp.where(valid[:, None, :], scores, -1e30)
    shifted = jnp.exp(scores - jnp.max(scores, axis=2, keepdims=True))
    probabilities = (shifted / jnp.sum(shifted, axis=2, keepdims=True)).astype(jnp.bfloat16)
    attended = jnp.einsum(
        "rgp,rpd->rgd", probabilities, values[:, 0], preferred_element_type=jnp.float32
    )
    return attended.astype(jnp.bfloat16).reshape(rows, group * width)


def body(
    queries,
    keys,
    values,
    lengths,
    o_proj,
    residual,
    norm_gain,
    gate_up,
    down,
    routes,
    route_weights,
):
    req_count = lax.axis_size("req")
    group_count = lax.axis_size("kvh")
    tok_src = residual.shape[0]
    attended = attend(queries, keys, values, lengths)
    partial_columns = jnp.dot(
        lax.all_gather(attended, "req", axis=0, tiled=True),
        o_proj,
        preferred_element_type=jnp.float32,
    )
    columns = partial_columns.shape[1]
    ordered = (
        partial_columns.reshape(req_count, group_count, tok_src, columns)
        .transpose(1, 0, 2, 3)
        .reshape(-1, columns)
    )
    summed = lax.psum_scatter(ordered, "kvh", scatter_dimension=0, tiled=True)
    projected = lax.all_to_all(summed, "req", split_axis=0, concat_axis=1, tiled=True)
    state = residual.astype(jnp.float32) + projected
    return experts(state, norm_gain, routes, route_weights, gate_up[0], down[0])


def solution(mesh):
    in_specs = (
        P("req", "kvh"),
        P("req", "kvh", None, None),
        P("req", "kvh", None, None),
        P("req"),
        P("kvh", "req"),
        P(("req", "kvh"), None),
        P(),
        P(("req", "kvh"), None, None),
        P(("req", "kvh"), None, None),
        P(("req", "kvh"), None),
        P(("req", "kvh"), None),
    )
    out_specs = P(("req", "kvh"), None)
    return jax.shard_map(body, mesh=mesh, in_specs=in_specs, out_specs=out_specs, check_vma=False)
```

```python
import math

import jax
import jax.numpy as jnp
from jax import lax
from jax.experimental import pallas as pl
from jax.experimental.pallas import tpu as pltpu
from jax.sharding import PartitionSpec as P


K_STEP = 37
K_INV = 45
N_DEV = 128
MESH = pl.DeviceIdType.MESH


def coords():
    r = lax.axis_index("req")
    k = lax.axis_index("kvh")
    return lax.rem(r, 2) * 2 + k // 2, r // 8, lax.rem(r // 2, 4), lax.rem(k, 2)


def place(x, y, z, c):
    x, y, z, c = lax.rem(x, 4), lax.rem(y, 4), lax.rem(z, 4), lax.rem(c, 2)
    return ((y * 4 + z) * 2 + x // 2, lax.rem(x, 2) * 2 + c)


def iota(shape, dim):
    return lax.broadcasted_iota(jnp.int32, shape, dim)


def route_keys(expert, token, routes_smem, me):
    slot = jnp.zeros_like(expert)
    for t in range(12):
        for k in range(8):
            slot = slot + jnp.where((expert == routes_smem[t, k]) & (token > t), 1, 0)
    key = (((expert - me + N_DEV) * K_INV) & (N_DEV - 1)) * 2 + slot
    return jnp.where(token < 12, key, -1)


def kernel(
    queries_ref, keys_hbm, values_hbm, lengths_smem, o_proj_hbm, residual_ref, gain_ref, routes_smem, routes_ref,
    weights_ref, gate_up_hbm, down_hbm,
    out_ref,
    keys, values, heads, attended, gathered, projection, partial, pieces, collected, state, routes_padded,
    weights_padded, gate_up, down, sent, received, rows, active, permuted, results, returned, normed, mix, table,
    cache_sem, weight_sem, o_own_sem, o_send_sem, o_recv_sem, a_send_sem, a_recv_sem, p_send_sem, p_recv_sem,
    send_sem, recv_sem, back_sem, return_sem, along_y, along_z,
):
    r, kv = lax.axis_index("req"), lax.axis_index("kvh")
    me = r * 4 + kv
    x, y, z, c = coords()
    at = lax.rem(r, 8)
    bf16, f32 = jnp.bfloat16, jnp.float32

    barrier = pltpu.get_barrier_semaphore()
    for dx in range(4):
        for dc in range(2):
            if dx or dc:
                pl.semaphore_signal(barrier, inc=1, device_id=place(x + dx, y, z, c + dc), device_id_type=MESH)
    for d in range(1, 4):
        pl.semaphore_signal(barrier, inc=1, device_id=place(x, y + d, z, c), device_id_type=MESH)
        pl.semaphore_signal(barrier, inc=1, device_id=place(x, y, z + d, c), device_id_type=MESH)

    def cache_load(g, which):
        source, target = ((keys_hbm, keys), (values_hbm, values))[which]
        part = pl.ds(g * 12, 12)
        return pltpu.make_async_copy(source.at[part], target.at[part], cache_sem.at[which, g])

    for g in range(4):
        cache_load(g, 0).start()
        cache_load(g, 1).start()
    o_own = pltpu.make_async_copy(o_proj_hbm, projection.at[:, pl.ds(0, 128)], o_own_sem)
    o_own.start()
    loads = [
        pltpu.make_async_copy(gate_up_hbm, gate_up, weight_sem.at[0]),
        pltpu.make_async_copy(down_hbm, down, weight_sem.at[1]),
    ]
    for load in loads:
        load.start()
    for h in range(16):
        heads[:, h, :] = queries_ref[:, h * 128 : (h + 1) * 128].astype(f32)

    pl.semaphore_wait(barrier, 13)
    for d in range(1, 4):
        pltpu.make_async_remote_copy(
            src_ref=o_proj_hbm, dst_ref=projection.at[:, pl.ds(d * 128, 128)], send_sem=o_send_sem.at[d - 1],
            recv_sem=o_recv_sem, device_id=place(x, y + d, z, c), device_id_type=MESH,
        ).start()
    for d in range(1, 4):
        pl.semaphore_signal(along_y, inc=1, device_id=place(x, y + d, z, c), device_id_type=MESH)

    position = iota((16, 192), 1)

    def attend(g, carry):
        cache_load(g, 0).wait()
        cache_load(g, 1).wait()
        for b in range(12):
            i = g * 12 + b
            scores = lax.dot_general(
                heads[i].astype(bf16), keys[i], (((1,), (1,)), ((), ())), preferred_element_type=f32
            ) * (1.0 / math.sqrt(128.0))
            scores = jnp.where(position < lengths_smem[i], scores, -1e30)
            shifted = jnp.exp(scores - jnp.max(scores, axis=1, keepdims=True))
            shares = (shifted / jnp.sum(shifted, axis=1, keepdims=True)).astype(bf16)
            attended[i] = jnp.dot(shares, values[i], preferred_element_type=f32)
        return carry

    lax.fori_loop(0, 4, attend, 0)
    pl.semaphore_wait(along_y, 3)
    for d in range(1, 4):
        pl.semaphore_signal(along_z, inc=1, device_id=place(x, y, z + d, c), device_id_type=MESH)
    for h in range(16):
        gathered[0, :, h * 128 : (h + 1) * 128] = attended[:, h, :].astype(bf16)
    pl.semaphore_wait(along_z, 3)

    for d in range(1, 8):
        to = (y * 8 + lax.rem(at + d, 8), kv)
        pltpu.make_async_remote_copy(
            src_ref=gathered.at[0], dst_ref=gathered.at[d], send_sem=a_send_sem.at[d - 1],
            recv_sem=a_recv_sem, device_id=to, device_id_type=MESH,
        ).start()

    routes_padded[...] = jnp.zeros((16, 8), jnp.int32)
    routes_padded[:12, :] = routes_ref[...]
    weights_padded[...] = jnp.zeros((16, 8), f32)
    weights_padded[:12, :] = weights_ref[...]
    state[...] = jnp.zeros((16, 4096), f32)
    state[:12, :] = residual_ref[...].astype(f32)
    partial[384:, :] = jnp.zeros((8, 512), f32)

    lane = iota((8, 128), 1)
    sub = iota((8, 128), 0)
    token = lane & 15
    expert = jnp.full((8, 128), -1, jnp.int32)
    for t in range(12):
        for k in range(8):
            expert = jnp.where((sub == k) & (token == t), routes_smem[t, k], expert)
    keys_row = route_keys(expert, token, routes_smem, me)
    for part in range(8):
        row = iota((256, 128), 0) + part * 256
        hit = jnp.zeros((256, 128), f32)
        for k in range(8):
            hit = jnp.where(row // 8 == keys_row[k : k + 1, :], 1.0, hit)
        hit = jnp.where((row & 7) == iota((256, 128), 1) // 16, hit, 0.0)
        table[part * 256 : (part + 1) * 256, :] = hit.astype(bf16)

    expert_column = jnp.concatenate([routes_padded[...]] * 8, axis=0)
    token_column = iota((128, 8), 0) & 15
    key_column = route_keys(expert_column, token_column, routes_smem, me)
    gates = jnp.concatenate([weights_padded[...]] * 8, axis=0)
    for part in range(8):
        column = iota((128, 256), 1) + part * 256
        share = jnp.zeros((128, 256), f32)
        for k in range(8):
            share = jnp.where(column // 8 == key_column[:, k : k + 1], gates[:, k : k + 1], share)
        share = jnp.where((column & 7) == iota((128, 256), 0) // 16, share, 0.0)
        high = share.astype(bf16)
        mix[:128, part * 256 : (part + 1) * 256] = high
        mix[128:, part * 256 : (part + 1) * 256] = (share - high.astype(f32)).astype(bf16)

    o_own.wait()
    landed = projection.at[:, pl.ds(128, 384)]
    pltpu.make_async_copy(landed, landed, o_recv_sem).wait()
    landed = gathered.at[pl.ds(1, 7)]
    pltpu.make_async_copy(landed, landed, a_recv_sem).wait()
    for n in range(2):
        columns = slice(n * 256, (n + 1) * 256)
        partial[:384, columns] = jnp.dot(
            gathered[...].reshape(384, 2048), projection[:, columns], preferred_element_type=f32
        )
    for d in range(8):
        for k in range(4):
            start = ((8 - d) % 8) * 48 + k * 12
            pieces[d, k] = partial[start : start + 16, :].astype(bf16)

    def hand_out(q, carry):
        d, e = q // 4, lax.rem(q, 4)
        to = lax.rem(kv + e, 4)
        pltpu.make_async_remote_copy(
            src_ref=pieces.at[d, to], dst_ref=collected.at[q], send_sem=p_send_sem, recv_sem=p_recv_sem,
            device_id=(y * 8 + lax.rem(at + d, 8), to), device_id_type=MESH,
        ).start()
        return carry

    lax.fori_loop(1, 32, hand_out, 0)
    collected[0] = pieces[0, kv]
    landed = collected.at[pl.ds(1, 31)]
    pltpu.make_async_copy(landed, landed, p_recv_sem).wait()
    square = jnp.zeros((16, 128), f32)
    for p in range(8):
        slot = lax.rem(at + 8 - p, 8) * 4
        for w in range(4):
            piece = pl.ds(pl.multiple_of(lax.rem(y + 4 - w, 4) * 128, 128), 128)
            total = collected[slot, :, piece].astype(f32)
            for e in range(1, 4):
                total = total + collected[slot + e, :, piece].astype(f32)
            columns = slice((w * 8 + p) * 128, (w * 8 + p + 1) * 128)
            total = state[:, columns] + total
            state[:, columns] = total
            square = square + total * total
    factor = lax.rsqrt(jnp.sum(square, axis=1, keepdims=True) * (1.0 / 4096.0) + 1e-06)
    for s in range(8):
        columns = slice(s * 512, (s + 1) * 512)
        normed[s * 16 : (s + 1) * 16, :] = (state[:, columns] * factor * gain_ref[:, columns]).astype(bf16)

    for part in range(8):
        block = jnp.dot(
            table[part * 256 : (part + 1) * 256, :], normed[...], preferred_element_type=f32
        ).astype(bf16)
        sent[part * 16 : (part + 1) * 16] = block.reshape(16, 16, 512)

    def send(d, carry):
        to = lax.rem(me + d * K_STEP, N_DEV)
        group = d // 64
        pltpu.make_async_remote_copy(
            src_ref=sent.at[d], dst_ref=received.at[d], send_sem=send_sem.at[group],
            recv_sem=recv_sem.at[group], device_id=(to // 4, lax.rem(to, 4)), device_id_type=MESH,
        ).start()
        return carry

    lax.fori_loop(1, N_DEV, send, 0)
    received[0] = sent[0]

    i, j = iota((256, 256), 0), iota((256, 256), 1)
    spread = jnp.where(j == (i & 31) * 8 + i // 32, 1.0, 0.0).astype(bf16)
    gather = jnp.where(i == (j & 31) * 8 + j // 32, 1.0, 0.0).astype(bf16)

    for group in range(2):
        first = 1 if group == 0 else 64
        landed = received.at[pl.ds(first, 64 * (group + 1) - first)]
        pltpu.make_async_copy(landed, landed, recv_sem.at[group]).wait()
        for chunk in range(4):
            block = received[group * 64 + chunk * 16 : group * 64 + (chunk + 1) * 16].reshape(256, 512)
            block = jnp.dot(spread, block, preferred_element_type=f32).astype(bf16)
            for s in range(8):
                rows[chunk * 32 : (chunk + 1) * 32, s * 512 : (s + 1) * 512] = block[s * 32 : (s + 1) * 32]
        if group == 0:
            loads[0].wait()
        for n in range(3):
            gate = jnp.dot(rows[...], gate_up[:, n * 256 : (n + 1) * 256], preferred_element_type=f32)
            up = jnp.dot(rows[...], gate_up[:, 768 + n * 256 : 768 + (n + 1) * 256], preferred_element_type=f32)
            active[:, n * 256 : (n + 1) * 256] = (gate / (1.0 + jnp.exp(-gate)) * up).astype(bf16)
        if group == 0:
            loads[1].wait()
        for s in range(8):
            part = jnp.dot(active[...], down[:, s * 512 : (s + 1) * 512], preferred_element_type=f32).astype(bf16)
            for chunk in range(4):
                permuted[chunk, s * 32 : (s + 1) * 32, :] = part[chunk * 32 : (chunk + 1) * 32]
        for chunk in range(4):
            block = jnp.dot(gather, permuted[chunk], preferred_element_type=f32).astype(bf16)
            results[group * 64 + chunk * 16 : group * 64 + (chunk + 1) * 16] = block.reshape(16, 16, 512)

        def send_back(d, carry):
            to = lax.rem(me + N_DEV * K_STEP - d * K_STEP, N_DEV)
            pltpu.make_async_remote_copy(
                src_ref=results.at[d], dst_ref=returned.at[d], send_sem=back_sem.at[0],
                recv_sem=return_sem.at[0], device_id=(to // 4, lax.rem(to, 4)), device_id_type=MESH,
            ).start()
            return carry

        lax.fori_loop(first, 64 * (group + 1), send_back, 0)
        if group == 0:
            returned[0] = results[0]

    landed = returned.at[pl.ds(1, 127)]
    pltpu.make_async_copy(landed, landed, return_sem.at[0]).wait()
    both = jnp.dot(mix[...], returned[...].reshape(2048, 512), preferred_element_type=f32)
    blended = both[:128] + both[128:]
    for s in range(8):
        columns = slice(s * 512, (s + 1) * 512)
        total = state[:, columns] + blended[s * 16 : (s + 1) * 16]
        out_ref[:, columns] = total[:12].astype(bf16)
    gone = sent.at[pl.ds(1, 63)]
    pltpu.make_async_copy(gone, gone, send_sem.at[0]).wait()
    gone = sent.at[pl.ds(64, 64)]
    pltpu.make_async_copy(gone, gone, send_sem.at[1]).wait()
    gone = results.at[pl.ds(1, 127)]
    pltpu.make_async_copy(gone, gone, back_sem.at[0]).wait()
    for d in range(1, 4):
        pltpu.make_async_copy(o_proj_hbm, projection.at[:, pl.ds(d * 128, 128)], o_send_sem.at[d - 1]).wait()
        pltpu.make_async_copy(gathered.at[0], gathered.at[d], a_send_sem.at[d - 1]).wait()
    for d in range(4, 8):
        pltpu.make_async_copy(gathered.at[0], gathered.at[d], a_send_sem.at[d - 1]).wait()
    gone = collected.at[pl.ds(1, 31)]
    pltpu.make_async_copy(gone, gone, p_send_sem).wait()


def body(
    queries, keys, values, lengths, o_proj, residual, norm_gain, gate_up, down, routes, route_weights,
):
    bf16, f32 = jnp.bfloat16, jnp.float32
    vmem = pl.BlockSpec(memory_space=pltpu.VMEM)
    smem = pl.BlockSpec(memory_space=pltpu.SMEM)
    hbm = pl.BlockSpec(memory_space=pl.ANY)
    dma, plain = pltpu.SemaphoreType.DMA, pltpu.SemaphoreType.REGULAR
    return pl.pallas_call(
        kernel,
        out_shape=jax.ShapeDtypeStruct((12, 4096), bf16),
        in_specs=[vmem, hbm, hbm, smem, hbm, vmem, vmem, smem, vmem, vmem, hbm, hbm],
        out_specs=vmem,
        scratch_shapes=[
            pltpu.VMEM((48, 192, 128), bf16),
            pltpu.VMEM((48, 192, 128), bf16),
            pltpu.VMEM((48, 16, 128), f32),
            pltpu.VMEM((48, 16, 128), f32),
            pltpu.VMEM((8, 48, 2048), bf16),
            pltpu.VMEM((2048, 512), bf16),
            pltpu.VMEM((392, 512), f32),
            pltpu.VMEM((8, 4, 16, 512), bf16),
            pltpu.VMEM((32, 16, 512), bf16),
            pltpu.VMEM((16, 4096), f32),
            pltpu.VMEM((16, 8), jnp.int32),
            pltpu.VMEM((16, 8), f32),
            pltpu.VMEM((4096, 1536), bf16),
            pltpu.VMEM((768, 4096), bf16),
            pltpu.VMEM((128, 16, 512), bf16),
            pltpu.VMEM((128, 16, 512), bf16),
            pltpu.VMEM((128, 4096), bf16),
            pltpu.VMEM((128, 768), bf16),
            pltpu.VMEM((4, 256, 512), bf16),
            pltpu.VMEM((128, 16, 512), bf16),
            pltpu.VMEM((128, 16, 512), bf16),
            pltpu.VMEM((128, 512), bf16),
            pltpu.VMEM((256, 2048), bf16),
            pltpu.VMEM((2048, 128), bf16),
            dma((2, 4)), dma((2,)), dma, dma((3,)), dma, dma((7,)), dma, dma, dma,
            dma((2,)), dma((2,)), dma((1,)), dma((1,)), plain, plain,
        ],
        compiler_params=pltpu.CompilerParams(
            collective_id=1, has_side_effects=True, vmem_limit_bytes=60 * 2**20
        ),
        cost_estimate=pl.CostEstimate(flops=6 * 10**9, bytes_accessed=3 * 10**7, transcendentals=10**6),
        name="layer",
    )(
        queries, keys[:, 0], values[:, 0], lengths, o_proj, residual, norm_gain[None, :], routes, routes,
        route_weights, gate_up[0], down[0],
    )


def solution(mesh):
    in_specs = (
        P("req", "kvh"),
        P("req", "kvh", None, None),
        P("req", "kvh", None, None),
        P("req"),
        P("kvh", "req"),
        P(("req", "kvh"), None),
        P(),
        P(("req", "kvh"), None, None),
        P(("req", "kvh"), None, None),
        P(("req", "kvh"), None),
        P(("req", "kvh"), None),
    )
    out_specs = P(("req", "kvh"), None)
    return jax.shard_map(body, mesh=mesh, in_specs=in_specs, out_specs=out_specs, check_vma=False)
```

```python
import math

import jax
import jax.numpy as jnp
from jax import lax
from jax.experimental import pallas as pl
from jax.experimental.pallas import tpu as pltpu
from jax.sharding import PartitionSpec as P


K_STEP = 37
K_INV = 45
N_DEV = 128
MESH = pl.DeviceIdType.MESH


def coords():
    r = lax.axis_index("req")
    k = lax.axis_index("kvh")
    return lax.rem(r, 2) * 2 + k // 2, r // 8, lax.rem(r // 2, 4), lax.rem(k, 2)


def place(x, y, z, c):
    x, y, z, c = lax.rem(x, 4), lax.rem(y, 4), lax.rem(z, 4), lax.rem(c, 2)
    return ((y * 4 + z) * 2 + x // 2, lax.rem(x, 2) * 2 + c)


def iota(shape, dim):
    return lax.broadcasted_iota(jnp.int32, shape, dim)


def kernel(
    queries_ref, keys_hbm, values_hbm, lengths_smem, o_proj_hbm, residual_ref, gain_ref, routes_smem, weights_smem,
    gate_up_hbm, down_hbm,
    out_ref,
    keys, values, heads, attended, gathered, projection, partial, staged, pieces, collected, summed, state, gate_up, down, sent, received, rows, active, permuted, results, returned, normed, mix, table,
    cache_sem, weight_sem, o_own_sem, o_send_sem, o_recv_sem, a_send_sem, a_recv_sem, p_send_sem, p_recv_sem,
    send_sem, recv_sem, back_sem, return_sem, along_y, along_z,
):
    r, kv = lax.axis_index("req"), lax.axis_index("kvh")
    me = r * 4 + kv
    x, y, z, c = coords()
    half = lax.rem(r, 2)
    bf16, f32 = jnp.bfloat16, jnp.float32

    barrier = pltpu.get_barrier_semaphore()
    for dx in range(4):
        for dc in range(2):
            if dx or dc:
                pl.semaphore_signal(barrier, inc=1, device_id=place(x + dx, y, z, c + dc), device_id_type=MESH)
    for d in range(1, 4):
        pl.semaphore_signal(barrier, inc=1, device_id=place(x, y + d, z, c), device_id_type=MESH)
        pl.semaphore_signal(barrier, inc=1, device_id=place(x, y, z + d, c), device_id_type=MESH)

    def cache_load(m, which):
        source, target = ((keys_hbm, keys), (values_hbm, values))[which]
        part = pl.ds(m * 16, 16)
        return pltpu.make_async_copy(source.at[part], target.at[part], cache_sem.at[which, m])

    for m in range(3):
        cache_load(m, 0).start()
        cache_load(m, 1).start()
    o_own = pltpu.make_async_copy(o_proj_hbm, projection.at[:, pl.ds(0, 128)], o_own_sem)
    o_own.start()
    loads = [
        pltpu.make_async_copy(gate_up_hbm, gate_up, weight_sem.at[0]),
        pltpu.make_async_copy(down_hbm, down, weight_sem.at[1]),
    ]
    for load in loads:
        load.start()
    for h in range(16):
        heads[:, h, :] = queries_ref[:, h * 128 : (h + 1) * 128].astype(f32)

    def o_copy(source, slot, part, n, dy, rows):
        return pltpu.make_async_remote_copy(
            src_ref=source, dst_ref=projection.at[pl.ds(part * 1024, rows), pl.ds(slot * 128, 128)],
            send_sem=o_send_sem.at[n], recv_sem=o_recv_sem.at[n], device_id=place(x, y + dy, z, c),
            device_id_type=MESH,
        )

    def o_first(n):
        slot, part, dy = ((1, 0, 1), (3, 1, 3), (1, 1, 1), (3, 0, 3))[n]
        return o_copy(o_proj_hbm.at[pl.ds(part * 1024, 1024)], slot, part, n, dy, 1024)

    def o_pass(n):
        slot, part, dy = ((1, 0, 1), (3, 1, 3))[n]
        held = projection.at[pl.ds(part * 1024, 1024), pl.ds(slot * 128, 128)]
        return o_copy(held, 2, part, 4 + n, dy, 1024)

    pl.semaphore_wait(barrier, 13)
    for n in range(4):
        o_first(n).start()
    for d in range(1, 4):
        pl.semaphore_signal(along_y, inc=1, device_id=place(x, y + d, z, c), device_id_type=MESH)

    position = iota((192, 128), 0)
    request = iota((128, 128), 1) // 16

    def attend(g):
        first = g * 8
        turned = jnp.transpose(heads[first : first + 8].reshape(128, 128))
        scores = jnp.zeros((192, 128), f32)
        for b in range(0, 8, 2):
            two = jnp.concatenate([keys[first + b], keys[first + b + 1]], axis=1)
            asked = jnp.concatenate(
                [jnp.where(request == b, turned, 0.0), jnp.where(request == b + 1, turned, 0.0)], axis=0
            ).astype(bf16)
            scores = scores + jnp.dot(two, asked, preferred_element_type=f32)
        scores = scores * (1.0 / math.sqrt(128.0))
        limit = jnp.zeros((1, 128), jnp.int32)
        for b in range(8):
            limit = jnp.where(request[:1] == b, lengths_smem[first + b], limit)
        scores = jnp.where(position < limit, scores, -1e30)
        shifted = jnp.exp(scores - jnp.max(scores, axis=0, keepdims=True))
        shares = shifted / jnp.sum(shifted, axis=0, keepdims=True)
        shares = jnp.transpose(shares).astype(bf16)
        for b in range(8):
            attended[first + b] = jnp.dot(
                shares[b * 16 : (b + 1) * 16], values[first + b], preferred_element_type=f32
            )

    def a_copy(slot, m, dz, dh):
        part = pl.ds(m * 16, 16)
        to = ((y * 4 + lax.rem(z + dz, 4)) * 2 + lax.rem(half + dh, 2), kv)
        return pltpu.make_async_remote_copy(
            src_ref=gathered.at[slot, part], dst_ref=gathered.at[slot + dz * 2 + dh, part], send_sem=a_send_sem,
            recv_sem=a_recv_sem.at[m, slot + dz * 2 + dh], device_id=to, device_id_type=MESH,
        )

    def a_wait(m, slot):
        landed = gathered.at[slot, pl.ds(m * 16, 16)]
        pltpu.make_async_copy(landed, landed, a_recv_sem.at[m, slot]).wait()

    def a_start(m):
        rows_here = slice(m * 16, (m + 1) * 16)
        for h in range(16):
            gathered[0, rows_here, h * 128 : (h + 1) * 128] = attended[rows_here, h, :].astype(bf16)

    def a_send(m):
        a_copy(0, m, 0, 1).start()
        for dz in (1, 3, 2):
            a_copy(0, m, dz, 0).start()

    for m in range(3):
        cache_load(m, 0).wait()
        cache_load(m, 1).wait()
        attend(2 * m)
        attend(2 * m + 1)
        a_start(m)
        if m == 0:
            pl.semaphore_wait(along_y, 3)
            for d in range(1, 4):
                pl.semaphore_signal(along_z, inc=1, device_id=place(x, y, z + d, c), device_id_type=MESH)
            pl.semaphore_wait(along_z, 3)
        a_send(m)
    for n in range(2):
        pltpu.make_async_copy(o_proj_hbm.at[pl.ds(0, 1024)], projection.at[pl.ds(0, 1024), pl.ds(128, 128)], o_recv_sem.at[n]).wait()
        o_pass(n).start()
    a_wait(0, 1)
    for dz in (1, 3, 2):
        a_copy(1, 0, dz, 0).start()
    for m in (1, 2):
        for dz in (1, 3, 2):
            a_wait(m, dz * 2)
            a_copy(dz * 2, m, 0, 1).start()

    state[...] = jnp.zeros((16, 4096), f32)
    state[:12, :] = residual_ref[...].astype(f32)

    lane = iota((8, 128), 1)
    sub = iota((8, 128), 0)
    token = lane & 15
    expert = jnp.full((8, 128), -1, jnp.int32)
    gates = jnp.zeros((8, 128), f32)
    for t in range(12):
        for k in range(8):
            here = (sub == k) & (token == t)
            expert = jnp.where(here, routes_smem[k, t], expert)
            gates = jnp.where(here, weights_smem[k, t], gates)
    slot_of = jnp.zeros((8, 128), jnp.int32)
    for t in range(12):
        for k in range(8):
            slot_of = slot_of + jnp.where((expert == routes_smem[k, t]) & (token > t), 1, 0)
    keys_row = (((expert - me + N_DEV) * K_INV) & (N_DEV - 1)) * 2 + slot_of
    keys_row = jnp.where(token < 12, keys_row, -1)
    for part in range(8):
        row = iota((256, 128), 0) + part * 256
        hit = jnp.zeros((256, 128), f32)
        for k in range(8):
            hit = jnp.where(row // 8 == keys_row[k : k + 1, :], 1.0, hit)
        hit = jnp.where((row & 7) == iota((256, 128), 1) // 16, hit, 0.0)
        table[part * 256 : (part + 1) * 256, :] = hit.astype(bf16)

    key_column = jnp.transpose(keys_row.astype(f32)).astype(jnp.int32)
    gates = jnp.transpose(gates)
    for part in range(8):
        column = iota((128, 256), 1) + part * 256
        share = jnp.zeros((128, 256), f32)
        for k in range(8):
            share = jnp.where(column // 8 == key_column[:, k : k + 1], gates[:, k : k + 1], share)
        share = jnp.where((column & 7) == iota((128, 256), 0) // 16, share, 0.0)
        high = share.astype(bf16)
        mix[:128, part * 256 : (part + 1) * 256] = high
        mix[128:, part * 256 : (part + 1) * 256] = (share - high.astype(f32)).astype(bf16)

    o_own.wait()
    for n in range(2, 6):
        pltpu.make_async_copy(o_proj_hbm.at[pl.ds(0, 1024)], projection.at[pl.ds(0, 1024), pl.ds(128, 128)], o_recv_sem.at[n]).wait()
    for m in range(3):
        for slot in range(1, 8):
            if not (slot == 1 and m == 0 or slot in (2, 4, 6) and m > 0):
                a_wait(m, slot)
    for n in range(2):
        columns = slice(n * 256, (n + 1) * 256)
        partial[:, columns] = jnp.dot(
            gathered[...].reshape(384, 2048), projection[:, columns], preferred_element_type=f32
        )
    for d in range(8):
        slot = ((4 - d // 2) % 4) * 2 + d % 2
        for k in range(4):
            for w in range(4):
                staged[d * 4 + k, w * 12 : (w + 1) * 12, :] = partial[
                    slot * 48 + k * 12 : slot * 48 + (k + 1) * 12, w * 128 : (w + 1) * 128
                ]
        pieces[d * 4 : d * 4 + 4] = staged[d * 4 : d * 4 + 4].astype(bf16)

    def hand_out(q, carry):
        d, e = q // 4, lax.rem(q, 4)
        to = lax.rem(kv + e, 4)
        there = (y * 4 + lax.rem(z + d // 2, 4)) * 2 + lax.rem(half + lax.rem(d, 2), 2)
        pltpu.make_async_remote_copy(
            src_ref=pieces.at[d * 4 + to], dst_ref=collected.at[q], send_sem=p_send_sem, recv_sem=p_recv_sem,
            device_id=(there, to), device_id_type=MESH,
        ).start()
        return carry

    lax.fori_loop(1, 32, hand_out, 0)
    collected[0] = pieces[kv]
    landed = collected.at[pl.ds(1, 31)]
    pltpu.make_async_copy(landed, landed, p_recv_sem).wait()
    square = jnp.zeros((12, 128), f32)
    for p in range(8):
        slot = (lax.rem(z + 4 - p // 2, 4) * 2 + lax.rem(half + p % 2, 2)) * 4
        total = collected[slot].astype(f32)
        for e in range(1, 4):
            total = total + collected[slot + e].astype(f32)
        summed[p] = total
        for w in range(4):
            columns = pl.ds(pl.multiple_of((lax.rem(y + 4 - w, 4) * 8 + p) * 128, 128), 128)
            total = state[:12, columns] + summed[p, w * 12 : (w + 1) * 12, :]
            state[:12, columns] = total
            square = square + total * total
    factor = lax.rsqrt(jnp.sum(square, axis=1, keepdims=True) * (1.0 / 4096.0) + 1e-06)
    normed[...] = jnp.zeros((128, 512), bf16)
    for s in range(8):
        columns = slice(s * 512, (s + 1) * 512)
        normed[s * 16 : s * 16 + 12, :] = (state[:12, columns] * factor * gain_ref[:, columns]).astype(bf16)

    for part in range(8):
        block = jnp.dot(
            table[part * 256 : (part + 1) * 256, :], normed[...], preferred_element_type=f32
        ).astype(bf16)
        sent[part * 16 : (part + 1) * 16] = block.reshape(16, 16, 512)

    def send(d, carry):
        to = lax.rem(me + d * K_STEP, N_DEV)
        group = d // 64
        pltpu.make_async_remote_copy(
            src_ref=sent.at[d], dst_ref=received.at[d], send_sem=send_sem.at[group],
            recv_sem=recv_sem.at[group], device_id=(to // 4, lax.rem(to, 4)), device_id_type=MESH,
        ).start()
        return carry

    lax.fori_loop(1, N_DEV, send, 0)
    received[0] = sent[0]

    i, j = iota((256, 256), 0), iota((256, 256), 1)
    spread = jnp.where(j == (i & 31) * 8 + i // 32, 1.0, 0.0).astype(bf16)
    gather = jnp.where(i == (j & 31) * 8 + j // 32, 1.0, 0.0).astype(bf16)

    for group in range(2):
        first = 1 if group == 0 else 64
        landed = received.at[pl.ds(first, 64 * (group + 1) - first)]
        pltpu.make_async_copy(landed, landed, recv_sem.at[group]).wait()
        for chunk in range(4):
            block = received[group * 64 + chunk * 16 : group * 64 + (chunk + 1) * 16].reshape(256, 512)
            block = jnp.dot(spread, block, preferred_element_type=f32).astype(bf16)
            for s in range(8):
                rows[chunk * 32 : (chunk + 1) * 32, s * 512 : (s + 1) * 512] = block[s * 32 : (s + 1) * 32]
        if group == 0:
            loads[0].wait()
        for n in range(3):
            gate = jnp.dot(rows[...], gate_up[:, n * 256 : (n + 1) * 256], preferred_element_type=f32)
            up = jnp.dot(rows[...], gate_up[:, 768 + n * 256 : 768 + (n + 1) * 256], preferred_element_type=f32)
            active[:, n * 256 : (n + 1) * 256] = (gate / (1.0 + jnp.exp(-gate)) * up).astype(bf16)
        if group == 0:
            loads[1].wait()
        for s in range(8):
            part = jnp.dot(active[...], down[:, s * 512 : (s + 1) * 512], preferred_element_type=f32).astype(bf16)
            for chunk in range(4):
                permuted[chunk, s * 32 : (s + 1) * 32, :] = part[chunk * 32 : (chunk + 1) * 32]
        for chunk in range(4):
            block = jnp.dot(gather, permuted[chunk], preferred_element_type=f32).astype(bf16)
            results[group * 64 + chunk * 16 : group * 64 + (chunk + 1) * 16] = block.reshape(16, 16, 512)

        def send_back(d, carry):
            to = lax.rem(me + N_DEV * K_STEP - d * K_STEP, N_DEV)
            pltpu.make_async_remote_copy(
                src_ref=results.at[d], dst_ref=returned.at[d], send_sem=back_sem.at[0],
                recv_sem=return_sem.at[0], device_id=(to // 4, lax.rem(to, 4)), device_id_type=MESH,
            ).start()
            return carry

        lax.fori_loop(first, 64 * (group + 1), send_back, 0)
        if group == 0:
            returned[0] = results[0]

    landed = returned.at[pl.ds(1, 127)]
    pltpu.make_async_copy(landed, landed, return_sem.at[0]).wait()
    both = jnp.dot(mix[...], returned[...].reshape(2048, 512), preferred_element_type=f32)
    blended = both[:128] + both[128:]
    for s in range(8):
        columns = slice(s * 512, (s + 1) * 512)
        total = state[:, columns] + blended[s * 16 : (s + 1) * 16]
        out_ref[:, columns] = total[:12].astype(bf16)
    gone = sent.at[pl.ds(1, 63)]
    pltpu.make_async_copy(gone, gone, send_sem.at[0]).wait()
    gone = sent.at[pl.ds(64, 64)]
    pltpu.make_async_copy(gone, gone, send_sem.at[1]).wait()
    gone = results.at[pl.ds(1, 127)]
    pltpu.make_async_copy(gone, gone, back_sem.at[0]).wait()
    for n in range(6):
        pltpu.make_async_copy(o_proj_hbm.at[pl.ds(0, 1024)], projection.at[pl.ds(0, 1024), pl.ds(128, 128)], o_send_sem.at[n]).wait()
    gone = gathered.at[pl.ds(1, 7)]
    pltpu.make_async_copy(gone, gone, a_send_sem).wait()
    gone = collected.at[pl.ds(1, 31)]
    pltpu.make_async_copy(gone, gone, p_send_sem).wait()


def body(
    queries, keys, values, lengths, o_proj, residual, norm_gain, gate_up, down, routes, route_weights,
):
    bf16, f32 = jnp.bfloat16, jnp.float32
    vmem = pl.BlockSpec(memory_space=pltpu.VMEM)
    smem = pl.BlockSpec(memory_space=pltpu.SMEM)
    hbm = pl.BlockSpec(memory_space=pl.ANY)
    dma, plain = pltpu.SemaphoreType.DMA, pltpu.SemaphoreType.REGULAR
    return pl.pallas_call(
        kernel,
        out_shape=jax.ShapeDtypeStruct((12, 4096), bf16),
        in_specs=[vmem, hbm, hbm, smem, hbm, vmem, vmem, smem, smem, hbm, hbm],
        out_specs=vmem,
        scratch_shapes=[
            pltpu.VMEM((48, 192, 128), bf16),
            pltpu.VMEM((48, 192, 128), bf16),
            pltpu.VMEM((48, 16, 128), f32),
            pltpu.VMEM((48, 16, 128), f32),
            pltpu.VMEM((8, 48, 2048), bf16),
            pltpu.VMEM((2048, 512), bf16),
            pltpu.VMEM((384, 512), f32),
            pltpu.VMEM((32, 48, 128), f32),
            pltpu.VMEM((32, 48, 128), bf16),
            pltpu.VMEM((32, 48, 128), bf16),
            pltpu.VMEM((8, 48, 128), f32),
            pltpu.VMEM((16, 4096), f32),
            pltpu.VMEM((4096, 1536), bf16),
            pltpu.VMEM((768, 4096), bf16),
            pltpu.VMEM((128, 16, 512), bf16),
            pltpu.VMEM((128, 16, 512), bf16),
            pltpu.VMEM((128, 4096), bf16),
            pltpu.VMEM((128, 768), bf16),
            pltpu.VMEM((4, 256, 512), bf16),
            pltpu.VMEM((128, 16, 512), bf16),
            pltpu.VMEM((128, 16, 512), bf16),
            pltpu.VMEM((128, 512), bf16),
            pltpu.VMEM((256, 2048), bf16),
            pltpu.VMEM((2048, 128), bf16),
            dma((2, 3)), dma((2,)), dma, dma((6,)), dma((6,)), dma, dma((3, 8)), dma, dma,
            dma((2,)), dma((2,)), dma((1,)), dma((1,)), plain, plain,
        ],
        compiler_params=pltpu.CompilerParams(
            collective_id=1, has_side_effects=True, vmem_limit_bytes=60 * 2**20
        ),
        cost_estimate=pl.CostEstimate(flops=6 * 10**9, bytes_accessed=3 * 10**7, transcendentals=10**6),
        name="layer",
    )(
        queries, keys[:, 0], values[:, 0], lengths, o_proj, residual, norm_gain[None, :], routes.T,
        route_weights.T, gate_up[0], down[0],
    )


def solution(mesh):
    in_specs = (
        P("req", "kvh"),
        P("req", "kvh", None, None),
        P("req", "kvh", None, None),
        P("req"),
        P("kvh", "req"),
        P(("req", "kvh"), None),
        P(),
        P(("req", "kvh"), None, None),
        P(("req", "kvh"), None, None),
        P(("req", "kvh"), None),
        P(("req", "kvh"), None),
    )
    out_specs = P(("req", "kvh"), None)
    return jax.shard_map(body, mesh=mesh, in_specs=in_specs, out_specs=out_specs, check_vma=False)
```

```python
import math

import jax
import jax.numpy as jnp
from jax import lax
from jax.experimental import pallas as pl
from jax.experimental.pallas import tpu as pltpu
from jax.sharding import PartitionSpec as P


MESH = pl.DeviceIdType.MESH


def coords():
    r = lax.axis_index("req")
    k = lax.axis_index("kvh")
    return lax.rem(r, 2) * 2 + k // 2, r // 8, lax.rem(r // 2, 4), lax.rem(k, 2)


def place(x, y, z, c):
    x, y, z, c = lax.rem(x, 4), lax.rem(y, 4), lax.rem(z, 4), lax.rem(c, 2)
    return ((y * 4 + z) * 2 + x // 2, lax.rem(x, 2) * 2 + c)


def iota(shape, dim):
    return lax.broadcasted_iota(jnp.int32, shape, dim)


WIDTHS = (1536, 1280, 1280)
STARTS = (0, 1536, 2816)


def ahead(axis, d):
    x, y, z, c = coords()
    return ((x, y, z + d, c), (x, y + d, z, c), (x + d, y, z, c))[axis]


def kernel(
    queries_ref, keys_hbm, values_hbm, lengths_smem, o_proj_hbm, residual_ref, gain_ref, routes_smem, weights_smem,
    gate_up_hbm, down_hbm,
    out_ref,
    keys, values, heads, attended, gathered, projection, partial, staged, pieces, collected, summed, state, gate_up,
    down, tiles, line, sent, received, rows, active, results, returned, shared, arrived, table, mix, spread, gather,
    cache_sem, weight_sem, o_own_sem, o_send_sem, o_recv_sem, a_send_sem, a_recv_sem, p_send_sem, p_recv_sem,
    tile_send_sem, tile_recv_sem, line_send_sem, line_recv_sem, send_sem, recv_sem, back_sem, return_sem,
    share_send_sem, share_recv_sem, along_y, along_z,
):
    r, kv = lax.axis_index("req"), lax.axis_index("kvh")
    x, y, z, c = coords()
    half = lax.rem(r, 2)
    bf16, f32 = jnp.bfloat16, jnp.float32

    xs, ys, zs = ([lax.rem(at + d, 4) for d in range(4)] for at in (x, y, z))
    high_x, low_x, cores = [at // 2 for at in xs], [lax.rem(at, 2) * 2 for at in xs], [c, 1 - c]

    def away(dx, dy, dz, dc):
        return ((ys[dy % 4] * 4 + zs[dz % 4]) * 2 + high_x[dx % 4], low_x[dx % 4] + cores[dc])

    barrier = pltpu.get_barrier_semaphore()
    for dx in range(4):
        for dc in range(2):
            if dx or dc:
                pl.semaphore_signal(barrier, inc=1, device_id=place(x + dx, y, z, c + dc), device_id_type=MESH)
    for d in range(1, 4):
        pl.semaphore_signal(barrier, inc=1, device_id=place(x, y + d, z, c), device_id_type=MESH)
        pl.semaphore_signal(barrier, inc=1, device_id=place(x, y, z + d, c), device_id_type=MESH)

    def cache_load(m, which):
        source, target = ((keys_hbm, keys), (values_hbm, values))[which]
        part = pl.ds(m * 16, 16)
        return pltpu.make_async_copy(source.at[part], target.at[part], cache_sem.at[which, m])

    for m in range(3):
        cache_load(m, 0).start()
        cache_load(m, 1).start()
    o_own = pltpu.make_async_copy(o_proj_hbm, projection.at[:, pl.ds(0, 128)], o_own_sem)
    o_own.start()
    loads = [
        pltpu.make_async_copy(gate_up_hbm, gate_up, weight_sem.at[0]),
        pltpu.make_async_copy(down_hbm, down, weight_sem.at[1]),
    ]
    for load in loads:
        load.start()
    for h in range(16):
        heads[:, h, :] = queries_ref[:, h * 128 : (h + 1) * 128].astype(f32)

    def o_copy(source, slot, part, n, dy, rows):
        return pltpu.make_async_remote_copy(
            src_ref=source, dst_ref=projection.at[pl.ds(part * 1024, rows), pl.ds(slot * 128, 128)],
            send_sem=o_send_sem.at[n], recv_sem=o_recv_sem.at[n], device_id=place(x, y + dy, z, c),
            device_id_type=MESH,
        )

    def o_first(n):
        slot, part, dy = ((1, 0, 1), (3, 1, 3), (1, 1, 1), (3, 0, 3))[n]
        return o_copy(o_proj_hbm.at[pl.ds(part * 1024, 1024)], slot, part, n, dy, 1024)

    def o_pass(n):
        slot, part, dy = ((1, 0, 1), (3, 1, 3))[n]
        held = projection.at[pl.ds(part * 1024, 1024), pl.ds(slot * 128, 128)]
        return o_copy(held, 2, part, 4 + n, dy, 1024)

    pl.semaphore_wait(barrier, 13)
    for n in range(4):
        o_first(n).start()
    for d in range(1, 4):
        pl.semaphore_signal(along_y, inc=1, device_id=place(x, y + d, z, c), device_id_type=MESH)

    position = iota((192, 128), 0)
    request = iota((128, 128), 1) // 16

    def attend(g):
        first = g * 8
        turned = jnp.transpose(heads[first : first + 8].reshape(128, 128))
        scores = jnp.zeros((192, 128), f32)
        for b in range(0, 8, 2):
            two = jnp.concatenate([keys[first + b], keys[first + b + 1]], axis=1)
            asked = jnp.concatenate(
                [jnp.where(request == b, turned, 0.0), jnp.where(request == b + 1, turned, 0.0)], axis=0
            ).astype(bf16)
            scores = scores + jnp.dot(two, asked, preferred_element_type=f32)
        scores = scores * (1.0 / math.sqrt(128.0))
        limit = jnp.zeros((1, 128), jnp.int32)
        for b in range(8):
            limit = jnp.where(request[:1] == b, lengths_smem[first + b], limit)
        scores = jnp.where(position < limit, scores, -1e30)
        shifted = jnp.exp(scores - jnp.max(scores, axis=0, keepdims=True))
        shares = shifted / jnp.sum(shifted, axis=0, keepdims=True)
        shares = jnp.transpose(shares).astype(bf16)
        for b in range(8):
            attended[first + b] = jnp.dot(
                shares[b * 16 : (b + 1) * 16], values[first + b], preferred_element_type=f32
            )

    def a_copy(slot, m, dz, dh):
        part = pl.ds(m * 16, 16)
        to = ((y * 4 + lax.rem(z + dz, 4)) * 2 + lax.rem(half + dh, 2), kv)
        return pltpu.make_async_remote_copy(
            src_ref=gathered.at[slot, part], dst_ref=gathered.at[slot + dz * 2 + dh, part], send_sem=a_send_sem,
            recv_sem=a_recv_sem.at[m, slot + dz * 2 + dh], device_id=to, device_id_type=MESH,
        )

    def a_wait(m, slot):
        landed = gathered.at[slot, pl.ds(m * 16, 16)]
        pltpu.make_async_copy(landed, landed, a_recv_sem.at[m, slot]).wait()

    def a_start(m):
        rows_here = slice(m * 16, (m + 1) * 16)
        for h in range(16):
            gathered[0, rows_here, h * 128 : (h + 1) * 128] = attended[rows_here, h, :].astype(bf16)

    def a_send(m):
        a_copy(0, m, 0, 1).start()
        for dz in (1, 3, 2):
            a_copy(0, m, dz, 0).start()

    for m in range(3):
        cache_load(m, 0).wait()
        cache_load(m, 1).wait()
        attend(2 * m)
        attend(2 * m + 1)
        a_start(m)
        if m == 0:
            pl.semaphore_wait(along_y, 3)
            for d in range(1, 4):
                pl.semaphore_signal(along_z, inc=1, device_id=place(x, y, z + d, c), device_id_type=MESH)
            pl.semaphore_wait(along_z, 3)
        a_send(m)
    for n in range(2):
        pltpu.make_async_copy(o_proj_hbm.at[pl.ds(0, 1024)], projection.at[pl.ds(0, 1024), pl.ds(128, 128)], o_recv_sem.at[n]).wait()
        o_pass(n).start()
    a_wait(0, 1)
    for dz in (1, 3, 2):
        a_copy(1, 0, dz, 0).start()
    for m in (1, 2):
        for dz in (1, 3, 2):
            a_wait(m, dz * 2)
            a_copy(dz * 2, m, 0, 1).start()

    state[...] = jnp.zeros((16, 4096), f32)
    state[:12, :] = residual_ref[...].astype(f32)

    lane = iota((8, 128), 1)
    sub = iota((8, 128), 0)
    token = lane & 15
    expert = jnp.full((8, 128), -1, jnp.int32)
    gates = jnp.zeros((8, 128), f32)
    for t in range(12):
        for k in range(8):
            here = (sub == k) & (token == t)
            expert = jnp.where(here, routes_smem[k, t], expert)
            gates = jnp.where(here, weights_smem[k, t], gates)
    place_of = jnp.zeros((8, 128), jnp.int32)
    for t in range(12):
        for k in range(8):
            place_of = place_of + jnp.where((expert == routes_smem[k, t]) & (token > t), 1, 0)
    tiles[9, :8, :] = jnp.where(token < 12, expert * 2 + place_of, -1).astype(f32)
    tiles[9, 8:, :] = gates

    for f in range(3):
        for d in range(1, 4):
            pltpu.make_async_remote_copy(
                src_ref=tiles.at[9], dst_ref=tiles.at[f * 3 + d - 1], send_sem=tile_send_sem, recv_sem=tile_recv_sem,
                device_id=place(*ahead(f, d)), device_id_type=MESH,
            ).start()
        line[f][0] = jnp.zeros((16, WIDTHS[f]), bf16)

    for f in range(3):
        def column(i):
            half_of, n = i // 128, i & 127
            dx, dy, dz, row = n // 32, (n // 8) & 3, (n // 2) & 3, n & 1
            p, q, g = ((dx, dy, dz), (dx, dz, dy), (dy, dz, dx))[f]
            return (p * 4 + q) * 16 + half_of * 8 + g * 2 + row

        i, j = iota((256, 256), 0), iota((256, 256), 1)
        spread[f] = jnp.where(j == column(i), 1.0, 0.0).astype(bf16)
        gather[f] = jnp.where(i == column(j), 1.0, 0.0).astype(bf16)

    landed = tiles.at[pl.ds(0, 9)]
    pltpu.make_async_copy(landed, landed, tile_recv_sem).wait()
    for f in range(3):
        marks = jnp.full((8, 128), -1, jnp.int32)
        gates = jnp.zeros((8, 128), f32)
        for d in range(4):
            tile = tiles[9] if d == 0 else tiles[f * 3 + d - 1]
            marks = jnp.where(lane // 16 == d, tile[:8].astype(jnp.int32), marks)
            gates = jnp.where(lane // 16 == d, tile[8:], gates)
        number = marks // 2
        ring, group = number // 4, number & 3
        dx = ((ring & 1) * 2 + group // 2 + 4 - x) & 3
        dy = (ring // 8 + 4 - y) & 3
        dz = ((ring // 2) & 3) + 4 - z & 3
        dc = ((group & 1) + 2 - c) & 1
        p, q, g = ((dx, dy, dz), (dx, dz, dy), (dy, dz, dx))[f]
        key = ((dc * 16 + p * 4 + q) * 4 + lane // 16) * 2 + (marks & 1)
        key = jnp.where((marks >= 0) & (g == 0), key, -1)
        row = iota((256, 64), 0)
        hit = jnp.zeros((256, 64), f32)
        for k in range(8):
            hit = jnp.where(row == key[k : k + 1, :64], 1.0, hit)
        table[f] = hit.astype(bf16)
        key_column = jnp.transpose(key.astype(f32))[:64].astype(jnp.int32)
        gate_column = jnp.transpose(gates)[:64]
        spot = iota((64, 512), 1)
        share = jnp.zeros((64, 512), f32)
        for k in range(8):
            share = jnp.where(
                (spot // 16) * 8 + (spot & 7) == key_column[:, k : k + 1], gate_column[:, k : k + 1], share
            )
        for h in range(2):
            part = jnp.where((spot // 8) & 1 == h, share, 0.0)
            high = part.astype(bf16)
            mix[f, h, :64, :] = high
            mix[f, h, 64:, :] = (part - high.astype(f32)).astype(bf16)

    o_own.wait()
    for n in range(2, 6):
        pltpu.make_async_copy(o_proj_hbm.at[pl.ds(0, 1024)], projection.at[pl.ds(0, 1024), pl.ds(128, 128)], o_recv_sem.at[n]).wait()
    for m in range(3):
        for slot in range(1, 8):
            if not (slot == 1 and m == 0 or slot in (2, 4, 6) and m > 0):
                a_wait(m, slot)
    def hand_out(q, carry):
        d, e = q // 4, lax.rem(q, 4)
        to = lax.rem(kv + e, 4)
        there = (y * 4 + lax.rem(z + d // 2, 4)) * 2 + lax.rem(half + lax.rem(d, 2), 2)
        pltpu.make_async_remote_copy(
            src_ref=pieces.at[d * 4 + to], dst_ref=collected.at[q], send_sem=p_send_sem, recv_sem=p_recv_sem,
            device_id=(there, to), device_id_type=MESH,
        ).start()
        return carry

    for turn in range(2):
        slots = slice(turn * 4, turn * 4 + 4)
        partial[turn * 192 : (turn + 1) * 192, :] = jnp.dot(
            gathered[slots].reshape(192, 2048), projection[...], preferred_element_type=f32
        )
        for slot in range(turn * 4, turn * 4 + 4):
            d = ((4 - slot // 2) % 4) * 2 + slot % 2
            for k in range(4):
                for w in range(4):
                    staged[d * 4 + k, w * 12 : (w + 1) * 12, :] = partial[
                        slot * 48 + k * 12 : slot * 48 + (k + 1) * 12, w * 128 : (w + 1) * 128
                    ]
            pieces[d * 4 : d * 4 + 4] = staged[d * 4 : d * 4 + 4].astype(bf16)
            lax.fori_loop(d * 4 + (d == 0), d * 4 + 4, hand_out, 0)
    collected[0] = pieces[kv]
    landed = collected.at[pl.ds(1, 31)]
    pltpu.make_async_copy(landed, landed, p_recv_sem).wait()
    square = jnp.zeros((12, 128), f32)
    for p in range(8):
        slot = (lax.rem(z + 4 - p // 2, 4) * 2 + lax.rem(half + p % 2, 2)) * 4
        total = collected[slot].astype(f32)
        for e in range(1, 4):
            total = total + collected[slot + e].astype(f32)
        summed[p] = total
        for w in range(4):
            columns = pl.ds(pl.multiple_of((lax.rem(y + 4 - w, 4) * 8 + p) * 128, 128), 128)
            total = state[:12, columns] + summed[p, w * 12 : (w + 1) * 12, :]
            state[:12, columns] = total
            square = square + total * total
    factor = lax.rsqrt(jnp.sum(square, axis=1, keepdims=True) * (1.0 / 4096.0) + 1e-06)
    for f in range(3):
        columns = slice(STARTS[f], STARTS[f] + WIDTHS[f])
        line[f][0, :12, :] = (state[:12, columns] * factor * gain_ref[:, columns]).astype(bf16)
        for d in (2, 1, 3):
            pltpu.make_async_remote_copy(
                src_ref=line[f].at[0], dst_ref=line[f].at[d], send_sem=line_send_sem.at[f],
                recv_sem=line_recv_sem.at[f], device_id=place(*ahead(f, d)), device_id_type=MESH,
            ).start()

    def across(f, j, sign):
        p, q, dc = sign * (j // 4 % 4), sign * (j % 4), j // 16
        return away(*((p, q, 0, dc), (p, 0, q, dc), (0, p, q, dc))[f])

    for group in range(2):
        blocks = range(group * 16, group * 16 + 16)
        for f in range(3):
            width = WIDTHS[f] // 2
            if group == 0:
                landed = line[f].at[pl.ds(1, 3)]
                pltpu.make_async_copy(landed, landed, line_recv_sem.at[f]).wait()
            block = jnp.dot(
                table[f, group * 128 : (group + 1) * 128], line[f][...].reshape(64, WIDTHS[f]),
                preferred_element_type=f32,
            ).reshape(16, 8, WIDTHS[f])
            sent[f][group * 16 : (group + 1) * 16] = jnp.concatenate(
                [block[:, :, :width], block[:, :, width:]], axis=1
            ).astype(bf16)
            for j in blocks:
                if j:
                    pltpu.make_async_remote_copy(
                        src_ref=sent[f].at[j], dst_ref=received[f].at[j], send_sem=send_sem.at[f],
                        recv_sem=recv_sem.at[f, group], device_id=across(f, j, 1), device_id_type=MESH,
                    ).start()
    for f in range(3):
        received[f][0] = sent[f][0]

    for group in range(2):
        first = 1 - group
        for f in range(3):
            width, start = WIDTHS[f] // 2, STARTS[f]
            landed = received[f].at[pl.ds(group * 16 + first, 16 - first)]
            pltpu.make_async_copy(landed, landed, recv_sem.at[f, group]).wait()
            block = received[f][group * 16 : (group + 1) * 16].reshape(256, width)
            block = jnp.dot(spread[f], block, preferred_element_type=f32).astype(bf16)
            for h in range(2):
                rows[:, start + h * width : start + (h + 1) * width] = block[h * 128 : (h + 1) * 128]
        if group == 0:
            loads[0].wait()
        for n in range(3):
            gate = jnp.dot(rows[...], gate_up[:, n * 256 : (n + 1) * 256], preferred_element_type=f32)
            up = jnp.dot(rows[...], gate_up[:, 768 + n * 256 : 768 + (n + 1) * 256], preferred_element_type=f32)
            active[:, n * 256 : (n + 1) * 256] = (gate / (1.0 + jnp.exp(-gate)) * up).astype(bf16)
        if group == 0:
            loads[1].wait()
        for f in range(3):
            width, start = WIDTHS[f] // 2, STARTS[f]
            served = jnp.dot(active[...], down[:, start : start + 2 * width], preferred_element_type=f32).astype(bf16)
            served = jnp.concatenate([served[:, :width], served[:, width:]], axis=0)
            block = jnp.dot(gather[f], served, preferred_element_type=f32).astype(bf16)
            results[f][group * 16 : (group + 1) * 16] = block.reshape(16, 16, width)

            for j in range(group * 16 + first, group * 16 + 16):
                pltpu.make_async_remote_copy(
                    src_ref=results[f].at[j], dst_ref=returned[f].at[j], send_sem=back_sem.at[f],
                    recv_sem=return_sem.at[f], device_id=across(f, j, -1), device_id_type=MESH,
                ).start()
            if group == 0:
                returned[f][0] = results[f][0]

    for f in range(3):
        width, start = WIDTHS[f] // 2, STARTS[f]
        landed = returned[f].at[pl.ds(1, 31)]
        pltpu.make_async_copy(landed, landed, return_sem.at[f]).wait()
        for h in range(2):
            columns = slice(start + h * width, start + (h + 1) * width)
            both = jnp.dot(mix[f, h], returned[f][...].reshape(512, width), preferred_element_type=f32)
            both = both[:64] + both[64:]
            state[:12, columns] = state[:12, columns] + both[:12]
            for d in range(1, 4):
                shared[f][d - 1, :, h * width : (h + 1) * width] = both[d * 16 : (d + 1) * 16].astype(bf16)
        for d in (2, 1, 3):
            pltpu.make_async_remote_copy(
                src_ref=shared[f].at[d - 1], dst_ref=arrived[f].at[d - 1], send_sem=share_send_sem.at[f],
                recv_sem=share_recv_sem.at[f], device_id=place(*ahead(f, 4 - d)), device_id_type=MESH,
            ).start()
    for f in range(3):
        columns = slice(STARTS[f], STARTS[f] + WIDTHS[f])
        pltpu.make_async_copy(arrived[f], arrived[f], share_recv_sem.at[f]).wait()
        total = state[:12, columns]
        for d in range(3):
            total = total + arrived[f][d, :12, :].astype(f32)
        out_ref[:, columns] = total.astype(bf16)

    for n in range(6):
        pltpu.make_async_copy(
            o_proj_hbm.at[pl.ds(0, 1024)], projection.at[pl.ds(0, 1024), pl.ds(128, 128)], o_send_sem.at[n]
        ).wait()
    gone = gathered.at[pl.ds(1, 7)]
    pltpu.make_async_copy(gone, gone, a_send_sem).wait()
    gone = collected.at[pl.ds(1, 31)]
    pltpu.make_async_copy(gone, gone, p_send_sem).wait()
    gone = tiles.at[pl.ds(0, 9)]
    pltpu.make_async_copy(gone, gone, tile_send_sem).wait()
    for f in range(3):
        gone = line[f].at[pl.ds(1, 3)]
        pltpu.make_async_copy(gone, gone, line_send_sem.at[f]).wait()
        gone = sent[f].at[pl.ds(1, 31)]
        pltpu.make_async_copy(gone, gone, send_sem.at[f]).wait()
        gone = results[f].at[pl.ds(1, 31)]
        pltpu.make_async_copy(gone, gone, back_sem.at[f]).wait()
        pltpu.make_async_copy(shared[f], shared[f], share_send_sem.at[f]).wait()


def body(
    queries, keys, values, lengths, o_proj, residual, norm_gain, gate_up, down, routes, route_weights,
):
    bf16, f32 = jnp.bfloat16, jnp.float32
    vmem = pl.BlockSpec(memory_space=pltpu.VMEM)
    smem = pl.BlockSpec(memory_space=pltpu.SMEM)
    hbm = pl.BlockSpec(memory_space=pl.ANY)
    each = lambda shape: tuple(shape(w) for w in WIDTHS)
    dma, plain = pltpu.SemaphoreType.DMA, pltpu.SemaphoreType.REGULAR
    return pl.pallas_call(
        kernel,
        out_shape=jax.ShapeDtypeStruct((12, 4096), bf16),
        in_specs=[vmem, hbm, hbm, smem, hbm, vmem, vmem, smem, smem, hbm, hbm],
        out_specs=vmem,
        scratch_shapes=[
            pltpu.VMEM((48, 192, 128), bf16),
            pltpu.VMEM((48, 192, 128), bf16),
            pltpu.VMEM((48, 16, 128), f32),
            pltpu.VMEM((48, 16, 128), f32),
            pltpu.VMEM((8, 48, 2048), bf16),
            pltpu.VMEM((2048, 512), bf16),
            pltpu.VMEM((384, 512), f32),
            pltpu.VMEM((32, 48, 128), f32),
            pltpu.VMEM((32, 48, 128), bf16),
            pltpu.VMEM((32, 48, 128), bf16),
            pltpu.VMEM((8, 48, 128), f32),
            pltpu.VMEM((16, 4096), f32),
            pltpu.VMEM((4096, 1536), bf16),
            pltpu.VMEM((768, 4096), bf16),
            pltpu.VMEM((10, 16, 128), f32),
            each(lambda w: pltpu.VMEM((4, 16, w), bf16)),
            each(lambda w: pltpu.VMEM((32, 16, w // 2), bf16)),
            each(lambda w: pltpu.VMEM((32, 16, w // 2), bf16)),
            pltpu.VMEM((128, 4096), bf16),
            pltpu.VMEM((128, 768), bf16),
            each(lambda w: pltpu.VMEM((32, 16, w // 2), bf16)),
            each(lambda w: pltpu.VMEM((32, 16, w // 2), bf16)),
            each(lambda w: pltpu.VMEM((3, 16, w), bf16)),
            each(lambda w: pltpu.VMEM((3, 16, w), bf16)),
            pltpu.VMEM((3, 256, 64), bf16),
            pltpu.VMEM((3, 2, 128, 512), bf16),
            pltpu.VMEM((3, 256, 256), bf16),
            pltpu.VMEM((3, 256, 256), bf16),
            dma((2, 3)), dma((2,)), dma, dma((6,)), dma((6,)), dma, dma((3, 8)), dma, dma,
            dma, dma, dma((3,)), dma((3,)), dma((3,)), dma((3, 2)), dma((3,)), dma((3,)),
            dma((3,)), dma((3,)), plain, plain,
        ],
        compiler_params=pltpu.CompilerParams(
            collective_id=1, has_side_effects=True, vmem_limit_bytes=60 * 2**20
        ),
        cost_estimate=pl.CostEstimate(flops=6 * 10**9, bytes_accessed=3 * 10**7, transcendentals=10**6),
        name="layer",
    )(
        queries, keys[:, 0], values[:, 0], lengths, o_proj, residual, norm_gain[None, :], routes.T,
        route_weights.T, gate_up[0], down[0],
    )


def solution(mesh):
    in_specs = (
        P("req", "kvh"),
        P("req", "kvh", None, None),
        P("req", "kvh", None, None),
        P("req"),
        P("kvh", "req"),
        P(("req", "kvh"), None),
        P(),
        P(("req", "kvh"), None, None),
        P(("req", "kvh"), None, None),
        P(("req", "kvh"), None),
        P(("req", "kvh"), None),
    )
    out_specs = P(("req", "kvh"), None)
    return jax.shard_map(body, mesh=mesh, in_specs=in_specs, out_specs=out_specs, check_vma=False)
```

```python
import math

import jax
import jax.numpy as jnp
from jax import lax
from jax.experimental import pallas as pl
from jax.experimental.pallas import tpu as pltpu
from jax.sharding import PartitionSpec as P


MESH = pl.DeviceIdType.MESH


def coords():
    r = lax.axis_index("req")
    k = lax.axis_index("kvh")
    return lax.rem(r, 2) * 2 + k // 2, r // 8, lax.rem(r // 2, 4), lax.rem(k, 2)


def place(x, y, z, c):
    x, y, z, c = lax.rem(x, 4), lax.rem(y, 4), lax.rem(z, 4), lax.rem(c, 2)
    return ((y * 4 + z) * 2 + x // 2, lax.rem(x, 2) * 2 + c)


def iota(shape, dim):
    return lax.broadcasted_iota(jnp.int32, shape, dim)


WIDTHS = (1024, 1024, 1024)
STARTS = (0, 1024, 2048)
REST = 3072


def ahead(axis, d):
    x, y, z, c = coords()
    return ((x, y, z + d, c), (x, y + d, z, c), (x + d, y, z, c))[axis]


def kernel(
    queries_hbm, keys_hbm, values_hbm, lengths_smem, o_proj_hbm, residual_hbm, gain_hbm, routes_smem, weights_smem,
    gate_up_hbm, down_hbm,
    out_ref,
    queries, residual, gain, keys, values, heads, attended, gathered, projection, partial, staged, pieces, collected, summed, state, gate_up,
    down, tiles, line, sent, received, rows, active, results, returned, shared, arrived, table, mix, spread, gather, blend,
    straight, straight_table, straight_mix, swap, out_straight, in_straight, back_straight, home_straight,
    row_sem, cache_sem, weight_sem, o_own_sem, o_send_sem, o_recv_sem, a_send_sem, a_recv_sem, p_send_sem, p_recv_sem,
    tile_send_sem, tile_recv_sem, line_send_sem, line_recv_sem, send_sem, recv_sem, back_sem, return_sem,
    share_send_sem, share_recv_sem, straight_send_sem, straight_recv_sem, straight_back_sem, straight_home_sem,
    along_y, along_z,
):
    r, kv = lax.axis_index("req"), lax.axis_index("kvh")
    x, y, z, c = coords()
    half = lax.rem(r, 2)
    bf16, f32 = jnp.bfloat16, jnp.float32

    xs, ys, zs = ([lax.rem(at + d, 4) for d in range(4)] for at in (x, y, z))
    high_x, low_x, cores = [at // 2 for at in xs], [lax.rem(at, 2) * 2 for at in xs], [c, 1 - c]

    def away(dx, dy, dz, dc):
        return ((ys[dy % 4] * 4 + zs[dz % 4]) * 2 + high_x[dx % 4], low_x[dx % 4] + cores[dc])

    barrier = pltpu.get_barrier_semaphore()
    for dx in range(4):
        for dc in range(2):
            if dx or dc:
                pl.semaphore_signal(barrier, inc=1, device_id=place(x + dx, y, z, c + dc), device_id_type=MESH)
    for d in range(1, 4):
        pl.semaphore_signal(barrier, inc=1, device_id=place(x, y + d, z, c), device_id_type=MESH)
        pl.semaphore_signal(barrier, inc=1, device_id=place(x, y, z + d, c), device_id_type=MESH)

    def cache_load(m, which):
        source, target = ((keys_hbm, keys), (values_hbm, values))[which]
        part = pl.ds(m * 16, 16)
        return pltpu.make_async_copy(source.at[part], target.at[part], cache_sem.at[which, m])

    small = [
        pltpu.make_async_copy(source, target, row_sem.at[n])
        for n, (source, target) in enumerate(((queries_hbm, queries), (residual_hbm, residual), (gain_hbm, gain)))
    ]
    small[0].start()
    cache_load(0, 0).start()
    cache_load(0, 1).start()
    o_own = pltpu.make_async_copy(o_proj_hbm, projection.at[:, pl.ds(0, 128)], o_own_sem)
    loads = [
        pltpu.make_async_copy(gate_up_hbm, gate_up, weight_sem.at[0]),
        pltpu.make_async_copy(down_hbm, down, weight_sem.at[1]),
    ]

    def o_copy(source, slot, part, n, dy, rows):
        return pltpu.make_async_remote_copy(
            src_ref=source, dst_ref=projection.at[pl.ds(part * 1024, rows), pl.ds(slot * 128, 128)],
            send_sem=o_send_sem.at[n], recv_sem=o_recv_sem.at[n], device_id=place(x, y + dy, z, c),
            device_id_type=MESH,
        )

    def o_first(n):
        slot, part, dy = ((1, 0, 1), (3, 1, 3), (1, 1, 1), (3, 0, 3))[n]
        return o_copy(o_proj_hbm.at[pl.ds(part * 1024, 1024)], slot, part, n, dy, 1024)

    def o_pass(n):
        slot, part, dy = ((1, 0, 1), (3, 1, 3))[n]
        held = projection.at[pl.ds(part * 1024, 1024), pl.ds(slot * 128, 128)]
        return o_copy(held, 2, part, 4 + n, dy, 1024)

    pl.semaphore_wait(barrier, 13)
    for n in range(4):
        o_first(n).start()
    for d in range(1, 4):
        pl.semaphore_signal(along_y, inc=1, device_id=place(x, y + d, z, c), device_id_type=MESH)

    for m in range(1, 3):
        cache_load(m, 0).start()
        cache_load(m, 1).start()
    small[0].wait()
    for h in range(16):
        heads[:, h, :] = queries[:, h * 128 : (h + 1) * 128].astype(f32)

    position = iota((192, 128), 0)
    request = iota((128, 128), 1) // 16

    def attend(g):
        first = g * 8
        turned = jnp.transpose(heads[first : first + 8].reshape(128, 128))
        scores = jnp.zeros((192, 128), f32)
        for b in range(0, 8, 2):
            two = jnp.concatenate([keys[first + b], keys[first + b + 1]], axis=1)
            asked = jnp.concatenate(
                [jnp.where(request == b, turned, 0.0), jnp.where(request == b + 1, turned, 0.0)], axis=0
            ).astype(bf16)
            scores = scores + jnp.dot(two, asked, preferred_element_type=f32)
        scores = scores * (1.0 / math.sqrt(128.0))
        limit = jnp.zeros((1, 128), jnp.int32)
        for b in range(8):
            limit = jnp.where(request[:1] == b, lengths_smem[first + b], limit)
        scores = jnp.where(position < limit, scores, -1e30)
        shifted = jnp.exp(scores - jnp.max(scores, axis=0, keepdims=True))
        shares = shifted / jnp.sum(shifted, axis=0, keepdims=True)
        shares = jnp.transpose(shares).astype(bf16)
        for b in range(8):
            attended[first + b] = jnp.dot(
                shares[b * 16 : (b + 1) * 16], values[first + b], preferred_element_type=f32
            )

    def a_copy(slot, m, dz, dh):
        part = pl.ds(m * 16, 16)
        to = ((y * 4 + lax.rem(z + dz, 4)) * 2 + lax.rem(half + dh, 2), kv)
        return pltpu.make_async_remote_copy(
            src_ref=gathered.at[slot, part], dst_ref=gathered.at[slot + dz * 2 + dh, part], send_sem=a_send_sem,
            recv_sem=a_recv_sem.at[m, slot + dz * 2 + dh], device_id=to, device_id_type=MESH,
        )

    def a_wait(m, slot):
        landed = gathered.at[slot, pl.ds(m * 16, 16)]
        pltpu.make_async_copy(landed, landed, a_recv_sem.at[m, slot]).wait()

    def a_start(m):
        rows_here = slice(m * 16, (m + 1) * 16)
        for h in range(16):
            gathered[0, rows_here, h * 128 : (h + 1) * 128] = attended[rows_here, h, :].astype(bf16)

    def a_send(m):
        a_copy(0, m, 0, 1).start()
        for dz in (1, 3, 2):
            a_copy(0, m, dz, 0).start()

    for m in range(3):
        cache_load(m, 0).wait()
        cache_load(m, 1).wait()
        attend(2 * m)
        attend(2 * m + 1)
        a_start(m)
        if m == 0:
            pl.semaphore_wait(along_y, 3)
            for d in range(1, 4):
                pl.semaphore_signal(along_z, inc=1, device_id=place(x, y, z + d, c), device_id_type=MESH)
            pl.semaphore_wait(along_z, 3)
        a_send(m)
        if m == 0:
            o_own.start()
            small[1].start()
            small[2].start()
            for load in loads:
                load.start()
    for n in range(2):
        pltpu.make_async_copy(o_proj_hbm.at[pl.ds(0, 1024)], projection.at[pl.ds(0, 1024), pl.ds(128, 128)], o_recv_sem.at[n]).wait()
        o_pass(n).start()
    a_wait(0, 1)
    for dz in (1, 3, 2):
        a_copy(1, 0, dz, 0).start()
    for m in (1, 2):
        for dz in (1, 3, 2):
            a_wait(m, dz * 2)
            a_copy(dz * 2, m, 0, 1).start()

    state[...] = jnp.zeros((16, 4096), f32)
    small[1].wait()
    small[2].wait()
    state[:12, :] = residual[...].astype(f32)

    lane = iota((8, 128), 1)
    sub = iota((8, 128), 0)
    token = lane & 15
    expert = jnp.full((8, 128), -1, jnp.int32)
    gates = jnp.zeros((8, 128), f32)
    for t in range(12):
        for k in range(8):
            here = (sub == k) & (token == t)
            expert = jnp.where(here, routes_smem[k, t], expert)
            gates = jnp.where(here, weights_smem[k, t], gates)
    place_of = jnp.zeros((8, 128), jnp.int32)
    for t in range(12):
        for k in range(8):
            place_of = place_of + jnp.where((expert == routes_smem[k, t]) & (token > t), 1, 0)
    tiles[9, :8, :] = jnp.where(token < 12, expert * 2 + place_of, -1).astype(f32)
    tiles[9, 8:, :] = gates

    for f in range(3):
        for d in range(1, 4):
            pltpu.make_async_remote_copy(
                src_ref=tiles.at[9], dst_ref=tiles.at[f * 3 + d - 1], send_sem=tile_send_sem, recv_sem=tile_recv_sem,
                device_id=place(*ahead(f, d)), device_id_type=MESH,
            ).start()
        line[f][0] = jnp.zeros((16, WIDTHS[f]), bf16)

    for f in range(3):
        def column(i):
            half_of, n = i // 128, i & 127
            dx, dy, dz, row = n // 32, (n // 8) & 3, (n // 2) & 3, n & 1
            p, q, g = ((dx, dy, dz), (dx, dz, dy), (dy, dz, dx))[f]
            return (p * 4 + q) * 16 + half_of * 8 + g * 2 + row

        i, j = iota((256, 256), 0), iota((256, 256), 1)
        spread[f] = jnp.where(j == column(i), 1.0, 0.0).astype(bf16)
        gather[f] = jnp.where(i == column(j), 1.0, 0.0).astype(bf16)

    number = expert
    ring, group = number // 4, number & 3
    dx = ((ring & 1) * 2 + group // 2 + 4 - x) & 3
    dy = (ring // 8 + 4 - y) & 3
    dz = (((ring // 2) & 3) + 4 - z) & 3
    dc = ((group & 1) + 2 - c) & 1
    key = (dc * 64 + dx * 16 + dy * 4 + dz) * 2 + place_of
    key = jnp.where(token < 12, key, -1)
    for part in range(8):
        row = iota((256, 128), 0) + part * 256
        hit = jnp.zeros((256, 128), f32)
        for k in range(8):
            hit = jnp.where(row // 8 == key[k : k + 1, :], 1.0, hit)
        hit = jnp.where((row & 7) == iota((256, 128), 1) // 16, hit, 0.0)
        straight_table[part * 256 : (part + 1) * 256, :] = hit.astype(bf16)
    key_column = jnp.transpose(key.astype(f32)).astype(jnp.int32)
    gate_column = jnp.transpose(gates)
    for part in range(8):
        spot = iota((128, 256), 1) + part * 256
        share = jnp.zeros((128, 256), f32)
        for k in range(8):
            share = jnp.where(spot // 8 == key_column[:, k : k + 1], gate_column[:, k : k + 1], share)
        share = jnp.where((spot & 7) == iota((128, 256), 0) // 16, share, 0.0)
        high = share.astype(bf16)
        straight_mix[:128, part * 256 : (part + 1) * 256] = high
        straight_mix[128:, part * 256 : (part + 1) * 256] = (share - high.astype(f32)).astype(bf16)
    i, j = iota((256, 256), 0), iota((256, 256), 1)
    swap[0] = jnp.where(j == (i & 31) * 8 + i // 32, 1.0, 0.0).astype(bf16)
    swap[1] = jnp.where(i == (j & 31) * 8 + j // 32, 1.0, 0.0).astype(bf16)
    straight[...] = jnp.zeros((128, 128), bf16)

    landed = tiles.at[pl.ds(0, 9)]
    pltpu.make_async_copy(landed, landed, tile_recv_sem).wait()
    for f in range(3):
        marks = jnp.full((8, 128), -1, jnp.int32)
        gates = jnp.zeros((8, 128), f32)
        for d in range(4):
            tile = tiles[9] if d == 0 else tiles[f * 3 + d - 1]
            marks = jnp.where(lane // 16 == d, tile[:8].astype(jnp.int32), marks)
            gates = jnp.where(lane // 16 == d, tile[8:], gates)
        number = marks // 2
        ring, group = number // 4, number & 3
        dx = ((ring & 1) * 2 + group // 2 + 4 - x) & 3
        dy = (ring // 8 + 4 - y) & 3
        dz = ((ring // 2) & 3) + 4 - z & 3
        dc = ((group & 1) + 2 - c) & 1
        p, q, g = ((dx, dy, dz), (dx, dz, dy), (dy, dz, dx))[f]
        key = ((dc * 16 + p * 4 + q) * 4 + lane // 16) * 2 + (marks & 1)
        key = jnp.where((marks >= 0) & (g == 0), key, -1)
        row = iota((256, 64), 0)
        hit = jnp.zeros((256, 64), f32)
        for k in range(8):
            hit = jnp.where(row == key[k : k + 1, :64], 1.0, hit)
        table[f] = hit.astype(bf16)
        key_column = jnp.transpose(key.astype(f32))[:64].astype(jnp.int32)
        gate_column = jnp.transpose(gates)[:64]
        spot = iota((64, 512), 1)
        share = jnp.zeros((64, 512), f32)
        for k in range(8):
            share = jnp.where(
                (spot // 16) * 8 + (spot & 7) == key_column[:, k : k + 1], gate_column[:, k : k + 1], share
            )
        for h in range(2):
            part = jnp.where((spot // 8) & 1 == h, share, 0.0)
            high = part.astype(bf16)
            mix[f, h, :64, :] = high
            mix[f, h, 64:, :] = (part - high.astype(f32)).astype(bf16)

    o_own.wait()
    for n in range(2, 6):
        pltpu.make_async_copy(o_proj_hbm.at[pl.ds(0, 1024)], projection.at[pl.ds(0, 1024), pl.ds(128, 128)], o_recv_sem.at[n]).wait()
    for m in range(3):
        for slot in range(1, 8):
            if not (slot == 1 and m == 0 or slot in (2, 4, 6) and m > 0):
                a_wait(m, slot)
    halves, lows = [half, 1 - half], [kv // 2, 1 - kv // 2]

    def hand_out(d, e):
        to = lows[e // 2] * 2 + cores[e % 2]
        pltpu.make_async_remote_copy(
            src_ref=pieces.at[d * 4 + to], dst_ref=collected.at[d * 4 + e], send_sem=p_send_sem, recv_sem=p_recv_sem,
            device_id=((y * 4 + zs[d // 2]) * 2 + halves[d % 2], to), device_id_type=MESH,
        ).start()

    for turn in range(2):
        slots = slice(turn * 4, turn * 4 + 4)
        partial[turn * 192 : (turn + 1) * 192, :] = jnp.dot(
            gathered[slots].reshape(192, 2048), projection[...], preferred_element_type=f32
        )
        for slot in range(turn * 4, turn * 4 + 4):
            d = ((4 - slot // 2) % 4) * 2 + slot % 2
            for k in range(4):
                for w in range(4):
                    staged[d * 4 + k, w * 12 : (w + 1) * 12, :] = partial[
                        slot * 48 + k * 12 : slot * 48 + (k + 1) * 12, w * 128 : (w + 1) * 128
                    ]
            pieces[d * 4 : d * 4 + 4] = staged[d * 4 : d * 4 + 4].astype(bf16)
            for e in range(4):
                if d or e:
                    hand_out(d, e)
    collected[0] = pieces[kv]
    landed = collected.at[pl.ds(1, 31)]
    pltpu.make_async_copy(landed, landed, p_recv_sem).wait()
    square = jnp.zeros((12, 128), f32)
    for p in range(8):
        slot = (lax.rem(z + 4 - p // 2, 4) * 2 + lax.rem(half + p % 2, 2)) * 4
        total = collected[slot].astype(f32)
        for e in range(1, 4):
            total = total + collected[slot + e].astype(f32)
        summed[p] = total
        for w in range(4):
            columns = pl.ds(pl.multiple_of((lax.rem(y + 4 - w, 4) * 8 + p) * 128, 128), 128)
            total = state[:12, columns] + summed[p, w * 12 : (w + 1) * 12, :]
            state[:12, columns] = total
            square = square + total * total
    factor = lax.rsqrt(jnp.sum(square, axis=1, keepdims=True) * (1.0 / 4096.0) + 1e-06)
    for f in range(3):
        columns = slice(STARTS[f], STARTS[f] + WIDTHS[f])
        line[f][0, :12, :] = (state[:12, columns] * factor * gain[:, columns]).astype(bf16)
        for d in (2, 1, 3):
            pltpu.make_async_remote_copy(
                src_ref=line[f].at[0], dst_ref=line[f].at[d], send_sem=line_send_sem.at[f],
                recv_sem=line_recv_sem.at[f], device_id=place(*ahead(f, d)), device_id_type=MESH,
            ).start()

    for s in range(8):
        columns = slice(REST + s * 128, REST + (s + 1) * 128)
        straight[s * 16 : s * 16 + 12, :] = (state[:12, columns] * factor * gain[:, columns]).astype(bf16)

    def straight_sends(source, target, send_sems, recv_sems, group, sign):
        def start(dx, dy, i, dz):
            there = (lax.rem(y + dy, 4) * 4 + zs[sign * dz % 4]) * 2 + lax.rem(x + dx, 4) // 2
            j = group * 64 + i * 4 + dz
            pltpu.make_async_remote_copy(
                src_ref=source.at[j], dst_ref=target.at[j], send_sem=send_sems.at[group], recv_sem=recv_sems.at[group],
                device_id=(there, lax.rem(x + dx, 2) * 2 + cores[group]), device_id_type=MESH,
            ).start()

        def four(i, carry):
            for dz in range(4):
                start(sign * (i // 4) + 4, sign * lax.rem(i, 4) + 4, i, dz)
            return carry

        for dz in range(1 - group, 4):
            start(0, 0, 0, dz)
        lax.fori_loop(1, 16, four, 0)

    def straight_out(group):
        for part in range(group * 4, group * 4 + 4):
            block = jnp.dot(
                straight_table[part * 256 : (part + 1) * 256, :], straight[...], preferred_element_type=f32
            ).astype(bf16)
            out_straight[part * 16 : (part + 1) * 16] = block.reshape(16, 16, 128)
        straight_sends(out_straight, in_straight, straight_send_sem, straight_recv_sem, group, 1)

    straight_out(0)
    in_straight[0] = out_straight[0]

    def across(f, j, sign):
        p, q, dc = sign * (j // 4 % 4), sign * (j % 4), j // 16
        return away(*((p, q, 0, dc), (p, 0, q, dc), (0, p, q, dc))[f])

    for group in range(2):
        blocks = range(group * 16, group * 16 + 16)
        for f in range(3):
            width = WIDTHS[f] // 2
            if group == 0:
                landed = line[f].at[pl.ds(1, 3)]
                pltpu.make_async_copy(landed, landed, line_recv_sem.at[f]).wait()
            block = jnp.dot(
                table[f, group * 128 : (group + 1) * 128], line[f][...].reshape(64, WIDTHS[f]),
                preferred_element_type=f32,
            ).reshape(16, 8, WIDTHS[f])
            sent[f][group * 16 : (group + 1) * 16] = jnp.concatenate(
                [block[:, :, :width], block[:, :, width:]], axis=1
            ).astype(bf16)
            for j in blocks:
                if j:
                    pltpu.make_async_remote_copy(
                        src_ref=sent[f].at[j], dst_ref=received[f].at[j], send_sem=send_sem.at[f],
                        recv_sem=recv_sem.at[f, group], device_id=across(f, j, 1), device_id_type=MESH,
                    ).start()
    straight_out(1)
    for f in range(3):
        received[f][0] = sent[f][0]

    for group in range(2):
        first = 1 - group
        for f in range(3):
            width, start = WIDTHS[f] // 2, STARTS[f]
            landed = received[f].at[pl.ds(group * 16 + first, 16 - first)]
            pltpu.make_async_copy(landed, landed, recv_sem.at[f, group]).wait()
            block = received[f][group * 16 : (group + 1) * 16].reshape(256, width)
            block = jnp.dot(spread[f], block, preferred_element_type=f32).astype(bf16)
            for h in range(2):
                rows[:, start + h * width : start + (h + 1) * width] = block[h * 128 : (h + 1) * 128]
        landed = in_straight.at[pl.ds(group * 64 + first, 64 - first)]
        pltpu.make_async_copy(landed, landed, straight_recv_sem.at[group]).wait()
        for chunk in range(4):
            block = in_straight[group * 64 + chunk * 16 : group * 64 + (chunk + 1) * 16].reshape(256, 128)
            block = jnp.dot(swap[0], block, preferred_element_type=f32).astype(bf16)
            for s in range(8):
                rows[chunk * 32 : (chunk + 1) * 32, REST + s * 128 : REST + (s + 1) * 128] = block[s * 32 : (s + 1) * 32]
        if group == 0:
            loads[0].wait()
        for n in range(3):
            gate = jnp.dot(rows[...], gate_up[:, n * 256 : (n + 1) * 256], preferred_element_type=f32)
            up = jnp.dot(rows[...], gate_up[:, 768 + n * 256 : 768 + (n + 1) * 256], preferred_element_type=f32)
            active[:, n * 256 : (n + 1) * 256] = (gate / (1.0 + jnp.exp(-gate)) * up).astype(bf16)
        if group == 0:
            loads[1].wait()
        for f in range(3):
            width, start = WIDTHS[f] // 2, STARTS[f]
            served = jnp.dot(active[...], down[:, start : start + 2 * width], preferred_element_type=f32).astype(bf16)
            served = jnp.concatenate([served[:, :width], served[:, width:]], axis=0)
            block = jnp.dot(gather[f], served, preferred_element_type=f32).astype(bf16)
            results[f][group * 16 : (group + 1) * 16] = block.reshape(16, 16, width)

            for j in range(group * 16 + first, group * 16 + 16):
                pltpu.make_async_remote_copy(
                    src_ref=results[f].at[j], dst_ref=returned[f].at[j], send_sem=back_sem.at[f],
                    recv_sem=return_sem.at[f, group], device_id=across(f, j, -1), device_id_type=MESH,
                ).start()
            if group == 0:
                returned[f][0] = results[f][0]

        served = jnp.dot(active[...], down[:, REST : REST + 1024], preferred_element_type=f32).astype(bf16)
        for chunk in range(4):
            block = jnp.concatenate(
                [served[chunk * 32 : (chunk + 1) * 32, s * 128 : (s + 1) * 128] for s in range(8)], axis=0
            )
            block = jnp.dot(swap[1], block, preferred_element_type=f32).astype(bf16)
            back_straight[group * 64 + chunk * 16 : group * 64 + (chunk + 1) * 16] = block.reshape(16, 16, 128)
        straight_sends(back_straight, home_straight, straight_back_sem, straight_home_sem, group, -1)
        if group == 0:
            home_straight[0] = back_straight[0]

    def mixed(f, group, h):
        block = returned[f][group * 16 : (group + 1) * 16].reshape(256, WIDTHS[f] // 2)
        both = jnp.dot(mix[f, h, :, group * 256 : (group + 1) * 256], block, preferred_element_type=f32)
        return both[:64] + both[64:]

    for f in range(3):
        width, start = WIDTHS[f] // 2, STARTS[f]
        landed = returned[f].at[pl.ds(1, 15)]
        pltpu.make_async_copy(landed, landed, return_sem.at[f, 0]).wait()
        for h in range(2):
            blend[:, start + h * width : start + (h + 1) * width] = mixed(f, 0, h)
    for f in range(3):
        width, start = WIDTHS[f] // 2, STARTS[f]
        landed = returned[f].at[pl.ds(16, 16)]
        pltpu.make_async_copy(landed, landed, return_sem.at[f, 1]).wait()
        for h in range(2):
            columns = slice(start + h * width, start + (h + 1) * width)
            both = blend[:, columns] + mixed(f, 1, h)
            state[:12, columns] = state[:12, columns] + both[:12]
            for d in range(1, 4):
                shared[f][d - 1, :, h * width : (h + 1) * width] = both[d * 16 : (d + 1) * 16].astype(bf16)
        for d in (2, 1, 3):
            pltpu.make_async_remote_copy(
                src_ref=shared[f].at[d - 1], dst_ref=arrived[f].at[d - 1], send_sem=share_send_sem.at[f],
                recv_sem=share_recv_sem.at[f], device_id=place(*ahead(f, 4 - d)), device_id_type=MESH,
            ).start()
    for group in range(2):
        landed = home_straight.at[pl.ds(group * 64 + 1 - group, 63 + group)]
        pltpu.make_async_copy(landed, landed, straight_home_sem.at[group]).wait()
    both = jnp.dot(straight_mix[...], home_straight[...].reshape(2048, 128), preferred_element_type=f32)
    both = both[:128] + both[128:]
    for s in range(8):
        columns = slice(REST + s * 128, REST + (s + 1) * 128)
        out_ref[:, columns] = (state[:12, columns] + both[s * 16 : s * 16 + 12]).astype(bf16)
    for f in range(3):
        columns = slice(STARTS[f], STARTS[f] + WIDTHS[f])
        pltpu.make_async_copy(arrived[f], arrived[f], share_recv_sem.at[f]).wait()
        total = state[:12, columns]
        for d in range(3):
            total = total + arrived[f][d, :12, :].astype(f32)
        out_ref[:, columns] = total.astype(bf16)

    for n in range(6):
        pltpu.make_async_copy(
            o_proj_hbm.at[pl.ds(0, 1024)], projection.at[pl.ds(0, 1024), pl.ds(128, 128)], o_send_sem.at[n]
        ).wait()
    gone = gathered.at[pl.ds(1, 7)]
    pltpu.make_async_copy(gone, gone, a_send_sem).wait()
    gone = collected.at[pl.ds(1, 31)]
    pltpu.make_async_copy(gone, gone, p_send_sem).wait()
    gone = tiles.at[pl.ds(0, 9)]
    pltpu.make_async_copy(gone, gone, tile_send_sem).wait()
    for f in range(3):
        gone = line[f].at[pl.ds(1, 3)]
        pltpu.make_async_copy(gone, gone, line_send_sem.at[f]).wait()
        gone = sent[f].at[pl.ds(1, 31)]
        pltpu.make_async_copy(gone, gone, send_sem.at[f]).wait()
        gone = results[f].at[pl.ds(1, 31)]
        pltpu.make_async_copy(gone, gone, back_sem.at[f]).wait()
        pltpu.make_async_copy(shared[f], shared[f], share_send_sem.at[f]).wait()
    for group in range(2):
        gone = out_straight.at[pl.ds(group * 64 + 1 - group, 63 + group)]
        pltpu.make_async_copy(gone, gone, straight_send_sem.at[group]).wait()
        gone = back_straight.at[pl.ds(group * 64 + 1 - group, 63 + group)]
        pltpu.make_async_copy(gone, gone, straight_back_sem.at[group]).wait()


def body(
    queries, keys, values, lengths, o_proj, residual, norm_gain, gate_up, down, routes, route_weights,
):
    bf16, f32 = jnp.bfloat16, jnp.float32
    vmem = pl.BlockSpec(memory_space=pltpu.VMEM)
    smem = pl.BlockSpec(memory_space=pltpu.SMEM)
    hbm = pl.BlockSpec(memory_space=pl.ANY)
    each = lambda shape: tuple(shape(w) for w in WIDTHS)
    dma, plain = pltpu.SemaphoreType.DMA, pltpu.SemaphoreType.REGULAR
    return pl.pallas_call(
        kernel,
        out_shape=jax.ShapeDtypeStruct((12, 4096), bf16),
        in_specs=[hbm, hbm, hbm, smem, hbm, hbm, hbm, smem, smem, hbm, hbm],
        out_specs=vmem,
        scratch_shapes=[
            pltpu.VMEM((48, 2048), bf16),
            pltpu.VMEM((12, 4096), bf16),
            pltpu.VMEM((1, 4096), f32),
            pltpu.VMEM((48, 192, 128), bf16),
            pltpu.VMEM((48, 192, 128), bf16),
            pltpu.VMEM((48, 16, 128), f32),
            pltpu.VMEM((48, 16, 128), f32),
            pltpu.VMEM((8, 48, 2048), bf16),
            pltpu.VMEM((2048, 512), bf16),
            pltpu.VMEM((384, 512), f32),
            pltpu.VMEM((32, 48, 128), f32),
            pltpu.VMEM((32, 48, 128), bf16),
            pltpu.VMEM((32, 48, 128), bf16),
            pltpu.VMEM((8, 48, 128), f32),
            pltpu.VMEM((16, 4096), f32),
            pltpu.VMEM((4096, 1536), bf16),
            pltpu.VMEM((768, 4096), bf16),
            pltpu.VMEM((10, 16, 128), f32),
            each(lambda w: pltpu.VMEM((4, 16, w), bf16)),
            each(lambda w: pltpu.VMEM((32, 16, w // 2), bf16)),
            each(lambda w: pltpu.VMEM((32, 16, w // 2), bf16)),
            pltpu.VMEM((128, 4096), bf16),
            pltpu.VMEM((128, 768), bf16),
            each(lambda w: pltpu.VMEM((32, 16, w // 2), bf16)),
            each(lambda w: pltpu.VMEM((32, 16, w // 2), bf16)),
            each(lambda w: pltpu.VMEM((3, 16, w), bf16)),
            each(lambda w: pltpu.VMEM((3, 16, w), bf16)),
            pltpu.VMEM((3, 256, 64), bf16),
            pltpu.VMEM((3, 2, 128, 512), bf16),
            pltpu.VMEM((3, 256, 256), bf16),
            pltpu.VMEM((3, 256, 256), bf16),
            pltpu.VMEM((64, 3072), f32),
            pltpu.VMEM((128, 128), bf16),
            pltpu.VMEM((2048, 128), bf16),
            pltpu.VMEM((256, 2048), bf16),
            pltpu.VMEM((2, 256, 256), bf16),
            pltpu.VMEM((128, 16, 128), bf16),
            pltpu.VMEM((128, 16, 128), bf16),
            pltpu.VMEM((128, 16, 128), bf16),
            pltpu.VMEM((128, 16, 128), bf16),
            dma((3,)), dma((2, 3)), dma((2,)), dma, dma((6,)), dma((6,)), dma, dma((3, 8)), dma, dma,
            dma, dma, dma((3,)), dma((3,)), dma((3,)), dma((3, 2)), dma((3,)), dma((3, 2)),
            dma((3,)), dma((3,)), dma((2,)), dma((2,)), dma((2,)), dma((2,)), plain, plain,
        ],
        compiler_params=pltpu.CompilerParams(
            collective_id=1, has_side_effects=True, vmem_limit_bytes=60 * 2**20
        ),
        cost_estimate=pl.CostEstimate(flops=6 * 10**9, bytes_accessed=3 * 10**7, transcendentals=10**6),
        name="layer",
    )(
        queries, keys[:, 0], values[:, 0], lengths, o_proj, residual, norm_gain[None, :], routes.T,
        route_weights.T, gate_up[0], down[0],
    )


def solution(mesh):
    in_specs = (
        P("req", "kvh"),
        P("req", "kvh", None, None),
        P("req", "kvh", None, None),
        P("req"),
        P("kvh", "req"),
        P(("req", "kvh"), None),
        P(),
        P(("req", "kvh"), None, None),
        P(("req", "kvh"), None, None),
        P(("req", "kvh"), None),
        P(("req", "kvh"), None),
    )
    out_specs = P(("req", "kvh"), None)
    return jax.shard_map(body, mesh=mesh, in_specs=in_specs, out_specs=out_specs, check_vma=False)
```

```python
import math

import jax
import jax.numpy as jnp
from jax import lax
from jax.experimental import pallas as pl
from jax.experimental.pallas import tpu as pltpu
from jax.sharding import PartitionSpec as P


MESH = pl.DeviceIdType.MESH


def coords():
    r = lax.axis_index("req")
    k = lax.axis_index("kvh")
    return lax.rem(r, 2) * 2 + k // 2, r // 8, lax.rem(r // 2, 4), lax.rem(k, 2)


def place(x, y, z, c):
    x, y, z, c = lax.rem(x, 4), lax.rem(y, 4), lax.rem(z, 4), lax.rem(c, 2)
    return ((y * 4 + z) * 2 + x // 2, lax.rem(x, 2) * 2 + c)


def iota(shape, dim):
    return lax.broadcasted_iota(jnp.int32, shape, dim)


WIDTHS = (1024, 1024, 1024)
STARTS = (0, 1024, 2048)
REST = 3072


def ahead(axis, d):
    x, y, z, c = coords()
    return ((x, y, z + d, c), (x, y + d, z, c), (x + d, y, z, c))[axis]


def kernel(
    queries_hbm, keys_hbm, values_hbm, lengths_smem, o_proj_hbm, residual_hbm, gain_hbm, routes_smem, weights_smem,
    gate_up_hbm, down_hbm,
    out_hbm,
    out_ref, queries, residual, gain, keys, values, heads, attended, gathered, projection, partial, staged, pieces, collected, summed, state, gate_up,
    down, tiles, line, sent, received, rows, active, results, returned, shared, arrived, table, mix, spread, gather, blend,
    straight, straight_table, straight_mix, swap, out_straight, in_straight, back_straight, home_straight,
    out_sem, row_sem, cache_sem, weight_sem, o_own_sem, o_send_sem, o_recv_sem, a_send_sem, a_recv_sem, p_send_sem, p_recv_sem,
    tile_send_sem, tile_recv_sem, line_send_sem, line_recv_sem, send_sem, recv_sem, back_sem, return_sem,
    share_send_sem, share_recv_sem, straight_send_sem, straight_recv_sem, straight_back_sem, straight_home_sem,
    along_y, along_z,
):
    r, kv = lax.axis_index("req"), lax.axis_index("kvh")
    x, y, z, c = coords()
    half = lax.rem(r, 2)
    bf16, f32 = jnp.bfloat16, jnp.float32

    xs, ys, zs = ([lax.rem(at + d, 4) for d in range(4)] for at in (x, y, z))
    high_x, low_x, cores = [at // 2 for at in xs], [lax.rem(at, 2) * 2 for at in xs], [c, 1 - c]

    def away(dx, dy, dz, dc):
        return ((ys[dy % 4] * 4 + zs[dz % 4]) * 2 + high_x[dx % 4], low_x[dx % 4] + cores[dc])

    barrier = pltpu.get_barrier_semaphore()
    for d in range(1, 4):
        pl.semaphore_signal(barrier, inc=1, device_id=away(0, d, 0, 0), device_id_type=MESH)
    for d in range(1, 4):
        pl.semaphore_signal(barrier, inc=1, device_id=away(0, 0, d, 0), device_id_type=MESH)
    for dx in range(4):
        for dc in range(2):
            if dx or dc:
                pl.semaphore_signal(barrier, inc=1, device_id=away(dx, 0, 0, dc), device_id_type=MESH)

    def cache_load(m, which):
        source, target = ((keys_hbm, keys), (values_hbm, values))[which]
        part = pl.ds(m * 16, 16)
        return pltpu.make_async_copy(source.at[part], target.at[part], cache_sem.at[which, m])

    small = [
        pltpu.make_async_copy(source, target, row_sem.at[n])
        for n, (source, target) in enumerate(((queries_hbm, queries), (residual_hbm, residual), (gain_hbm, gain)))
    ]
    small[0].start()
    cache_load(0, 0).start()
    cache_load(0, 1).start()
    o_own = pltpu.make_async_copy(o_proj_hbm, projection.at[:, pl.ds(0, 128)], o_own_sem)
    loads = [
        pltpu.make_async_copy(gate_up_hbm, gate_up, weight_sem.at[0]),
        pltpu.make_async_copy(down_hbm, down, weight_sem.at[1]),
    ]

    def o_copy(source, slot, part, n, dy, rows):
        return pltpu.make_async_remote_copy(
            src_ref=source, dst_ref=projection.at[pl.ds(part * 1024, rows), pl.ds(slot * 128, 128)],
            send_sem=o_send_sem.at[n], recv_sem=o_recv_sem.at[n], device_id=place(x, y + dy, z, c),
            device_id_type=MESH,
        )

    def o_first(n):
        slot, part, dy = ((1, 0, 1), (3, 1, 3), (1, 1, 1), (3, 0, 3))[n]
        return o_copy(o_proj_hbm.at[pl.ds(part * 1024, 1024)], slot, part, n, dy, 1024)

    def o_pass(n):
        slot, part, dy = ((1, 0, 1), (3, 1, 3))[n]
        held = projection.at[pl.ds(part * 1024, 1024), pl.ds(slot * 128, 128)]
        return o_copy(held, 2, part, 4 + n, dy, 1024)

    pl.semaphore_wait(barrier, 13)
    for n in range(4):
        o_first(n).start()
    for d in range(1, 4):
        pl.semaphore_signal(along_y, inc=1, device_id=place(x, y + d, z, c), device_id_type=MESH)

    for m in range(1, 3):
        cache_load(m, 0).start()
        cache_load(m, 1).start()
    small[0].wait()
    for h in range(16):
        heads[:, h, :] = queries[:, h * 128 : (h + 1) * 128].astype(f32)

    position = iota((192, 128), 0)
    request = iota((128, 128), 1) // 16

    def attend(g):
        first = g * 8
        turned = jnp.transpose(heads[first : first + 8].reshape(128, 128))
        scores = jnp.zeros((192, 128), f32)
        for b in range(0, 8, 2):
            two = jnp.concatenate([keys[first + b], keys[first + b + 1]], axis=1)
            asked = jnp.concatenate(
                [jnp.where(request == b, turned, 0.0), jnp.where(request == b + 1, turned, 0.0)], axis=0
            ).astype(bf16)
            scores = scores + jnp.dot(two, asked, preferred_element_type=f32)
        scores = scores * (1.0 / math.sqrt(128.0))
        limit = jnp.zeros((1, 128), jnp.int32)
        for b in range(8):
            limit = jnp.where(request[:1] == b, lengths_smem[first + b], limit)
        scores = jnp.where(position < limit, scores, -1e30)
        shifted = jnp.exp(scores - jnp.max(scores, axis=0, keepdims=True))
        shares = shifted / jnp.sum(shifted, axis=0, keepdims=True)
        shares = jnp.transpose(shares).astype(bf16)
        for b in range(8):
            attended[first + b] = jnp.dot(
                shares[b * 16 : (b + 1) * 16], values[first + b], preferred_element_type=f32
            )

    def a_copy(slot, m, dz, dh):
        part = pl.ds(m * 16, 16)
        to = ((y * 4 + lax.rem(z + dz, 4)) * 2 + lax.rem(half + dh, 2), kv)
        return pltpu.make_async_remote_copy(
            src_ref=gathered.at[slot, part], dst_ref=gathered.at[slot + dz * 2 + dh, part], send_sem=a_send_sem,
            recv_sem=a_recv_sem.at[m, slot + dz * 2 + dh], device_id=to, device_id_type=MESH,
        )

    def a_wait(m, slot):
        landed = gathered.at[slot, pl.ds(m * 16, 16)]
        pltpu.make_async_copy(landed, landed, a_recv_sem.at[m, slot]).wait()

    def a_start(m):
        rows_here = slice(m * 16, (m + 1) * 16)
        for h in range(16):
            gathered[0, rows_here, h * 128 : (h + 1) * 128] = attended[rows_here, h, :].astype(bf16)

    def a_send(m):
        a_copy(0, m, 0, 1).start()
        for dz in (1, 3, 2):
            a_copy(0, m, dz, 0).start()

    for m in range(3):
        cache_load(m, 0).wait()
        cache_load(m, 1).wait()
        attend(2 * m)
        attend(2 * m + 1)
        a_start(m)
        a_send(m)
        if m == 1:
            pl.semaphore_wait(along_y, 3)
            for d in range(1, 4):
                pl.semaphore_signal(along_z, inc=1, device_id=place(x, y, z + d, c), device_id_type=MESH)
        if m == 2:
            pl.semaphore_wait(along_z, 3)
        if m == 0:
            o_own.start()
            small[1].start()
            small[2].start()
            for load in loads:
                load.start()
    for n in range(2):
        pltpu.make_async_copy(o_proj_hbm.at[pl.ds(0, 1024)], projection.at[pl.ds(0, 1024), pl.ds(128, 128)], o_recv_sem.at[n]).wait()
        o_pass(n).start()
    a_wait(0, 1)
    for dz in (1, 3, 2):
        a_copy(1, 0, dz, 0).start()
    for m in (1, 2):
        for dz in (1, 3, 2):
            a_wait(m, dz * 2)
            a_copy(dz * 2, m, 0, 1).start()

    state[...] = jnp.zeros((16, 4096), f32)
    small[1].wait()
    small[2].wait()
    state[:12, :] = residual[...].astype(f32)

    lane = iota((8, 128), 1)
    sub = iota((8, 128), 0)
    token = lane & 15
    expert = jnp.full((8, 128), -1, jnp.int32)
    gates = jnp.zeros((8, 128), f32)
    for t in range(12):
        for k in range(8):
            here = (sub == k) & (token == t)
            expert = jnp.where(here, routes_smem[k, t], expert)
            gates = jnp.where(here, weights_smem[k, t], gates)
    place_of = jnp.zeros((8, 128), jnp.int32)
    for t in range(12):
        for k in range(8):
            place_of = place_of + jnp.where((expert == routes_smem[k, t]) & (token > t), 1, 0)
    tiles[9, :8, :] = jnp.where(token < 12, expert * 2 + place_of, -1).astype(f32)
    tiles[9, 8:, :] = gates

    for f in range(3):
        for d in range(1, 4):
            pltpu.make_async_remote_copy(
                src_ref=tiles.at[9], dst_ref=tiles.at[f * 3 + d - 1], send_sem=tile_send_sem, recv_sem=tile_recv_sem,
                device_id=place(*ahead(f, d)), device_id_type=MESH,
            ).start()
        line[f][0] = jnp.zeros((16, WIDTHS[f]), bf16)

    for f in range(3):
        def column(i):
            half_of, n = i // 128, i & 127
            dx, dy, dz, row = n // 32, (n // 8) & 3, (n // 2) & 3, n & 1
            p, q, g = ((dx, dy, dz), (dx, dz, dy), (dy, dz, dx))[f]
            return (p * 4 + q) * 16 + half_of * 8 + g * 2 + row

        i, j = iota((256, 256), 0), iota((256, 256), 1)
        spread[f] = jnp.where(j == column(i), 1.0, 0.0).astype(bf16)
        gather[f] = jnp.where(i == column(j), 1.0, 0.0).astype(bf16)

    number = expert
    ring, group = number // 4, number & 3
    dx = ((ring & 1) * 2 + group // 2 + 4 - x) & 3
    dy = (ring // 8 + 4 - y) & 3
    dz = (((ring // 2) & 3) + 4 - z) & 3
    dc = ((group & 1) + 2 - c) & 1
    key = (dc * 64 + dx * 16 + dy * 4 + dz) * 2 + place_of
    key = jnp.where(token < 12, key, -1)
    for part in range(8):
        row = iota((256, 128), 0) + part * 256
        hit = jnp.zeros((256, 128), f32)
        for k in range(8):
            hit = jnp.where(row // 8 == key[k : k + 1, :], 1.0, hit)
        hit = jnp.where((row & 7) == iota((256, 128), 1) // 16, hit, 0.0)
        straight_table[part * 256 : (part + 1) * 256, :] = hit.astype(bf16)
    key_column = jnp.transpose(key.astype(f32)).astype(jnp.int32)
    gate_column = jnp.transpose(gates)
    for part in range(8):
        spot = iota((128, 256), 1) + part * 256
        share = jnp.zeros((128, 256), f32)
        for k in range(8):
            share = jnp.where(spot // 8 == key_column[:, k : k + 1], gate_column[:, k : k + 1], share)
        share = jnp.where((spot & 7) == iota((128, 256), 0) // 16, share, 0.0)
        high = share.astype(bf16)
        straight_mix[:128, part * 256 : (part + 1) * 256] = high
        straight_mix[128:, part * 256 : (part + 1) * 256] = (share - high.astype(f32)).astype(bf16)
    i, j = iota((256, 256), 0), iota((256, 256), 1)
    swap[0] = jnp.where(j == (i & 31) * 8 + i // 32, 1.0, 0.0).astype(bf16)
    swap[1] = jnp.where(i == (j & 31) * 8 + j // 32, 1.0, 0.0).astype(bf16)
    straight[...] = jnp.zeros((128, 128), bf16)

    landed = tiles.at[pl.ds(0, 9)]
    pltpu.make_async_copy(landed, landed, tile_recv_sem).wait()
    for f in range(3):
        marks = jnp.full((8, 128), -1, jnp.int32)
        gates = jnp.zeros((8, 128), f32)
        for d in range(4):
            tile = tiles[9] if d == 0 else tiles[f * 3 + d - 1]
            marks = jnp.where(lane // 16 == d, tile[:8].astype(jnp.int32), marks)
            gates = jnp.where(lane // 16 == d, tile[8:], gates)
        number = marks // 2
        ring, group = number // 4, number & 3
        dx = ((ring & 1) * 2 + group // 2 + 4 - x) & 3
        dy = (ring // 8 + 4 - y) & 3
        dz = ((ring // 2) & 3) + 4 - z & 3
        dc = ((group & 1) + 2 - c) & 1
        p, q, g = ((dx, dy, dz), (dx, dz, dy), (dy, dz, dx))[f]
        key = ((dc * 16 + p * 4 + q) * 4 + lane // 16) * 2 + (marks & 1)
        key = jnp.where((marks >= 0) & (g == 0), key, -1)
        row = iota((256, 64), 0)
        hit = jnp.zeros((256, 64), f32)
        for k in range(8):
            hit = jnp.where(row == key[k : k + 1, :64], 1.0, hit)
        table[f] = hit.astype(bf16)
        key_column = jnp.transpose(key.astype(f32))[:64].astype(jnp.int32)
        gate_column = jnp.transpose(gates)[:64]
        spot = iota((64, 512), 1)
        share = jnp.zeros((64, 512), f32)
        for k in range(8):
            share = jnp.where(
                (spot // 16) * 8 + (spot & 7) == key_column[:, k : k + 1], gate_column[:, k : k + 1], share
            )
        for h in range(2):
            part = jnp.where((spot // 8) & 1 == h, share, 0.0)
            high = part.astype(bf16)
            mix[f, h, :64, :] = high
            mix[f, h, 64:, :] = (part - high.astype(f32)).astype(bf16)

    o_own.wait()
    for n in range(2, 6):
        pltpu.make_async_copy(o_proj_hbm.at[pl.ds(0, 1024)], projection.at[pl.ds(0, 1024), pl.ds(128, 128)], o_recv_sem.at[n]).wait()
    for m in range(3):
        for slot in range(1, 8):
            if not (slot == 1 and m == 0 or slot in (2, 4, 6) and m > 0):
                a_wait(m, slot)
    halves, lows = [half, 1 - half], [kv // 2, 1 - kv // 2]

    def hand_out(d, e):
        to = lows[e // 2] * 2 + cores[e % 2]
        pltpu.make_async_remote_copy(
            src_ref=pieces.at[d * 4 + to], dst_ref=collected.at[d * 4 + e], send_sem=p_send_sem, recv_sem=p_recv_sem,
            device_id=((y * 4 + zs[d // 2]) * 2 + halves[d % 2], to), device_id_type=MESH,
        ).start()

    for turn in range(2):
        slots = slice(turn * 4, turn * 4 + 4)
        partial[turn * 192 : (turn + 1) * 192, :] = jnp.dot(
            gathered[slots].reshape(192, 2048), projection[...], preferred_element_type=f32
        )
        for slot in range(turn * 4, turn * 4 + 4):
            d = ((4 - slot // 2) % 4) * 2 + slot % 2
            for k in range(4):
                for w in range(4):
                    staged[d * 4 + k, w * 12 : (w + 1) * 12, :] = partial[
                        slot * 48 + k * 12 : slot * 48 + (k + 1) * 12, w * 128 : (w + 1) * 128
                    ]
            pieces[d * 4 : d * 4 + 4] = staged[d * 4 : d * 4 + 4].astype(bf16)
            for e in range(4):
                if d or e:
                    hand_out(d, e)
    collected[0] = pieces[kv]
    landed = collected.at[pl.ds(1, 31)]
    pltpu.make_async_copy(landed, landed, p_recv_sem).wait()
    square = jnp.zeros((12, 128), f32)
    for p in range(8):
        slot = (lax.rem(z + 4 - p // 2, 4) * 2 + lax.rem(half + p % 2, 2)) * 4
        total = collected[slot].astype(f32)
        for e in range(1, 4):
            total = total + collected[slot + e].astype(f32)
        summed[p] = total
        for w in range(4):
            columns = pl.ds(pl.multiple_of((lax.rem(y + 4 - w, 4) * 8 + p) * 128, 128), 128)
            total = state[:12, columns] + summed[p, w * 12 : (w + 1) * 12, :]
            state[:12, columns] = total
            square = square + total * total
    factor = lax.rsqrt(jnp.sum(square, axis=1, keepdims=True) * (1.0 / 4096.0) + 1e-06)
    for f in range(3):
        columns = slice(STARTS[f], STARTS[f] + WIDTHS[f])
        line[f][0, :12, :] = (state[:12, columns] * factor * gain[:, columns]).astype(bf16)
        for d in (2, 1, 3):
            pltpu.make_async_remote_copy(
                src_ref=line[f].at[0], dst_ref=line[f].at[d], send_sem=line_send_sem.at[f],
                recv_sem=line_recv_sem.at[f], device_id=place(*ahead(f, d)), device_id_type=MESH,
            ).start()

    for s in range(8):
        columns = slice(REST + s * 128, REST + (s + 1) * 128)
        straight[s * 16 : s * 16 + 12, :] = (state[:12, columns] * factor * gain[:, columns]).astype(bf16)

    def straight_sends(source, target, send_sems, recv_sems, group, sign):
        def start(dx, dy, i, dz):
            there = (lax.rem(y + dy, 4) * 4 + zs[sign * dz % 4]) * 2 + lax.rem(x + dx, 4) // 2
            j = group * 64 + i * 4 + dz
            pltpu.make_async_remote_copy(
                src_ref=source.at[j], dst_ref=target.at[j], send_sem=send_sems.at[group], recv_sem=recv_sems.at[group],
                device_id=(there, lax.rem(x + dx, 2) * 2 + cores[group]), device_id_type=MESH,
            ).start()

        def four(i, carry):
            for dz in range(4):
                start(sign * (i // 4) + 4, sign * lax.rem(i, 4) + 4, i, dz)
            return carry

        for dz in range(1 - group, 4):
            start(0, 0, 0, dz)
        lax.fori_loop(1, 16, four, 0)

    def straight_out(group):
        for part in range(group * 4, group * 4 + 4):
            block = jnp.dot(
                straight_table[part * 256 : (part + 1) * 256, :], straight[...], preferred_element_type=f32
            ).astype(bf16)
            out_straight[part * 16 : (part + 1) * 16] = block.reshape(16, 16, 128)
        straight_sends(out_straight, in_straight, straight_send_sem, straight_recv_sem, group, 1)

    straight_out(0)
    in_straight[0] = out_straight[0]

    def across(f, j, sign):
        p, q, dc = sign * (j // 4 % 4), sign * (j % 4), j // 16
        return away(*((p, q, 0, dc), (p, 0, q, dc), (0, p, q, dc))[f])

    for group in range(2):
        blocks = range(group * 16, group * 16 + 16)
        for f in range(3):
            width = WIDTHS[f] // 2
            if group == 0:
                landed = line[f].at[pl.ds(1, 3)]
                pltpu.make_async_copy(landed, landed, line_recv_sem.at[f]).wait()
            block = jnp.dot(
                table[f, group * 128 : (group + 1) * 128], line[f][...].reshape(64, WIDTHS[f]),
                preferred_element_type=f32,
            ).reshape(16, 8, WIDTHS[f])
            sent[f][group * 16 : (group + 1) * 16] = jnp.concatenate(
                [block[:, :, :width], block[:, :, width:]], axis=1
            ).astype(bf16)
        for j in blocks:
            for f in range(3):
                if j:
                    pltpu.make_async_remote_copy(
                        src_ref=sent[f].at[j], dst_ref=received[f].at[j], send_sem=send_sem.at[f],
                        recv_sem=recv_sem.at[f, group], device_id=across(f, j, 1), device_id_type=MESH,
                    ).start()
    straight_out(1)
    for f in range(3):
        received[f][0] = sent[f][0]

    for group in range(2):
        first = 1 - group
        for f in range(3):
            width, start = WIDTHS[f] // 2, STARTS[f]
            landed = received[f].at[pl.ds(group * 16 + first, 16 - first)]
            pltpu.make_async_copy(landed, landed, recv_sem.at[f, group]).wait()
            block = received[f][group * 16 : (group + 1) * 16].reshape(256, width)
            block = jnp.dot(spread[f], block, preferred_element_type=f32).astype(bf16)
            for h in range(2):
                rows[:, start + h * width : start + (h + 1) * width] = block[h * 128 : (h + 1) * 128]
        landed = in_straight.at[pl.ds(group * 64 + first, 64 - first)]
        pltpu.make_async_copy(landed, landed, straight_recv_sem.at[group]).wait()
        for chunk in range(4):
            block = in_straight[group * 64 + chunk * 16 : group * 64 + (chunk + 1) * 16].reshape(256, 128)
            block = jnp.dot(swap[0], block, preferred_element_type=f32).astype(bf16)
            for s in range(8):
                rows[chunk * 32 : (chunk + 1) * 32, REST + s * 128 : REST + (s + 1) * 128] = block[s * 32 : (s + 1) * 32]
        if group == 0:
            loads[0].wait()
        for n in range(3):
            gate = jnp.dot(rows[...], gate_up[:, n * 256 : (n + 1) * 256], preferred_element_type=f32)
            up = jnp.dot(rows[...], gate_up[:, 768 + n * 256 : 768 + (n + 1) * 256], preferred_element_type=f32)
            active[:, n * 256 : (n + 1) * 256] = (gate / (1.0 + jnp.exp(-gate)) * up).astype(bf16)
        if group == 0:
            loads[1].wait()
        for f in range(3):
            width, start = WIDTHS[f] // 2, STARTS[f]
            served = jnp.dot(active[...], down[:, start : start + 2 * width], preferred_element_type=f32).astype(bf16)
            served = jnp.concatenate([served[:, :width], served[:, width:]], axis=0)
            block = jnp.dot(gather[f], served, preferred_element_type=f32).astype(bf16)
            results[f][group * 16 : (group + 1) * 16] = block.reshape(16, 16, width)

            if group == 0:
                returned[f][0] = results[f][0]

        for j in range(group * 16 + first, group * 16 + 16):
            for f in range(3):
                pltpu.make_async_remote_copy(
                    src_ref=results[f].at[j], dst_ref=returned[f].at[j], send_sem=back_sem.at[f],
                    recv_sem=return_sem.at[f, group], device_id=across(f, j, -1), device_id_type=MESH,
                ).start()
        served = jnp.dot(active[...], down[:, REST : REST + 1024], preferred_element_type=f32).astype(bf16)
        for chunk in range(4):
            block = jnp.concatenate(
                [served[chunk * 32 : (chunk + 1) * 32, s * 128 : (s + 1) * 128] for s in range(8)], axis=0
            )
            block = jnp.dot(swap[1], block, preferred_element_type=f32).astype(bf16)
            back_straight[group * 64 + chunk * 16 : group * 64 + (chunk + 1) * 16] = block.reshape(16, 16, 128)
        straight_sends(back_straight, home_straight, straight_back_sem, straight_home_sem, group, -1)
        if group == 0:
            home_straight[0] = back_straight[0]

    def mixed(f, group, h):
        block = returned[f][group * 16 : (group + 1) * 16].reshape(256, WIDTHS[f] // 2)
        both = jnp.dot(mix[f, h, :, group * 256 : (group + 1) * 256], block, preferred_element_type=f32)
        return both[:64] + both[64:]

    for f in range(3):
        width, start = WIDTHS[f] // 2, STARTS[f]
        landed = returned[f].at[pl.ds(1, 15)]
        pltpu.make_async_copy(landed, landed, return_sem.at[f, 0]).wait()
        for h in range(2):
            blend[:, start + h * width : start + (h + 1) * width] = mixed(f, 0, h)
    for f in range(3):
        width, start = WIDTHS[f] // 2, STARTS[f]
        landed = returned[f].at[pl.ds(16, 16)]
        pltpu.make_async_copy(landed, landed, return_sem.at[f, 1]).wait()
        for h in range(2):
            columns = slice(start + h * width, start + (h + 1) * width)
            both = blend[:, columns] + mixed(f, 1, h)
            state[:12, columns] = state[:12, columns] + both[:12]
            for d in range(1, 4):
                shared[f][d - 1, :, h * width : (h + 1) * width] = both[d * 16 : (d + 1) * 16].astype(bf16)
        for d in (2, 1, 3):
            pltpu.make_async_remote_copy(
                src_ref=shared[f].at[d - 1], dst_ref=arrived[f].at[d - 1], send_sem=share_send_sem.at[f],
                recv_sem=share_recv_sem.at[f], device_id=place(*ahead(f, 4 - d)), device_id_type=MESH,
            ).start()
    for group in range(2):
        landed = home_straight.at[pl.ds(group * 64 + 1 - group, 63 + group)]
        pltpu.make_async_copy(landed, landed, straight_home_sem.at[group]).wait()
    both = jnp.dot(straight_mix[...], home_straight[...].reshape(2048, 128), preferred_element_type=f32)
    both = both[:128] + both[128:]
    for s in range(8):
        columns = slice(REST + s * 128, REST + (s + 1) * 128)
        out_ref[:, columns] = (state[:12, columns] + both[s * 16 : s * 16 + 12]).astype(bf16)
    def give(n, start, width):
        part = pl.ds(start, width)
        return pltpu.make_async_copy(out_ref.at[:, part], out_hbm.at[:, part], out_sem.at[n])

    give(3, REST, 1024).start()
    for f in range(3):
        columns = slice(STARTS[f], STARTS[f] + WIDTHS[f])
        pltpu.make_async_copy(arrived[f], arrived[f], share_recv_sem.at[f]).wait()
        total = state[:12, columns]
        for d in range(3):
            total = total + arrived[f][d, :12, :].astype(f32)
        out_ref[:, columns] = total.astype(bf16)
        give(f, STARTS[f], WIDTHS[f]).start()

    for n in range(6):
        pltpu.make_async_copy(
            o_proj_hbm.at[pl.ds(0, 1024)], projection.at[pl.ds(0, 1024), pl.ds(128, 128)], o_send_sem.at[n]
        ).wait()
    gone = gathered.at[pl.ds(1, 7)]
    pltpu.make_async_copy(gone, gone, a_send_sem).wait()
    gone = collected.at[pl.ds(1, 31)]
    pltpu.make_async_copy(gone, gone, p_send_sem).wait()
    gone = tiles.at[pl.ds(0, 9)]
    pltpu.make_async_copy(gone, gone, tile_send_sem).wait()
    for f in range(3):
        gone = line[f].at[pl.ds(1, 3)]
        pltpu.make_async_copy(gone, gone, line_send_sem.at[f]).wait()
        gone = sent[f].at[pl.ds(1, 31)]
        pltpu.make_async_copy(gone, gone, send_sem.at[f]).wait()
        gone = results[f].at[pl.ds(1, 31)]
        pltpu.make_async_copy(gone, gone, back_sem.at[f]).wait()
        pltpu.make_async_copy(shared[f], shared[f], share_send_sem.at[f]).wait()
    for group in range(2):
        gone = out_straight.at[pl.ds(group * 64 + 1 - group, 63 + group)]
        pltpu.make_async_copy(gone, gone, straight_send_sem.at[group]).wait()
        gone = back_straight.at[pl.ds(group * 64 + 1 - group, 63 + group)]
        pltpu.make_async_copy(gone, gone, straight_back_sem.at[group]).wait()
    for f in range(3):
        give(f, STARTS[f], WIDTHS[f]).wait()
    give(3, REST, 1024).wait()


def body(
    queries, keys, values, lengths, o_proj, residual, norm_gain, gate_up, down, routes, route_weights,
):
    bf16, f32 = jnp.bfloat16, jnp.float32
    vmem = pl.BlockSpec(memory_space=pltpu.VMEM)
    smem = pl.BlockSpec(memory_space=pltpu.SMEM)
    hbm = pl.BlockSpec(memory_space=pl.ANY)
    each = lambda shape: tuple(shape(w) for w in WIDTHS)
    dma, plain = pltpu.SemaphoreType.DMA, pltpu.SemaphoreType.REGULAR
    return pl.pallas_call(
        kernel,
        out_shape=jax.ShapeDtypeStruct((12, 4096), bf16),
        in_specs=[hbm, hbm, hbm, smem, hbm, hbm, hbm, smem, smem, hbm, hbm],
        out_specs=hbm,
        scratch_shapes=[
            pltpu.VMEM((12, 4096), bf16),
            pltpu.VMEM((48, 2048), bf16),
            pltpu.VMEM((12, 4096), bf16),
            pltpu.VMEM((1, 4096), f32),
            pltpu.VMEM((48, 192, 128), bf16),
            pltpu.VMEM((48, 192, 128), bf16),
            pltpu.VMEM((48, 16, 128), f32),
            pltpu.VMEM((48, 16, 128), f32),
            pltpu.VMEM((8, 48, 2048), bf16),
            pltpu.VMEM((2048, 512), bf16),
            pltpu.VMEM((384, 512), f32),
            pltpu.VMEM((32, 48, 128), f32),
            pltpu.VMEM((32, 48, 128), bf16),
            pltpu.VMEM((32, 48, 128), bf16),
            pltpu.VMEM((8, 48, 128), f32),
            pltpu.VMEM((16, 4096), f32),
            pltpu.VMEM((4096, 1536), bf16),
            pltpu.VMEM((768, 4096), bf16),
            pltpu.VMEM((10, 16, 128), f32),
            each(lambda w: pltpu.VMEM((4, 16, w), bf16)),
            each(lambda w: pltpu.VMEM((32, 16, w // 2), bf16)),
            each(lambda w: pltpu.VMEM((32, 16, w // 2), bf16)),
            pltpu.VMEM((128, 4096), bf16),
            pltpu.VMEM((128, 768), bf16),
            each(lambda w: pltpu.VMEM((32, 16, w // 2), bf16)),
            each(lambda w: pltpu.VMEM((32, 16, w // 2), bf16)),
            each(lambda w: pltpu.VMEM((3, 16, w), bf16)),
            each(lambda w: pltpu.VMEM((3, 16, w), bf16)),
            pltpu.VMEM((3, 256, 64), bf16),
            pltpu.VMEM((3, 2, 128, 512), bf16),
            pltpu.VMEM((3, 256, 256), bf16),
            pltpu.VMEM((3, 256, 256), bf16),
            pltpu.VMEM((64, 3072), f32),
            pltpu.VMEM((128, 128), bf16),
            pltpu.VMEM((2048, 128), bf16),
            pltpu.VMEM((256, 2048), bf16),
            pltpu.VMEM((2, 256, 256), bf16),
            pltpu.VMEM((128, 16, 128), bf16),
            pltpu.VMEM((128, 16, 128), bf16),
            pltpu.VMEM((128, 16, 128), bf16),
            pltpu.VMEM((128, 16, 128), bf16),
            dma((4,)), dma((3,)), dma((2, 3)), dma((2,)), dma, dma((6,)), dma((6,)), dma, dma((3, 8)), dma, dma,
            dma, dma, dma((3,)), dma((3,)), dma((3,)), dma((3, 2)), dma((3,)), dma((3, 2)),
            dma((3,)), dma((3,)), dma((2,)), dma((2,)), dma((2,)), dma((2,)), plain, plain,
        ],
        compiler_params=pltpu.CompilerParams(
            collective_id=1, has_side_effects=True, vmem_limit_bytes=60 * 2**20
        ),
        cost_estimate=pl.CostEstimate(flops=6 * 10**9, bytes_accessed=3 * 10**7, transcendentals=10**6),
        name="layer",
    )(
        queries, keys[:, 0], values[:, 0], lengths, o_proj, residual, norm_gain[None, :], routes.T,
        route_weights.T, gate_up[0], down[0],
    )


def solution(mesh):
    in_specs = (
        P("req", "kvh"),
        P("req", "kvh", None, None),
        P("req", "kvh", None, None),
        P("req"),
        P("kvh", "req"),
        P(("req", "kvh"), None),
        P(),
        P(("req", "kvh"), None, None),
        P(("req", "kvh"), None, None),
        P(("req", "kvh"), None),
        P(("req", "kvh"), None),
    )
    out_specs = P(("req", "kvh"), None)
    return jax.shard_map(body, mesh=mesh, in_specs=in_specs, out_specs=out_specs, check_vma=False)
```

```python
import math

import jax
import jax.numpy as jnp
from jax import lax
from jax.experimental import pallas as pl
from jax.experimental.pallas import tpu as pltpu
from jax.sharding import PartitionSpec as P


MESH = pl.DeviceIdType.MESH


def coords():
    r = lax.axis_index("req")
    k = lax.axis_index("kvh")
    return lax.rem(r, 2) * 2 + k // 2, r // 8, lax.rem(r // 2, 4), lax.rem(k, 2)


def place(x, y, z, c):
    x, y, z, c = lax.rem(x, 4), lax.rem(y, 4), lax.rem(z, 4), lax.rem(c, 2)
    return ((y * 4 + z) * 2 + x // 2, lax.rem(x, 2) * 2 + c)


def iota(shape, dim):
    return lax.broadcasted_iota(jnp.int32, shape, dim)


WIDTHS = (1024, 1024, 1024)
STARTS = (0, 1024, 2048)
REST = 3072


def ahead(axis, d):
    x, y, z, c = coords()
    return ((x, y, z + d, c), (x, y + d, z, c), (x + d, y, z, c))[axis]


def kernel(
    queries_hbm, keys_hbm, values_hbm, lengths_smem, o_proj_hbm, residual_hbm, gain_hbm, routes_smem, weights_smem,
    gate_up_hbm, down_hbm,
    out_hbm,
    out_ref, queries, residual, gain, keys, values, heads, attended, gathered, projection, partial, staged, pieces, collected, summed, state, gate_up,
    down, tiles, line, sent, received, rows, active, results, returned, shared, arrived, table, mix, spread, gather, blend,
    straight, straight_table, straight_mix, swap, out_straight, in_straight, back_straight, home_straight,
    out_sem, row_sem, cache_sem, weight_sem, o_own_sem, o_send_sem, o_recv_sem, a_send_sem, a_recv_sem, p_send_sem, p_recv_sem,
    tile_send_sem, tile_recv_sem, line_send_sem, line_recv_sem, send_sem, recv_sem, back_sem, return_sem,
    share_send_sem, share_recv_sem, straight_send_sem, straight_recv_sem, straight_back_sem, straight_home_sem,
    along_y, along_z,
):
    r, kv = lax.axis_index("req"), lax.axis_index("kvh")
    x, y, z, c = coords()
    half = lax.rem(r, 2)
    bf16, f32 = jnp.bfloat16, jnp.float32

    xs, ys, zs = ([lax.rem(at + d, 4) for d in range(4)] for at in (x, y, z))
    high_x, low_x, cores = [at // 2 for at in xs], [lax.rem(at, 2) * 2 for at in xs], [c, 1 - c]

    def away(dx, dy, dz, dc):
        return ((ys[dy % 4] * 4 + zs[dz % 4]) * 2 + high_x[dx % 4], low_x[dx % 4] + cores[dc])

    barrier = pltpu.get_barrier_semaphore()
    for d in range(1, 4):
        pl.semaphore_signal(barrier, inc=1, device_id=away(0, d, 0, 0), device_id_type=MESH)
    for d in range(1, 4):
        pl.semaphore_signal(barrier, inc=1, device_id=away(0, 0, d, 0), device_id_type=MESH)
    for dx in range(4):
        for dc in range(2):
            if dx or dc:
                pl.semaphore_signal(barrier, inc=1, device_id=away(dx, 0, 0, dc), device_id_type=MESH)

    def cache_load(m, which):
        source, target = ((keys_hbm, keys), (values_hbm, values))[which]
        part = pl.ds(m * 16, 16)
        return pltpu.make_async_copy(source.at[part], target.at[part], cache_sem.at[which, m])

    small = [
        pltpu.make_async_copy(source, target, row_sem.at[n])
        for n, (source, target) in enumerate(((queries_hbm, queries), (residual_hbm, residual), (gain_hbm, gain)))
    ]
    small[0].start()
    cache_load(0, 0).start()
    cache_load(0, 1).start()
    o_own = pltpu.make_async_copy(o_proj_hbm, projection.at[:, pl.ds(0, 128)], o_own_sem)
    loads = [
        pltpu.make_async_copy(gate_up_hbm, gate_up, weight_sem.at[0]),
        pltpu.make_async_copy(down_hbm, down, weight_sem.at[1]),
    ]

    def o_copy(source, slot, part, n, dy, rows):
        return pltpu.make_async_remote_copy(
            src_ref=source, dst_ref=projection.at[pl.ds(part * 1024, rows), pl.ds(slot * 128, 128)],
            send_sem=o_send_sem.at[n], recv_sem=o_recv_sem.at[n], device_id=place(x, y + dy, z, c),
            device_id_type=MESH,
        )

    def o_first(n):
        slot, part, dy = ((1, 0, 1), (3, 1, 3), (1, 1, 1), (3, 0, 3))[n]
        return o_copy(o_proj_hbm.at[pl.ds(part * 1024, 1024)], slot, part, n, dy, 1024)

    def o_pass(n):
        slot, part, dy = ((1, 0, 1), (3, 1, 3))[n]
        held = projection.at[pl.ds(part * 1024, 1024), pl.ds(slot * 128, 128)]
        return o_copy(held, 2, part, 4 + n, dy, 1024)

    pl.semaphore_wait(barrier, 13)
    for n in range(4):
        o_first(n).start()
    for d in range(1, 4):
        pl.semaphore_signal(along_y, inc=1, device_id=place(x, y + d, z, c), device_id_type=MESH)

    for m in range(1, 3):
        cache_load(m, 0).start()
        cache_load(m, 1).start()
    small[0].wait()
    for h in range(16):
        heads[:, h, :] = queries[:, h * 128 : (h + 1) * 128].astype(f32)

    position = iota((192, 128), 0)
    request = iota((128, 128), 1) // 16

    def attend(g):
        first = g * 8
        turned = jnp.transpose(heads[first : first + 8].reshape(128, 128))
        scores = jnp.zeros((192, 128), f32)
        for b in range(0, 8, 2):
            two = jnp.concatenate([keys[first + b], keys[first + b + 1]], axis=1)
            asked = jnp.concatenate(
                [jnp.where(request == b, turned, 0.0), jnp.where(request == b + 1, turned, 0.0)], axis=0
            ).astype(bf16)
            scores = scores + jnp.dot(two, asked, preferred_element_type=f32)
        scores = scores * (1.0 / math.sqrt(128.0))
        limit = jnp.zeros((1, 128), jnp.int32)
        for b in range(8):
            limit = jnp.where(request[:1] == b, lengths_smem[first + b], limit)
        scores = jnp.where(position < limit, scores, -1e30)
        shifted = jnp.exp(scores - jnp.max(scores, axis=0, keepdims=True))
        shares = shifted / jnp.sum(shifted, axis=0, keepdims=True)
        shares = jnp.transpose(shares).astype(bf16)
        for b in range(8):
            attended[first + b] = jnp.dot(
                shares[b * 16 : (b + 1) * 16], values[first + b], preferred_element_type=f32
            )

    def a_copy(slot, m, dz, dh):
        part = pl.ds(m * 16, 16)
        to = ((y * 4 + lax.rem(z + dz, 4)) * 2 + lax.rem(half + dh, 2), kv)
        return pltpu.make_async_remote_copy(
            src_ref=gathered.at[slot, part], dst_ref=gathered.at[slot + dz * 2 + dh, part], send_sem=a_send_sem,
            recv_sem=a_recv_sem.at[m, slot + dz * 2 + dh], device_id=to, device_id_type=MESH,
        )

    def a_wait(m, slot):
        landed = gathered.at[slot, pl.ds(m * 16, 16)]
        pltpu.make_async_copy(landed, landed, a_recv_sem.at[m, slot]).wait()

    def a_start(m):
        rows_here = slice(m * 16, (m + 1) * 16)
        for h in range(16):
            gathered[0, rows_here, h * 128 : (h + 1) * 128] = attended[rows_here, h, :].astype(bf16)

    def a_send(m):
        a_copy(0, m, 0, 1).start()
        for dz in (1, 3, 2):
            a_copy(0, m, dz, 0).start()

    for m in range(3):
        cache_load(m, 0).wait()
        cache_load(m, 1).wait()
        attend(2 * m)
        attend(2 * m + 1)
        a_start(m)
        a_send(m)
        if m == 1:
            pl.semaphore_wait(along_y, 3)
            for d in range(1, 4):
                pl.semaphore_signal(along_z, inc=1, device_id=place(x, y, z + d, c), device_id_type=MESH)
        if m == 2:
            pl.semaphore_wait(along_z, 3)
        if m == 0:
            o_own.start()
            small[1].start()
            small[2].start()
            for load in loads:
                load.start()
    for n in range(2):
        pltpu.make_async_copy(o_proj_hbm.at[pl.ds(0, 1024)], projection.at[pl.ds(0, 1024), pl.ds(128, 128)], o_recv_sem.at[n]).wait()
        o_pass(n).start()
    a_wait(0, 1)
    for dz in (1, 3, 2):
        a_copy(1, 0, dz, 0).start()
    for m in (1, 2):
        for dz in (1, 3, 2):
            a_wait(m, dz * 2)
            a_copy(dz * 2, m, 0, 1).start()

    state[...] = jnp.zeros((16, 4096), f32)
    small[1].wait()
    small[2].wait()
    state[:12, :] = residual[...].astype(f32)

    lane = iota((8, 128), 1)
    sub = iota((8, 128), 0)
    token = lane & 15
    expert = jnp.full((8, 128), -1, jnp.int32)
    gates = jnp.zeros((8, 128), f32)
    for t in range(12):
        for k in range(8):
            here = (sub == k) & (token == t)
            expert = jnp.where(here, routes_smem[k, t], expert)
            gates = jnp.where(here, weights_smem[k, t], gates)
    place_of = jnp.zeros((8, 128), jnp.int32)
    for t in range(12):
        for k in range(8):
            place_of = place_of + jnp.where((expert == routes_smem[k, t]) & (token > t), 1, 0)
    tiles[9, :8, :] = jnp.where(token < 12, expert * 2 + place_of, -1).astype(f32)
    tiles[9, 8:, :] = gates

    for f in range(3):
        for d in range(1, 4):
            pltpu.make_async_remote_copy(
                src_ref=tiles.at[9], dst_ref=tiles.at[f * 3 + d - 1], send_sem=tile_send_sem, recv_sem=tile_recv_sem,
                device_id=place(*ahead(f, d)), device_id_type=MESH,
            ).start()
        line[f][0] = jnp.zeros((16, WIDTHS[f]), bf16)

    o_own.wait()
    for n in range(2, 6):
        pltpu.make_async_copy(o_proj_hbm.at[pl.ds(0, 1024)], projection.at[pl.ds(0, 1024), pl.ds(128, 128)], o_recv_sem.at[n]).wait()
    for m in range(3):
        for slot in range(1, 8):
            if not (slot == 1 and m == 0 or slot in (2, 4, 6) and m > 0):
                a_wait(m, slot)
    halves, lows = [half, 1 - half], [kv // 2, 1 - kv // 2]

    def hand_out(d, e):
        to = lows[e // 2] * 2 + cores[e % 2]
        pltpu.make_async_remote_copy(
            src_ref=pieces.at[d * 4 + to], dst_ref=collected.at[d * 4 + e], send_sem=p_send_sem, recv_sem=p_recv_sem,
            device_id=((y * 4 + zs[d // 2]) * 2 + halves[d % 2], to), device_id_type=MESH,
        ).start()

    for turn in range(2):
        slots = slice(turn * 4, turn * 4 + 4)
        partial[turn * 192 : (turn + 1) * 192, :] = jnp.dot(
            gathered[slots].reshape(192, 2048), projection[...], preferred_element_type=f32
        )
        for slot in range(turn * 4, turn * 4 + 4):
            d = ((4 - slot // 2) % 4) * 2 + slot % 2
            for k in range(4):
                for w in range(4):
                    staged[d * 4 + k, w * 12 : (w + 1) * 12, :] = partial[
                        slot * 48 + k * 12 : slot * 48 + (k + 1) * 12, w * 128 : (w + 1) * 128
                    ]
            pieces[d * 4 : d * 4 + 4] = staged[d * 4 : d * 4 + 4].astype(bf16)
            for e in range(4):
                if d or e:
                    hand_out(d, e)
    collected[0] = pieces[kv]
    number = expert
    ring, group = number // 4, number & 3
    dx = ((ring & 1) * 2 + group // 2 + 4 - x) & 3
    dy = (ring // 8 + 4 - y) & 3
    dz = (((ring // 2) & 3) + 4 - z) & 3
    dc = ((group & 1) + 2 - c) & 1
    key = (dc * 64 + dx * 16 + dy * 4 + dz) * 2 + place_of
    key = jnp.where(token < 12, key, -1)
    for part in range(8):
        row = iota((256, 128), 0) + part * 256
        hit = jnp.zeros((256, 128), f32)
        for k in range(8):
            hit = jnp.where(row // 8 == key[k : k + 1, :], 1.0, hit)
        hit = jnp.where((row & 7) == iota((256, 128), 1) // 16, hit, 0.0)
        straight_table[part * 256 : (part + 1) * 256, :] = hit.astype(bf16)
    own_key, own_gates = key, gates
    straight[...] = jnp.zeros((128, 128), bf16)

    landed = tiles.at[pl.ds(0, 9)]
    pltpu.make_async_copy(landed, landed, tile_recv_sem).wait()
    line_tables = []
    for f in range(3):
        marks = jnp.full((8, 128), -1, jnp.int32)
        gates = jnp.zeros((8, 128), f32)
        for d in range(4):
            tile = tiles[9] if d == 0 else tiles[f * 3 + d - 1]
            marks = jnp.where(lane // 16 == d, tile[:8].astype(jnp.int32), marks)
            gates = jnp.where(lane // 16 == d, tile[8:], gates)
        number = marks // 2
        ring, group = number // 4, number & 3
        dx = ((ring & 1) * 2 + group // 2 + 4 - x) & 3
        dy = (ring // 8 + 4 - y) & 3
        dz = ((ring // 2) & 3) + 4 - z & 3
        dc = ((group & 1) + 2 - c) & 1
        p, q, g = ((dx, dy, dz), (dx, dz, dy), (dy, dz, dx))[f]
        key = ((dc * 16 + p * 4 + q) * 4 + lane // 16) * 2 + (marks & 1)
        key = jnp.where((marks >= 0) & (g == 0), key, -1)
        row = iota((256, 64), 0)
        hit = jnp.zeros((256, 64), f32)
        for k in range(8):
            hit = jnp.where(row == key[k : k + 1, :64], 1.0, hit)
        table[f] = hit.astype(bf16)
        line_tables.append((key, gates))

    landed = collected.at[pl.ds(1, 31)]
    pltpu.make_async_copy(landed, landed, p_recv_sem).wait()
    square = jnp.zeros((12, 128), f32)
    for p in range(8):
        slot = (lax.rem(z + 4 - p // 2, 4) * 2 + lax.rem(half + p % 2, 2)) * 4
        total = collected[slot].astype(f32)
        for e in range(1, 4):
            total = total + collected[slot + e].astype(f32)
        summed[p] = total
        for w in range(4):
            columns = pl.ds(pl.multiple_of((lax.rem(y + 4 - w, 4) * 8 + p) * 128, 128), 128)
            total = state[:12, columns] + summed[p, w * 12 : (w + 1) * 12, :]
            state[:12, columns] = total
            square = square + total * total
    factor = lax.rsqrt(jnp.sum(square, axis=1, keepdims=True) * (1.0 / 4096.0) + 1e-06)
    for f in range(3):
        columns = slice(STARTS[f], STARTS[f] + WIDTHS[f])
        line[f][0, :12, :] = (state[:12, columns] * factor * gain[:, columns]).astype(bf16)
        for d in (2, 1, 3):
            pltpu.make_async_remote_copy(
                src_ref=line[f].at[0], dst_ref=line[f].at[d], send_sem=line_send_sem.at[f],
                recv_sem=line_recv_sem.at[f], device_id=place(*ahead(f, d)), device_id_type=MESH,
            ).start()

    for s in range(8):
        columns = slice(REST + s * 128, REST + (s + 1) * 128)
        straight[s * 16 : s * 16 + 12, :] = (state[:12, columns] * factor * gain[:, columns]).astype(bf16)

    def straight_sends(source, target, send_sems, recv_sems, group, sign):
        def start(dx, dy, i, dz):
            there = (lax.rem(y + dy, 4) * 4 + zs[sign * dz % 4]) * 2 + lax.rem(x + dx, 4) // 2
            j = group * 64 + i * 4 + dz
            pltpu.make_async_remote_copy(
                src_ref=source.at[j], dst_ref=target.at[j], send_sem=send_sems.at[group], recv_sem=recv_sems.at[group],
                device_id=(there, lax.rem(x + dx, 2) * 2 + cores[group]), device_id_type=MESH,
            ).start()

        def four(i, carry):
            for dz in range(4):
                start(sign * (i // 4) + 4, sign * lax.rem(i, 4) + 4, i, dz)
            return carry

        for dz in range(1 - group, 4):
            start(0, 0, 0, dz)
        lax.fori_loop(1, 16, four, 0)

    def straight_out(group):
        for part in range(group * 4, group * 4 + 4):
            block = jnp.dot(
                straight_table[part * 256 : (part + 1) * 256, :], straight[...], preferred_element_type=f32
            ).astype(bf16)
            out_straight[part * 16 : (part + 1) * 16] = block.reshape(16, 16, 128)
        straight_sends(out_straight, in_straight, straight_send_sem, straight_recv_sem, group, 1)

    straight_out(0)
    in_straight[0] = out_straight[0]

    def across(f, j, sign):
        p, q, dc = sign * (j // 4 % 4), sign * (j % 4), j // 16
        return away(*((p, q, 0, dc), (p, 0, q, dc), (0, p, q, dc))[f])

    for group in range(2):
        blocks = range(group * 16, group * 16 + 16)
        for f in range(3):
            width = WIDTHS[f] // 2
            if group == 0:
                landed = line[f].at[pl.ds(1, 3)]
                pltpu.make_async_copy(landed, landed, line_recv_sem.at[f]).wait()
            block = jnp.dot(
                table[f, group * 128 : (group + 1) * 128], line[f][...].reshape(64, WIDTHS[f]),
                preferred_element_type=f32,
            ).reshape(16, 8, WIDTHS[f])
            sent[f][group * 16 : (group + 1) * 16] = jnp.concatenate(
                [block[:, :, :width], block[:, :, width:]], axis=1
            ).astype(bf16)
        for j in blocks:
            for f in range(3):
                if j:
                    pltpu.make_async_remote_copy(
                        src_ref=sent[f].at[j], dst_ref=received[f].at[j], send_sem=send_sem.at[f],
                        recv_sem=recv_sem.at[f, group], device_id=across(f, j, 1), device_id_type=MESH,
                    ).start()
    straight_out(1)
    for f in range(3):
        received[f][0] = sent[f][0]

    for f in range(3):
        def column(i):
            half_of, n = i // 128, i & 127
            dx, dy, dz, row = n // 32, (n // 8) & 3, (n // 2) & 3, n & 1
            p, q, g = ((dx, dy, dz), (dx, dz, dy), (dy, dz, dx))[f]
            return (p * 4 + q) * 16 + half_of * 8 + g * 2 + row

        i, j = iota((256, 256), 0), iota((256, 256), 1)
        spread[f] = jnp.where(j == column(i), 1.0, 0.0).astype(bf16)
        gather[f] = jnp.where(i == column(j), 1.0, 0.0).astype(bf16)

    i, j = iota((256, 256), 0), iota((256, 256), 1)
    swap[0] = jnp.where(j == (i & 31) * 8 + i // 32, 1.0, 0.0).astype(bf16)
    swap[1] = jnp.where(i == (j & 31) * 8 + j // 32, 1.0, 0.0).astype(bf16)
    key_column = jnp.transpose(own_key.astype(f32)).astype(jnp.int32)
    gate_column = jnp.transpose(own_gates)
    for part in range(8):
        spot = iota((128, 256), 1) + part * 256
        share = jnp.zeros((128, 256), f32)
        for k in range(8):
            share = jnp.where(spot // 8 == key_column[:, k : k + 1], gate_column[:, k : k + 1], share)
        share = jnp.where((spot & 7) == iota((128, 256), 0) // 16, share, 0.0)
        high = share.astype(bf16)
        straight_mix[:128, part * 256 : (part + 1) * 256] = high
        straight_mix[128:, part * 256 : (part + 1) * 256] = (share - high.astype(f32)).astype(bf16)
    for f, (key, gates) in enumerate(line_tables):
        key_column = jnp.transpose(key.astype(f32))[:64].astype(jnp.int32)
        gate_column = jnp.transpose(gates)[:64]
        spot = iota((64, 512), 1)
        share = jnp.zeros((64, 512), f32)
        for k in range(8):
            share = jnp.where(
                (spot // 16) * 8 + (spot & 7) == key_column[:, k : k + 1], gate_column[:, k : k + 1], share
            )
        for h in range(2):
            part = jnp.where((spot // 8) & 1 == h, share, 0.0)
            high = part.astype(bf16)
            mix[f, h, :64, :] = high
            mix[f, h, 64:, :] = (part - high.astype(f32)).astype(bf16)

    for group in range(2):
        first = 1 - group
        for f in range(3):
            width, start = WIDTHS[f] // 2, STARTS[f]
            landed = received[f].at[pl.ds(group * 16 + first, 16 - first)]
            pltpu.make_async_copy(landed, landed, recv_sem.at[f, group]).wait()
            block = received[f][group * 16 : (group + 1) * 16].reshape(256, width)
            block = jnp.dot(spread[f], block, preferred_element_type=f32).astype(bf16)
            for h in range(2):
                rows[:, start + h * width : start + (h + 1) * width] = block[h * 128 : (h + 1) * 128]
        landed = in_straight.at[pl.ds(group * 64 + first, 64 - first)]
        pltpu.make_async_copy(landed, landed, straight_recv_sem.at[group]).wait()
        for chunk in range(4):
            block = in_straight[group * 64 + chunk * 16 : group * 64 + (chunk + 1) * 16].reshape(256, 128)
            block = jnp.dot(swap[0], block, preferred_element_type=f32).astype(bf16)
            for s in range(8):
                rows[chunk * 32 : (chunk + 1) * 32, REST + s * 128 : REST + (s + 1) * 128] = block[s * 32 : (s + 1) * 32]
        if group == 0:
            loads[0].wait()
        for n in range(3):
            gate = jnp.dot(rows[...], gate_up[:, n * 256 : (n + 1) * 256], preferred_element_type=f32)
            up = jnp.dot(rows[...], gate_up[:, 768 + n * 256 : 768 + (n + 1) * 256], preferred_element_type=f32)
            active[:, n * 256 : (n + 1) * 256] = (gate / (1.0 + jnp.exp(-gate)) * up).astype(bf16)
        if group == 0:
            loads[1].wait()
        for f in range(3):
            width, start = WIDTHS[f] // 2, STARTS[f]
            served = jnp.dot(active[...], down[:, start : start + 2 * width], preferred_element_type=f32).astype(bf16)
            served = jnp.concatenate([served[:, :width], served[:, width:]], axis=0)
            block = jnp.dot(gather[f], served, preferred_element_type=f32).astype(bf16)
            results[f][group * 16 : (group + 1) * 16] = block.reshape(16, 16, width)

            if group == 0:
                returned[f][0] = results[f][0]

        for j in range(group * 16 + first, group * 16 + 16):
            for f in range(3):
                pltpu.make_async_remote_copy(
                    src_ref=results[f].at[j], dst_ref=returned[f].at[j], send_sem=back_sem.at[f],
                    recv_sem=return_sem.at[f, group], device_id=across(f, j, -1), device_id_type=MESH,
                ).start()
        served = jnp.dot(active[...], down[:, REST : REST + 1024], preferred_element_type=f32).astype(bf16)
        for chunk in range(4):
            block = jnp.concatenate(
                [served[chunk * 32 : (chunk + 1) * 32, s * 128 : (s + 1) * 128] for s in range(8)], axis=0
            )
            block = jnp.dot(swap[1], block, preferred_element_type=f32).astype(bf16)
            back_straight[group * 64 + chunk * 16 : group * 64 + (chunk + 1) * 16] = block.reshape(16, 16, 128)
        straight_sends(back_straight, home_straight, straight_back_sem, straight_home_sem, group, -1)
        if group == 0:
            home_straight[0] = back_straight[0]

    def mixed(f, group, h):
        block = returned[f][group * 16 : (group + 1) * 16].reshape(256, WIDTHS[f] // 2)
        both = jnp.dot(mix[f, h, :, group * 256 : (group + 1) * 256], block, preferred_element_type=f32)
        return both[:64] + both[64:]

    for f in range(3):
        width, start = WIDTHS[f] // 2, STARTS[f]
        landed = returned[f].at[pl.ds(1, 15)]
        pltpu.make_async_copy(landed, landed, return_sem.at[f, 0]).wait()
        for h in range(2):
            blend[:, start + h * width : start + (h + 1) * width] = mixed(f, 0, h)
    for f in range(3):
        width, start = WIDTHS[f] // 2, STARTS[f]
        landed = returned[f].at[pl.ds(16, 16)]
        pltpu.make_async_copy(landed, landed, return_sem.at[f, 1]).wait()
        for h in range(2):
            columns = slice(start + h * width, start + (h + 1) * width)
            both = blend[:, columns] + mixed(f, 1, h)
            state[:12, columns] = state[:12, columns] + both[:12]
            for d in range(1, 4):
                shared[f][d - 1, :, h * width : (h + 1) * width] = both[d * 16 : (d + 1) * 16].astype(bf16)
        for d in (2, 1, 3):
            pltpu.make_async_remote_copy(
                src_ref=shared[f].at[d - 1], dst_ref=arrived[f].at[d - 1], send_sem=share_send_sem.at[f],
                recv_sem=share_recv_sem.at[f], device_id=place(*ahead(f, 4 - d)), device_id_type=MESH,
            ).start()
    for group in range(2):
        landed = home_straight.at[pl.ds(group * 64 + 1 - group, 63 + group)]
        pltpu.make_async_copy(landed, landed, straight_home_sem.at[group]).wait()
    both = jnp.dot(straight_mix[...], home_straight[...].reshape(2048, 128), preferred_element_type=f32)
    both = both[:128] + both[128:]
    for s in range(8):
        columns = slice(REST + s * 128, REST + (s + 1) * 128)
        out_ref[:, columns] = (state[:12, columns] + both[s * 16 : s * 16 + 12]).astype(bf16)
    def give(n, start, width):
        part = pl.ds(start, width)
        return pltpu.make_async_copy(out_ref.at[:, part], out_hbm.at[:, part], out_sem.at[n])

    give(3, REST, 1024).start()
    for f in range(3):
        columns = slice(STARTS[f], STARTS[f] + WIDTHS[f])
        pltpu.make_async_copy(arrived[f], arrived[f], share_recv_sem.at[f]).wait()
        total = state[:12, columns]
        for d in range(3):
            total = total + arrived[f][d, :12, :].astype(f32)
        out_ref[:, columns] = total.astype(bf16)
        give(f, STARTS[f], WIDTHS[f]).start()

    for n in range(6):
        pltpu.make_async_copy(
            o_proj_hbm.at[pl.ds(0, 1024)], projection.at[pl.ds(0, 1024), pl.ds(128, 128)], o_send_sem.at[n]
        ).wait()
    gone = gathered.at[pl.ds(1, 7)]
    pltpu.make_async_copy(gone, gone, a_send_sem).wait()
    gone = collected.at[pl.ds(1, 31)]
    pltpu.make_async_copy(gone, gone, p_send_sem).wait()
    gone = tiles.at[pl.ds(0, 9)]
    pltpu.make_async_copy(gone, gone, tile_send_sem).wait()
    for f in range(3):
        gone = line[f].at[pl.ds(1, 3)]
        pltpu.make_async_copy(gone, gone, line_send_sem.at[f]).wait()
        gone = sent[f].at[pl.ds(1, 31)]
        pltpu.make_async_copy(gone, gone, send_sem.at[f]).wait()
        gone = results[f].at[pl.ds(1, 31)]
        pltpu.make_async_copy(gone, gone, back_sem.at[f]).wait()
        pltpu.make_async_copy(shared[f], shared[f], share_send_sem.at[f]).wait()
    for group in range(2):
        gone = out_straight.at[pl.ds(group * 64 + 1 - group, 63 + group)]
        pltpu.make_async_copy(gone, gone, straight_send_sem.at[group]).wait()
        gone = back_straight.at[pl.ds(group * 64 + 1 - group, 63 + group)]
        pltpu.make_async_copy(gone, gone, straight_back_sem.at[group]).wait()
    for f in range(3):
        give(f, STARTS[f], WIDTHS[f]).wait()
    give(3, REST, 1024).wait()


def body(
    queries, keys, values, lengths, o_proj, residual, norm_gain, gate_up, down, routes, route_weights,
):
    bf16, f32 = jnp.bfloat16, jnp.float32
    vmem = pl.BlockSpec(memory_space=pltpu.VMEM)
    smem = pl.BlockSpec(memory_space=pltpu.SMEM)
    hbm = pl.BlockSpec(memory_space=pl.ANY)
    each = lambda shape: tuple(shape(w) for w in WIDTHS)
    dma, plain = pltpu.SemaphoreType.DMA, pltpu.SemaphoreType.REGULAR
    return pl.pallas_call(
        kernel,
        out_shape=jax.ShapeDtypeStruct((12, 4096), bf16),
        in_specs=[hbm, hbm, hbm, smem, hbm, hbm, hbm, smem, smem, hbm, hbm],
        out_specs=hbm,
        scratch_shapes=[
            pltpu.VMEM((12, 4096), bf16),
            pltpu.VMEM((48, 2048), bf16),
            pltpu.VMEM((12, 4096), bf16),
            pltpu.VMEM((1, 4096), f32),
            pltpu.VMEM((48, 192, 128), bf16),
            pltpu.VMEM((48, 192, 128), bf16),
            pltpu.VMEM((48, 16, 128), f32),
            pltpu.VMEM((48, 16, 128), f32),
            pltpu.VMEM((8, 48, 2048), bf16),
            pltpu.VMEM((2048, 512), bf16),
            pltpu.VMEM((384, 512), f32),
            pltpu.VMEM((32, 48, 128), f32),
            pltpu.VMEM((32, 48, 128), bf16),
            pltpu.VMEM((32, 48, 128), bf16),
            pltpu.VMEM((8, 48, 128), f32),
            pltpu.VMEM((16, 4096), f32),
            pltpu.VMEM((4096, 1536), bf16),
            pltpu.VMEM((768, 4096), bf16),
            pltpu.VMEM((10, 16, 128), f32),
            each(lambda w: pltpu.VMEM((4, 16, w), bf16)),
            each(lambda w: pltpu.VMEM((32, 16, w // 2), bf16)),
            each(lambda w: pltpu.VMEM((32, 16, w // 2), bf16)),
            pltpu.VMEM((128, 4096), bf16),
            pltpu.VMEM((128, 768), bf16),
            each(lambda w: pltpu.VMEM((32, 16, w // 2), bf16)),
            each(lambda w: pltpu.VMEM((32, 16, w // 2), bf16)),
            each(lambda w: pltpu.VMEM((3, 16, w), bf16)),
            each(lambda w: pltpu.VMEM((3, 16, w), bf16)),
            pltpu.VMEM((3, 256, 64), bf16),
            pltpu.VMEM((3, 2, 128, 512), bf16),
            pltpu.VMEM((3, 256, 256), bf16),
            pltpu.VMEM((3, 256, 256), bf16),
            pltpu.VMEM((64, 3072), f32),
            pltpu.VMEM((128, 128), bf16),
            pltpu.VMEM((2048, 128), bf16),
            pltpu.VMEM((256, 2048), bf16),
            pltpu.VMEM((2, 256, 256), bf16),
            pltpu.VMEM((128, 16, 128), bf16),
            pltpu.VMEM((128, 16, 128), bf16),
            pltpu.VMEM((128, 16, 128), bf16),
            pltpu.VMEM((128, 16, 128), bf16),
            dma((4,)), dma((3,)), dma((2, 3)), dma((2,)), dma, dma((6,)), dma((6,)), dma, dma((3, 8)), dma, dma,
            dma, dma, dma((3,)), dma((3,)), dma((3,)), dma((3, 2)), dma((3,)), dma((3, 2)),
            dma((3,)), dma((3,)), dma((2,)), dma((2,)), dma((2,)), dma((2,)), plain, plain,
        ],
        compiler_params=pltpu.CompilerParams(
            collective_id=1, has_side_effects=True, vmem_limit_bytes=60 * 2**20
        ),
        cost_estimate=pl.CostEstimate(flops=6 * 10**9, bytes_accessed=3 * 10**7, transcendentals=10**6),
        name="layer",
    )(
        queries, keys[:, 0], values[:, 0], lengths, o_proj, residual, norm_gain[None, :], routes.T,
        route_weights.T, gate_up[0], down[0],
    )


def solution(mesh):
    in_specs = (
        P("req", "kvh"),
        P("req", "kvh", None, None),
        P("req", "kvh", None, None),
        P("req"),
        P("kvh", "req"),
        P(("req", "kvh"), None),
        P(),
        P(("req", "kvh"), None, None),
        P(("req", "kvh"), None, None),
        P(("req", "kvh"), None),
        P(("req", "kvh"), None),
    )
    out_specs = P(("req", "kvh"), None)
    return jax.shard_map(body, mesh=mesh, in_specs=in_specs, out_specs=out_specs, check_vma=False)
```

```python
import math

import jax
import jax.numpy as jnp
from jax import lax
from jax.experimental import pallas as pl
from jax.experimental.pallas import tpu as pltpu
from jax.sharding import PartitionSpec as P


MESH = pl.DeviceIdType.MESH


def coords():
    r = lax.axis_index("req")
    k = lax.axis_index("kvh")
    return lax.rem(r, 2) * 2 + k // 2, r // 8, lax.rem(r // 2, 4), lax.rem(k, 2)


def place(x, y, z, c):
    x, y, z, c = lax.rem(x, 4), lax.rem(y, 4), lax.rem(z, 4), lax.rem(c, 2)
    return ((y * 4 + z) * 2 + x // 2, lax.rem(x, 2) * 2 + c)


def iota(shape, dim):
    return lax.broadcasted_iota(jnp.int32, shape, dim)


WIDTHS = (1024, 1024, 1024)
STARTS = (0, 1024, 2048)
REST = 3072


def ahead(axis, d):
    x, y, z, c = coords()
    return ((x, y, z + d, c), (x, y + d, z, c), (x + d, y, z, c))[axis]


def kernel(
    queries_hbm, keys_hbm, values_hbm, lengths_smem, o_proj_hbm, residual_hbm, gain_hbm, routes_smem, weights_smem,
    gate_up_hbm, down_hbm,
    out_hbm,
    out_ref, queries, residual, gain, keys, values, heads, attended, gathered, projection, partial, staged, pieces, collected, summed, state, gate_up,
    down, tiles, line, sent, received, rows, active, results, returned, shared, arrived, table, mix, spread, gather, blend,
    straight, straight_table, straight_mix, swap, out_straight, in_straight, back_straight, home_straight,
    out_sem, row_sem, cache_sem, weight_sem, o_own_sem, o_send_sem, o_recv_sem, a_send_sem, a_recv_sem, p_send_sem, p_recv_sem,
    tile_send_sem, tile_recv_sem, line_send_sem, line_recv_sem, send_sem, recv_sem, back_sem, return_sem,
    share_send_sem, share_recv_sem, straight_send_sem, straight_recv_sem, straight_back_sem, straight_home_sem,
    along_y, along_z,
):
    r, kv = lax.axis_index("req"), lax.axis_index("kvh")
    x, y, z, c = coords()
    half = lax.rem(r, 2)
    bf16, f32 = jnp.bfloat16, jnp.float32

    xs, ys, zs = ([lax.rem(at + d, 4) for d in range(4)] for at in (x, y, z))
    high_x, low_x, cores = [at // 2 for at in xs], [lax.rem(at, 2) * 2 for at in xs], [c, 1 - c]

    def away(dx, dy, dz, dc):
        return ((ys[dy % 4] * 4 + zs[dz % 4]) * 2 + high_x[dx % 4], low_x[dx % 4] + cores[dc])

    barrier = pltpu.get_barrier_semaphore()
    for d in range(1, 4):
        pl.semaphore_signal(barrier, inc=1, device_id=away(0, d, 0, 0), device_id_type=MESH)
    for d in range(1, 4):
        pl.semaphore_signal(barrier, inc=1, device_id=away(0, 0, d, 0), device_id_type=MESH)
    for dx in range(4):
        for dc in range(2):
            if dx or dc:
                pl.semaphore_signal(barrier, inc=1, device_id=away(dx, 0, 0, dc), device_id_type=MESH)

    def cache_load(m, which):
        source, target = ((keys_hbm, keys), (values_hbm, values))[which]
        part = pl.ds(m * 16, 16)
        return pltpu.make_async_copy(source.at[part], target.at[part], cache_sem.at[which, m])

    small = [
        pltpu.make_async_copy(source, target, row_sem.at[n])
        for n, (source, target) in enumerate(((queries_hbm, queries), (residual_hbm, residual), (gain_hbm, gain)))
    ]
    small[0].start()
    cache_load(0, 0).start()
    cache_load(0, 1).start()
    o_own = pltpu.make_async_copy(o_proj_hbm, projection.at[:, pl.ds(0, 128)], o_own_sem)
    loads = [
        pltpu.make_async_copy(gate_up_hbm, gate_up, weight_sem.at[0]),
        pltpu.make_async_copy(down_hbm, down, weight_sem.at[1]),
    ]

    def o_copy(source, slot, part, n, dy, rows):
        return pltpu.make_async_remote_copy(
            src_ref=source, dst_ref=projection.at[pl.ds(part * 1024, rows), pl.ds(slot * 128, 128)],
            send_sem=o_send_sem.at[n], recv_sem=o_recv_sem.at[n], device_id=place(x, y + dy, z, c),
            device_id_type=MESH,
        )

    def o_first(n):
        slot, part, dy = ((1, 0, 1), (3, 1, 3), (1, 1, 1), (3, 0, 3))[n]
        return o_copy(o_proj_hbm.at[pl.ds(part * 1024, 1024)], slot, part, n, dy, 1024)

    def o_pass(n):
        slot, part, dy = ((1, 0, 1), (3, 1, 3))[n]
        held = projection.at[pl.ds(part * 1024, 1024), pl.ds(slot * 128, 128)]
        return o_copy(held, 2, part, 4 + n, dy, 1024)

    pl.semaphore_wait(barrier, 13)
    for n in range(4):
        o_first(n).start()
    for d in range(1, 4):
        pl.semaphore_signal(along_y, inc=1, device_id=place(x, y + d, z, c), device_id_type=MESH)

    for m in range(1, 3):
        cache_load(m, 0).start()
        cache_load(m, 1).start()
    small[0].wait()
    for h in range(16):
        heads[:, h, :] = queries[:, h * 128 : (h + 1) * 128].astype(f32)

    position = iota((192, 128), 0)
    request = iota((128, 128), 1) // 16

    def attend(g):
        first = g * 8
        turned = jnp.transpose(heads[first : first + 8].reshape(128, 128))
        scores = jnp.zeros((192, 128), f32)
        for b in range(0, 8, 2):
            two = jnp.concatenate([keys[first + b], keys[first + b + 1]], axis=1)
            asked = jnp.concatenate(
                [jnp.where(request == b, turned, 0.0), jnp.where(request == b + 1, turned, 0.0)], axis=0
            ).astype(bf16)
            scores = scores + jnp.dot(two, asked, preferred_element_type=f32)
        scores = scores * (1.0 / math.sqrt(128.0))
        limit = jnp.zeros((1, 128), jnp.int32)
        for b in range(8):
            limit = jnp.where(request[:1] == b, lengths_smem[first + b], limit)
        scores = jnp.where(position < limit, scores, -1e30)
        shifted = jnp.exp(scores - jnp.max(scores, axis=0, keepdims=True))
        shares = shifted / jnp.sum(shifted, axis=0, keepdims=True)
        shares = jnp.transpose(shares).astype(bf16)
        for b in range(8):
            attended[first + b] = jnp.dot(
                shares[b * 16 : (b + 1) * 16], values[first + b], preferred_element_type=f32
            )

    def a_copy(slot, m, dz, dh):
        part = pl.ds(m * 16, 16)
        to = ((y * 4 + lax.rem(z + dz, 4)) * 2 + lax.rem(half + dh, 2), kv)
        return pltpu.make_async_remote_copy(
            src_ref=gathered.at[slot, part], dst_ref=gathered.at[slot + dz * 2 + dh, part], send_sem=a_send_sem,
            recv_sem=a_recv_sem.at[m, slot + dz * 2 + dh], device_id=to, device_id_type=MESH,
        )

    def a_wait(m, slot):
        landed = gathered.at[slot, pl.ds(m * 16, 16)]
        pltpu.make_async_copy(landed, landed, a_recv_sem.at[m, slot]).wait()

    def a_start(m):
        rows_here = slice(m * 16, (m + 1) * 16)
        for h in range(16):
            gathered[0, rows_here, h * 128 : (h + 1) * 128] = attended[rows_here, h, :].astype(bf16)

    def a_send(m):
        a_copy(0, m, 0, 1).start()
        for dz in (1, 3, 2):
            a_copy(0, m, dz, 0).start()

    for m in range(3):
        cache_load(m, 0).wait()
        cache_load(m, 1).wait()
        attend(2 * m)
        attend(2 * m + 1)
        a_start(m)
        a_send(m)
        if m == 1:
            pl.semaphore_wait(along_y, 3)
            for d in range(1, 4):
                pl.semaphore_signal(along_z, inc=1, device_id=place(x, y, z + d, c), device_id_type=MESH)
        if m == 2:
            pl.semaphore_wait(along_z, 3)
        if m == 0:
            o_own.start()
            small[1].start()
            small[2].start()
            for load in loads:
                load.start()
    for n in range(2):
        pltpu.make_async_copy(o_proj_hbm.at[pl.ds(0, 1024)], projection.at[pl.ds(0, 1024), pl.ds(128, 128)], o_recv_sem.at[n]).wait()
        o_pass(n).start()
    a_wait(0, 1)
    for dz in (1, 3, 2):
        a_copy(1, 0, dz, 0).start()
    for m in (1, 2):
        for dz in (1, 3, 2):
            a_wait(m, dz * 2)
            a_copy(dz * 2, m, 0, 1).start()

    state[...] = jnp.zeros((16, 4096), f32)
    small[1].wait()
    small[2].wait()
    state[:12, :] = residual[...].astype(f32)

    lane = iota((8, 128), 1)
    sub = iota((8, 128), 0)
    token = lane & 15
    expert = jnp.full((8, 128), -1, jnp.int32)
    gates = jnp.zeros((8, 128), f32)
    for t in range(12):
        for k in range(8):
            here = (sub == k) & (token == t)
            expert = jnp.where(here, routes_smem[k, t], expert)
            gates = jnp.where(here, weights_smem[k, t], gates)
    place_of = jnp.zeros((8, 128), jnp.int32)
    for t in range(12):
        for k in range(8):
            place_of = place_of + jnp.where((expert == routes_smem[k, t]) & (token > t), 1, 0)
    tiles[9, :8, :] = jnp.where(token < 12, expert * 2 + place_of, -1).astype(f32)
    tiles[9, 8:, :] = gates

    for f in range(3):
        for d in range(1, 4):
            pltpu.make_async_remote_copy(
                src_ref=tiles.at[9], dst_ref=tiles.at[f * 3 + d - 1], send_sem=tile_send_sem, recv_sem=tile_recv_sem,
                device_id=place(*ahead(f, d)), device_id_type=MESH,
            ).start()
        line[f][0] = jnp.zeros((16, WIDTHS[f]), bf16)

    o_own.wait()
    for n in range(2, 4):
        pltpu.make_async_copy(o_proj_hbm.at[pl.ds(0, 1024)], projection.at[pl.ds(0, 1024), pl.ds(128, 128)], o_recv_sem.at[n]).wait()
    for m in range(3):
        for slot in range(1, 8):
            if not (slot == 1 and m == 0 or slot in (2, 4, 6) and m > 0):
                a_wait(m, slot)
    partial[:, :256] = jnp.dot(gathered[...].reshape(384, 2048), projection[:, :256], preferred_element_type=f32)
    for n in range(4, 6):
        pltpu.make_async_copy(o_proj_hbm.at[pl.ds(0, 1024)], projection.at[pl.ds(0, 1024), pl.ds(128, 128)], o_recv_sem.at[n]).wait()
    halves, lows = [half, 1 - half], [kv // 2, 1 - kv // 2]

    def hand_out(d, e):
        to = lows[e // 2] * 2 + cores[e % 2]
        pltpu.make_async_remote_copy(
            src_ref=pieces.at[d * 4 + to], dst_ref=collected.at[d * 4 + e], send_sem=p_send_sem, recv_sem=p_recv_sem,
            device_id=((y * 4 + zs[d // 2]) * 2 + halves[d % 2], to), device_id_type=MESH,
        ).start()

    for turn in range(2):
        slots = slice(turn * 4, turn * 4 + 4)
        partial[turn * 192 : (turn + 1) * 192, 256:] = jnp.dot(
            gathered[slots].reshape(192, 2048), projection[:, 256:], preferred_element_type=f32
        )
        for slot in range(turn * 4, turn * 4 + 4):
            d = ((4 - slot // 2) % 4) * 2 + slot % 2
            for k in range(4):
                for w in range(4):
                    staged[d * 4 + k, w * 12 : (w + 1) * 12, :] = partial[
                        slot * 48 + k * 12 : slot * 48 + (k + 1) * 12, w * 128 : (w + 1) * 128
                    ]
            pieces[d * 4 : d * 4 + 4] = staged[d * 4 : d * 4 + 4].astype(bf16)
            for e in range(4):
                if d or e:
                    hand_out(d, e)
    collected[0] = pieces[kv]
    number = expert
    ring, group = number // 4, number & 3
    dx = ((ring & 1) * 2 + group // 2 + 4 - x) & 3
    dy = (ring // 8 + 4 - y) & 3
    dz = (((ring // 2) & 3) + 4 - z) & 3
    dc = ((group & 1) + 2 - c) & 1
    key = (dc * 64 + dx * 16 + dy * 4 + dz) * 2 + place_of
    key = jnp.where(token < 12, key, -1)
    for part in range(8):
        row = iota((256, 128), 0) + part * 256
        hit = jnp.zeros((256, 128), f32)
        for k in range(8):
            hit = jnp.where(row // 8 == key[k : k + 1, :], 1.0, hit)
        hit = jnp.where((row & 7) == iota((256, 128), 1) // 16, hit, 0.0)
        straight_table[part * 256 : (part + 1) * 256, :] = hit.astype(bf16)
    own_key, own_gates = key, gates
    straight[...] = jnp.zeros((128, 128), bf16)

    landed = tiles.at[pl.ds(0, 9)]
    pltpu.make_async_copy(landed, landed, tile_recv_sem).wait()
    line_tables = []
    for f in range(3):
        marks = jnp.full((8, 128), -1, jnp.int32)
        gates = jnp.zeros((8, 128), f32)
        for d in range(4):
            tile = tiles[9] if d == 0 else tiles[f * 3 + d - 1]
            marks = jnp.where(lane // 16 == d, tile[:8].astype(jnp.int32), marks)
            gates = jnp.where(lane // 16 == d, tile[8:], gates)
        number = marks // 2
        ring, group = number // 4, number & 3
        dx = ((ring & 1) * 2 + group // 2 + 4 - x) & 3
        dy = (ring // 8 + 4 - y) & 3
        dz = ((ring // 2) & 3) + 4 - z & 3
        dc = ((group & 1) + 2 - c) & 1
        p, q, g = ((dx, dy, dz), (dx, dz, dy), (dy, dz, dx))[f]
        key = ((dc * 16 + p * 4 + q) * 4 + lane // 16) * 2 + (marks & 1)
        key = jnp.where((marks >= 0) & (g == 0), key, -1)
        row = iota((256, 64), 0)
        hit = jnp.zeros((256, 64), f32)
        for k in range(8):
            hit = jnp.where(row == key[k : k + 1, :64], 1.0, hit)
        table[f] = hit.astype(bf16)
        line_tables.append((key, gates))

    landed = collected.at[pl.ds(1, 31)]
    pltpu.make_async_copy(landed, landed, p_recv_sem).wait()
    square = jnp.zeros((12, 128), f32)
    for p in range(8):
        slot = (lax.rem(z + 4 - p // 2, 4) * 2 + lax.rem(half + p % 2, 2)) * 4
        total = collected[slot].astype(f32)
        for e in range(1, 4):
            total = total + collected[slot + e].astype(f32)
        summed[p] = total
        for w in range(4):
            columns = pl.ds(pl.multiple_of((lax.rem(y + 4 - w, 4) * 8 + p) * 128, 128), 128)
            total = state[:12, columns] + summed[p, w * 12 : (w + 1) * 12, :]
            state[:12, columns] = total
            square = square + total * total
    factor = lax.rsqrt(jnp.sum(square, axis=1, keepdims=True) * (1.0 / 4096.0) + 1e-06)
    for f in range(3):
        columns = slice(STARTS[f], STARTS[f] + WIDTHS[f])
        line[f][0, :12, :] = (state[:12, columns] * factor * gain[:, columns]).astype(bf16)
        for d in (2, 1, 3):
            pltpu.make_async_remote_copy(
                src_ref=line[f].at[0], dst_ref=line[f].at[d], send_sem=line_send_sem.at[f],
                recv_sem=line_recv_sem.at[f], device_id=place(*ahead(f, d)), device_id_type=MESH,
            ).start()

    for s in range(8):
        columns = slice(REST + s * 128, REST + (s + 1) * 128)
        straight[s * 16 : s * 16 + 12, :] = (state[:12, columns] * factor * gain[:, columns]).astype(bf16)

    def straight_sends(source, target, send_sems, recv_sems, group, sign):
        def start(dx, dy, i, dz):
            there = (lax.rem(y + dy, 4) * 4 + zs[sign * dz % 4]) * 2 + lax.rem(x + dx, 4) // 2
            j = group * 64 + i * 4 + dz
            pltpu.make_async_remote_copy(
                src_ref=source.at[j], dst_ref=target.at[j], send_sem=send_sems.at[group], recv_sem=recv_sems.at[group],
                device_id=(there, lax.rem(x + dx, 2) * 2 + cores[group]), device_id_type=MESH,
            ).start()

        def four(i, carry):
            for dz in range(4):
                start(sign * (i // 4) + 4, sign * lax.rem(i, 4) + 4, i, dz)
            return carry

        for dz in range(1 - group, 4):
            start(0, 0, 0, dz)
        lax.fori_loop(1, 16, four, 0)

    def straight_out(group):
        for part in range(group * 4, group * 4 + 4):
            block = jnp.dot(
                straight_table[part * 256 : (part + 1) * 256, :], straight[...], preferred_element_type=f32
            ).astype(bf16)
            out_straight[part * 16 : (part + 1) * 16] = block.reshape(16, 16, 128)
        straight_sends(out_straight, in_straight, straight_send_sem, straight_recv_sem, group, 1)

    straight_out(0)
    in_straight[0] = out_straight[0]

    def across(f, j, sign):
        p, q, dc = sign * (j // 4 % 4), sign * (j % 4), j // 16
        return away(*((p, q, 0, dc), (p, 0, q, dc), (0, p, q, dc))[f])

    for group in range(2):
        blocks = range(group * 16, group * 16 + 16)
        for f in range(3):
            width = WIDTHS[f] // 2
            if group == 0:
                landed = line[f].at[pl.ds(1, 3)]
                pltpu.make_async_copy(landed, landed, line_recv_sem.at[f]).wait()
            block = jnp.dot(
                table[f, group * 128 : (group + 1) * 128], line[f][...].reshape(64, WIDTHS[f]),
                preferred_element_type=f32,
            ).reshape(16, 8, WIDTHS[f])
            sent[f][group * 16 : (group + 1) * 16] = jnp.concatenate(
                [block[:, :, :width], block[:, :, width:]], axis=1
            ).astype(bf16)
        for j in blocks:
            for f in range(3):
                if j:
                    pltpu.make_async_remote_copy(
                        src_ref=sent[f].at[j], dst_ref=received[f].at[j], send_sem=send_sem.at[f],
                        recv_sem=recv_sem.at[f, group], device_id=across(f, j, 1), device_id_type=MESH,
                    ).start()
    straight_out(1)
    for f in range(3):
        received[f][0] = sent[f][0]

    for f in range(3):
        def column(i):
            half_of, n = i // 128, i & 127
            dx, dy, dz, row = n // 32, (n // 8) & 3, (n // 2) & 3, n & 1
            p, q, g = ((dx, dy, dz), (dx, dz, dy), (dy, dz, dx))[f]
            return (p * 4 + q) * 16 + half_of * 8 + g * 2 + row

        i, j = iota((256, 256), 0), iota((256, 256), 1)
        spread[f] = jnp.where(j == column(i), 1.0, 0.0).astype(bf16)
        gather[f] = jnp.where(i == column(j), 1.0, 0.0).astype(bf16)

    i, j = iota((256, 256), 0), iota((256, 256), 1)
    swap[0] = jnp.where(j == (i & 31) * 8 + i // 32, 1.0, 0.0).astype(bf16)
    swap[1] = jnp.where(i == (j & 31) * 8 + j // 32, 1.0, 0.0).astype(bf16)
    key_column = jnp.transpose(own_key.astype(f32)).astype(jnp.int32)
    gate_column = jnp.transpose(own_gates)
    for part in range(8):
        spot = iota((128, 256), 1) + part * 256
        share = jnp.zeros((128, 256), f32)
        for k in range(8):
            share = jnp.where(spot // 8 == key_column[:, k : k + 1], gate_column[:, k : k + 1], share)
        share = jnp.where((spot & 7) == iota((128, 256), 0) // 16, share, 0.0)
        high = share.astype(bf16)
        straight_mix[:128, part * 256 : (part + 1) * 256] = high
        straight_mix[128:, part * 256 : (part + 1) * 256] = (share - high.astype(f32)).astype(bf16)
    for f, (key, gates) in enumerate(line_tables):
        key_column = jnp.transpose(key.astype(f32))[:64].astype(jnp.int32)
        gate_column = jnp.transpose(gates)[:64]
        spot = iota((64, 512), 1)
        share = jnp.zeros((64, 512), f32)
        for k in range(8):
            share = jnp.where(
                (spot // 16) * 8 + (spot & 7) == key_column[:, k : k + 1], gate_column[:, k : k + 1], share
            )
        for h in range(2):
            part = jnp.where((spot // 8) & 1 == h, share, 0.0)
            high = part.astype(bf16)
            mix[f, h, :64, :] = high
            mix[f, h, 64:, :] = (part - high.astype(f32)).astype(bf16)

    for group in range(2):
        first = 1 - group
        for f in range(3):
            width, start = WIDTHS[f] // 2, STARTS[f]
            landed = received[f].at[pl.ds(group * 16 + first, 16 - first)]
            pltpu.make_async_copy(landed, landed, recv_sem.at[f, group]).wait()
            block = received[f][group * 16 : (group + 1) * 16].reshape(256, width)
            block = jnp.dot(spread[f], block, preferred_element_type=f32).astype(bf16)
            for h in range(2):
                rows[:, start + h * width : start + (h + 1) * width] = block[h * 128 : (h + 1) * 128]
        landed = in_straight.at[pl.ds(group * 64 + first, 64 - first)]
        pltpu.make_async_copy(landed, landed, straight_recv_sem.at[group]).wait()
        for chunk in range(4):
            block = in_straight[group * 64 + chunk * 16 : group * 64 + (chunk + 1) * 16].reshape(256, 128)
            block = jnp.dot(swap[0], block, preferred_element_type=f32).astype(bf16)
            for s in range(8):
                rows[chunk * 32 : (chunk + 1) * 32, REST + s * 128 : REST + (s + 1) * 128] = block[s * 32 : (s + 1) * 32]
        if group == 0:
            loads[0].wait()
        for n in range(3):
            gate = jnp.dot(rows[...], gate_up[:, n * 256 : (n + 1) * 256], preferred_element_type=f32)
            up = jnp.dot(rows[...], gate_up[:, 768 + n * 256 : 768 + (n + 1) * 256], preferred_element_type=f32)
            active[:, n * 256 : (n + 1) * 256] = (gate / (1.0 + jnp.exp(-gate)) * up).astype(bf16)
        if group == 0:
            loads[1].wait()
        for f in range(3):
            width, start = WIDTHS[f] // 2, STARTS[f]
            served = jnp.dot(active[...], down[:, start : start + 2 * width], preferred_element_type=f32).astype(bf16)
            served = jnp.concatenate([served[:, :width], served[:, width:]], axis=0)
            block = jnp.dot(gather[f], served, preferred_element_type=f32).astype(bf16)
            results[f][group * 16 : (group + 1) * 16] = block.reshape(16, 16, width)

            if group == 0:
                returned[f][0] = results[f][0]

        for j in range(group * 16 + first, group * 16 + 16):
            for f in range(3):
                pltpu.make_async_remote_copy(
                    src_ref=results[f].at[j], dst_ref=returned[f].at[j], send_sem=back_sem.at[f],
                    recv_sem=return_sem.at[f, group], device_id=across(f, j, -1), device_id_type=MESH,
                ).start()
        served = jnp.dot(active[...], down[:, REST : REST + 1024], preferred_element_type=f32).astype(bf16)
        for chunk in range(4):
            block = jnp.concatenate(
                [served[chunk * 32 : (chunk + 1) * 32, s * 128 : (s + 1) * 128] for s in range(8)], axis=0
            )
            block = jnp.dot(swap[1], block, preferred_element_type=f32).astype(bf16)
            back_straight[group * 64 + chunk * 16 : group * 64 + (chunk + 1) * 16] = block.reshape(16, 16, 128)
        straight_sends(back_straight, home_straight, straight_back_sem, straight_home_sem, group, -1)
        if group == 0:
            home_straight[0] = back_straight[0]

    def mixed(f, group, h):
        block = returned[f][group * 16 : (group + 1) * 16].reshape(256, WIDTHS[f] // 2)
        both = jnp.dot(mix[f, h, :, group * 256 : (group + 1) * 256], block, preferred_element_type=f32)
        return both[:64] + both[64:]

    for f in range(3):
        width, start = WIDTHS[f] // 2, STARTS[f]
        landed = returned[f].at[pl.ds(1, 15)]
        pltpu.make_async_copy(landed, landed, return_sem.at[f, 0]).wait()
        for h in range(2):
            blend[:, start + h * width : start + (h + 1) * width] = mixed(f, 0, h)
    for f in range(3):
        width, start = WIDTHS[f] // 2, STARTS[f]
        landed = returned[f].at[pl.ds(16, 16)]
        pltpu.make_async_copy(landed, landed, return_sem.at[f, 1]).wait()
        for h in range(2):
            columns = slice(start + h * width, start + (h + 1) * width)
            both = blend[:, columns] + mixed(f, 1, h)
            state[:12, columns] = state[:12, columns] + both[:12]
            for d in range(1, 4):
                shared[f][d - 1, :, h * width : (h + 1) * width] = both[d * 16 : (d + 1) * 16].astype(bf16)
        for d in (2, 1, 3):
            pltpu.make_async_remote_copy(
                src_ref=shared[f].at[d - 1], dst_ref=arrived[f].at[d - 1], send_sem=share_send_sem.at[f],
                recv_sem=share_recv_sem.at[f], device_id=place(*ahead(f, 4 - d)), device_id_type=MESH,
            ).start()
    for group in range(2):
        landed = home_straight.at[pl.ds(group * 64 + 1 - group, 63 + group)]
        pltpu.make_async_copy(landed, landed, straight_home_sem.at[group]).wait()
    both = jnp.dot(straight_mix[...], home_straight[...].reshape(2048, 128), preferred_element_type=f32)
    both = both[:128] + both[128:]
    for s in range(8):
        columns = slice(REST + s * 128, REST + (s + 1) * 128)
        out_ref[:, columns] = (state[:12, columns] + both[s * 16 : s * 16 + 12]).astype(bf16)
    def give(n, start, width):
        part = pl.ds(start, width)
        return pltpu.make_async_copy(out_ref.at[:, part], out_hbm.at[:, part], out_sem.at[n])

    give(3, REST, 1024).start()
    for f in range(3):
        columns = slice(STARTS[f], STARTS[f] + WIDTHS[f])
        pltpu.make_async_copy(arrived[f], arrived[f], share_recv_sem.at[f]).wait()
        total = state[:12, columns]
        for d in range(3):
            total = total + arrived[f][d, :12, :].astype(f32)
        out_ref[:, columns] = total.astype(bf16)
        give(f, STARTS[f], WIDTHS[f]).start()

    for n in range(6):
        pltpu.make_async_copy(
            o_proj_hbm.at[pl.ds(0, 1024)], projection.at[pl.ds(0, 1024), pl.ds(128, 128)], o_send_sem.at[n]
        ).wait()
    gone = gathered.at[pl.ds(1, 7)]
    pltpu.make_async_copy(gone, gone, a_send_sem).wait()
    gone = collected.at[pl.ds(1, 31)]
    pltpu.make_async_copy(gone, gone, p_send_sem).wait()
    gone = tiles.at[pl.ds(0, 9)]
    pltpu.make_async_copy(gone, gone, tile_send_sem).wait()
    for f in range(3):
        gone = line[f].at[pl.ds(1, 3)]
        pltpu.make_async_copy(gone, gone, line_send_sem.at[f]).wait()
        gone = sent[f].at[pl.ds(1, 31)]
        pltpu.make_async_copy(gone, gone, send_sem.at[f]).wait()
        gone = results[f].at[pl.ds(1, 31)]
        pltpu.make_async_copy(gone, gone, back_sem.at[f]).wait()
        pltpu.make_async_copy(shared[f], shared[f], share_send_sem.at[f]).wait()
    for group in range(2):
        gone = out_straight.at[pl.ds(group * 64 + 1 - group, 63 + group)]
        pltpu.make_async_copy(gone, gone, straight_send_sem.at[group]).wait()
        gone = back_straight.at[pl.ds(group * 64 + 1 - group, 63 + group)]
        pltpu.make_async_copy(gone, gone, straight_back_sem.at[group]).wait()
    for f in range(3):
        give(f, STARTS[f], WIDTHS[f]).wait()
    give(3, REST, 1024).wait()


def body(
    queries, keys, values, lengths, o_proj, residual, norm_gain, gate_up, down, routes, route_weights,
):
    bf16, f32 = jnp.bfloat16, jnp.float32
    vmem = pl.BlockSpec(memory_space=pltpu.VMEM)
    smem = pl.BlockSpec(memory_space=pltpu.SMEM)
    hbm = pl.BlockSpec(memory_space=pl.ANY)
    each = lambda shape: tuple(shape(w) for w in WIDTHS)
    dma, plain = pltpu.SemaphoreType.DMA, pltpu.SemaphoreType.REGULAR
    return pl.pallas_call(
        kernel,
        out_shape=jax.ShapeDtypeStruct((12, 4096), bf16),
        in_specs=[hbm, hbm, hbm, smem, hbm, hbm, hbm, smem, smem, hbm, hbm],
        out_specs=hbm,
        scratch_shapes=[
            pltpu.VMEM((12, 4096), bf16),
            pltpu.VMEM((48, 2048), bf16),
            pltpu.VMEM((12, 4096), bf16),
            pltpu.VMEM((1, 4096), f32),
            pltpu.VMEM((48, 192, 128), bf16),
            pltpu.VMEM((48, 192, 128), bf16),
            pltpu.VMEM((48, 16, 128), f32),
            pltpu.VMEM((48, 16, 128), f32),
            pltpu.VMEM((8, 48, 2048), bf16),
            pltpu.VMEM((2048, 512), bf16),
            pltpu.VMEM((384, 512), f32),
            pltpu.VMEM((32, 48, 128), f32),
            pltpu.VMEM((32, 48, 128), bf16),
            pltpu.VMEM((32, 48, 128), bf16),
            pltpu.VMEM((8, 48, 128), f32),
            pltpu.VMEM((16, 4096), f32),
            pltpu.VMEM((4096, 1536), bf16),
            pltpu.VMEM((768, 4096), bf16),
            pltpu.VMEM((10, 16, 128), f32),
            each(lambda w: pltpu.VMEM((4, 16, w), bf16)),
            each(lambda w: pltpu.VMEM((32, 16, w // 2), bf16)),
            each(lambda w: pltpu.VMEM((32, 16, w // 2), bf16)),
            pltpu.VMEM((128, 4096), bf16),
            pltpu.VMEM((128, 768), bf16),
            each(lambda w: pltpu.VMEM((32, 16, w // 2), bf16)),
            each(lambda w: pltpu.VMEM((32, 16, w // 2), bf16)),
            each(lambda w: pltpu.VMEM((3, 16, w), bf16)),
            each(lambda w: pltpu.VMEM((3, 16, w), bf16)),
            pltpu.VMEM((3, 256, 64), bf16),
            pltpu.VMEM((3, 2, 128, 512), bf16),
            pltpu.VMEM((3, 256, 256), bf16),
            pltpu.VMEM((3, 256, 256), bf16),
            pltpu.VMEM((64, 3072), f32),
            pltpu.VMEM((128, 128), bf16),
            pltpu.VMEM((2048, 128), bf16),
            pltpu.VMEM((256, 2048), bf16),
            pltpu.VMEM((2, 256, 256), bf16),
            pltpu.VMEM((128, 16, 128), bf16),
            pltpu.VMEM((128, 16, 128), bf16),
            pltpu.VMEM((128, 16, 128), bf16),
            pltpu.VMEM((128, 16, 128), bf16),
            dma((4,)), dma((3,)), dma((2, 3)), dma((2,)), dma, dma((6,)), dma((6,)), dma, dma((3, 8)), dma, dma,
            dma, dma, dma((3,)), dma((3,)), dma((3,)), dma((3, 2)), dma((3,)), dma((3, 2)),
            dma((3,)), dma((3,)), dma((2,)), dma((2,)), dma((2,)), dma((2,)), plain, plain,
        ],
        compiler_params=pltpu.CompilerParams(
            collective_id=1, has_side_effects=True, vmem_limit_bytes=60 * 2**20
        ),
        cost_estimate=pl.CostEstimate(flops=6 * 10**9, bytes_accessed=3 * 10**7, transcendentals=10**6),
        name="layer",
    )(
        queries, keys[:, 0], values[:, 0], lengths, o_proj, residual, norm_gain[None, :], routes.T,
        route_weights.T, gate_up[0], down[0],
    )


def solution(mesh):
    in_specs = (
        P("req", "kvh"),
        P("req", "kvh", None, None),
        P("req", "kvh", None, None),
        P("req"),
        P("kvh", "req"),
        P(("req", "kvh"), None),
        P(),
        P(("req", "kvh"), None, None),
        P(("req", "kvh"), None, None),
        P(("req", "kvh"), None),
        P(("req", "kvh"), None),
    )
    out_specs = P(("req", "kvh"), None)
    return jax.shard_map(body, mesh=mesh, in_specs=in_specs, out_specs=out_specs, check_vma=False)
```
